32 devices in a mesh: dp: 8 (over z, y), mem: 4 (over x, core).
Axes of the slice: x: 2, y: 2, z: 4, core: 2. Of those that a mesh axis runs over, the one named last changes fastest.
Arguments:
- target: bfloat16 [8, 1024, 512], P('dp'), may hold values from -6 to 6
- memory: bfloat16 [8, 1024, 512], P('dp', 'mem'), may hold values from -6 to 6
- target_lengths: int32 [8, 8], P('dp'), may hold values from 1 to 512, 1024 in all within a row
- source_lengths: int32 [8, 8], P('dp'), may hold values from 1 to 512, 1024 in all within a row
- cotangent: bfloat16 [8, 1024, 512], P('dp'), may hold values from -6 to 6
- self_qkv: bfloat16 [512, 1536], replicated, may hold values from -0.25 to 0.25
- self_bias: bfloat16 [3, 512], replicated, may hold values from -1.5 to 1.5
- self_out: bfloat16 [512, 512], replicated, may hold values from -1 to 1
- cross_query: bfloat16 [512, 512], replicated, may hold values from -0.25 to 0.25
- cross_kv: bfloat16 [512, 1024], replicated, may hold values from -0.25 to 0.25
- cross_bias: bfloat16 [3, 512], replicated, may hold values from -1.5 to 1.5
- cross_out: bfloat16 [512, 512], replicated, may hold values from -1 to 1
- ffn_up: bfloat16 [512, 2048], replicated, may hold values from -0.25 to 0.25
- ffn_up_bias: bfloat16 [2048], replicated, may hold values from -1.5 to 1.5
- ffn_down: bfloat16 [2048, 512], replicated, may hold values from -0.1875 to 0.1875
- ffn_down_bias: bfloat16 [512], replicated, may hold values from -1.5 to 1.5
- norm_gains: bfloat16 [3, 512], replicated, may hold values from 0.5 to 1.5
- norm_biases: bfloat16 [3, 512], replicated, may hold values from -1.5 to 1.5
Outputs:
- layer_output: bfloat16 [8, 1024, 512], P('dp')
- target_grad: float32 [8, 1024, 512], P('dp')
- memory_grad: float32 [8, 1024, 512], P('dp', 'mem')
- self_qkv_grad: float32 [512, 1536], P('dp')
- self_bias_grad: float32 [3, 512], P(None, 'dp')
- self_out_grad: float32 [512, 512], P('dp')
- cross_query_grad: float32 [512, 512], P('dp')
- cross_kv_grad: float32 [512, 1024], P('dp')
- cross_bias_grad: float32 [3, 512], P(None, 'dp')
- cross_out_grad: float32 [512, 512], P('dp')
- ffn_up_grad: float32 [512, 2048], P('dp')
- ffn_up_bias_grad: float32 [2048], P('dp')
- ffn_down_grad: float32 [2048, 512], P('dp')
- ffn_down_bias_grad: float32 [512], P('dp')
- norm_gains_grad: float32 [3, 512], P(None, 'dp')
- norm_biases_grad: float32 [3, 512], P(None, 'dp')
The draws below stay inside these ranges and needn't reach their ends.
Inputs may be any that keep to these rules, and one draw needn't show every extreme that they name: `target_lengths`: each row's 8 target lengths sum to 1024 and the largest of a row is 512. `source_lengths`: each row's 8 source lengths sum to 1024 and the largest of a row is 512.
All inputs are finite; a program needn't handle non-finite values.
Results may differ from the reference program's by a relative error of at most 0.023.
Values may be sent and summed in bfloat16 or wider, within the bound.
No kernel may reach another device: no remote copies, remote signals or barrier semaphores. Data moves between devices by JAX's collectives and lax.ppermute only.
A program may use at most 256 MiB of HBM per device.

```python
import math
import jax
import jax.numpy as jnp
import numpy as np
from jax import lax

D = 512
HEADS = 8
HEAD = 64
FF = 2048
TGT_LEN = 1024
SRC_LEN = 1024
NSEG = 8
SEG_MOST = 512
ROWS = 8


def levels(key, dims, cuts, low, top_value):
    factor_of = 1.0
    for axis_at, shards_of in cuts:
        draws = jax.random.uniform(jax.random.fold_in(jax.random.fold_in(key, 6), axis_at), (shards_of,), jnp.float32, low / len(cuts), top_value / len(cuts))
        factor_of = factor_of * jnp.repeat(jnp.exp(draws), dims[axis_at] // shards_of).reshape((-1,) + (1,) * (len(dims) - 1 - axis_at))
    return factor_of


def split_up(amount, total, limit, lean):
    portions = [(1 << 20) // math.isqrt(rank ** lean) + 1 for rank in range(2, amount + 1)]
    rest, counts = total - limit - (amount - 1), [1] * (amount - 1)
    while rest > 0:
        movable = [i for i in range(amount - 1) if counts[i] < limit]
        mass, budget = sum([portions[i] for i in movable]), rest
        for i in movable:
            extra = min(limit - counts[i], max(1, budget * portions[i] // mass), rest)
            counts[i] = counts[i] + extra
            rest = rest - extra
    return np.array([limit] + counts)


def uneven(key, number_of, total, limit, lean):
    if number_of == 2:
        one = jax.random.randint(key, (), max(1, total - limit), min(limit, total - 1) + 1)
        return jnp.stack([one, total - one])
    sizes = jnp.asarray(split_up(number_of, total, limit, lean), jnp.int32)
    twos = (number_of - 1) // 2
    giver, taker = sizes[1:1 + 2 * twos:2], sizes[2:2 + 2 * twos:2]
    room = jnp.minimum(giver - 1, limit - taker)
    moved = jax.random.randint(jax.random.fold_in(key, 1), (twos,), 0, 1 << 20) % (room + 1)
    sizes = sizes.at[1:1 + 2 * twos:2].set(giver - moved).at[2:2 + 2 * twos:2].set(taker + moved)
    return sizes[jax.random.permutation(jax.random.fold_in(key, 2), number_of)]


def bell_draw(rng, extent, deviation, most, split=(), kind=jnp.bfloat16):
    result = jax.random.normal(rng, extent, jnp.float32) * deviation
    if len(split) > 0:
        result = levels(rng, extent, split, -0.22, 0.18) * result
    return jnp.clip(result, min=-most, max=most).astype(kind)


def setup_inputs(seed: int = 0) -> dict:
    keys = jax.random.split(jax.random.key(seed), 19)
    return {
        "target": bell_draw(keys[0], (ROWS, TGT_LEN, D), 1.0, 6.0, ((0, 8),)),
        "memory": bell_draw(keys[1], (ROWS, SRC_LEN, D), 1.0, 6.0, ((0, 8), (1, 4))),
        "target_lengths": jax.vmap(lambda own: uneven(own, NSEG, TGT_LEN, SEG_MOST, 2))(jax.random.split(keys[2], ROWS)).reshape((ROWS, NSEG)).astype(jnp.int32),
        "source_lengths": jax.vmap(lambda own: uneven(own, NSEG, SRC_LEN, SEG_MOST, 2))(jax.random.split(keys[3], ROWS)).reshape((ROWS, NSEG)).astype(jnp.int32),
        "cotangent": bell_draw(keys[4], (ROWS, TGT_LEN, D), 1.0, 6.0, ((0, 8),)),
        "self_qkv": bell_draw(keys[5], (D, 3 * D), D ** -0.5, 0.25),
        "self_bias": bell_draw(keys[6], (3, D), 0.3, 1.5),
        "self_out": bell_draw(keys[7], (D, D), (D // 16) ** -0.5, 1.0),
        "cross_query": bell_draw(keys[8], (D, D), D ** -0.5, 0.25),
        "cross_kv": bell_draw(keys[9], (D, 2 * D), D ** -0.5, 0.25),
        "cross_bias": bell_draw(keys[10], (3, D), 0.3, 1.5),
        "cross_out": bell_draw(keys[11], (D, D), (D // 16) ** -0.5, 1.0),
        "ffn_up": bell_draw(keys[12], (D, FF), D ** -0.5, 0.25),
        "ffn_up_bias": bell_draw(keys[13], (FF,), 0.3, 1.5),
        "ffn_down": bell_draw(keys[14], (FF, D), (FF // 2) ** -0.5, 0.1875),
        "ffn_down_bias": bell_draw(keys[15], (D,), 0.3, 1.5),
        "norm_gains": jnp.clip(1.0 + 0.1 * jax.random.normal(keys[16], (3, D), jnp.float32), 0.5, 1.5).astype(jnp.bfloat16),
        "norm_biases": bell_draw(keys[17], (3, D), 0.3, 1.5),
    }


@jax.custom_vjp
def low(v):
    return lax.optimization_barrier(v.astype(jnp.bfloat16)).astype(jnp.float32)

@jax.custom_vjp
def low_back(v):
    return v

def low_keep(v):
    return (low(v), None)

def low_pass(kept, grad):
    return (grad,)

def back_keep(v):
    return (v, None)

def back_low(kept, grad):
    return (low(grad),)
low.defvjp(low_keep, low_pass)
low_back.defvjp(back_keep, back_low)
epsilon = 1e-05
precise = lax.Precision.HIGHEST
very_negative = -1e+30

def matmul(left_matrix, right_matrix):
    return jnp.dot(left_matrix, right_matrix, precision=precise, preferred_element_type=jnp.float32)

def segment_ids(lengths, count):
    segment_ends = jnp.cumsum(lengths)
    places = jnp.arange(count, dtype=jnp.int32)
    return lax.optimization_barrier(jnp.sum((places[:, None] >= segment_ends[None, :]).astype(jnp.int32), axis=1)).astype(jnp.int32)

def layer_norm(hidden, gain_row, shift_row):
    center = hidden - lax.optimization_barrier(jnp.mean(hidden, axis=-1, keepdims=True))
    spread = lax.optimization_barrier(jnp.mean(center * center, axis=-1, keepdims=True))
    return center * lax.rsqrt(spread + epsilon) * gain_row + shift_row

def softmax_rows(scores, allowed):
    masked = jnp.where(allowed, scores, very_negative)
    row_top = lax.optimization_barrier(jnp.max(masked, axis=-1, keepdims=True))
    exp_terms = jnp.where(allowed, jnp.exp(masked - row_top), 0.0)
    return exp_terms / lax.optimization_barrier(jnp.sum(exp_terms, axis=-1, keepdims=True))

def row_layer(target_row, memory_row, target_len_row, source_len_row, params):
    self_qkv, self_bias, self_out, cross_query, cross_kv, cross_bias, cross_out, ffn_up, ffn_up_bias, ffn_down, ffn_down_bias, norm_gains, norm_biases = params
    model_width = HEADS * HEAD
    score_scale = HEAD ** (-0.5)
    target_seg = segment_ids(target_len_row, TGT_LEN)
    source_seg = segment_ids(source_len_row, SRC_LEN)
    qkv_shift = jnp.concatenate([self_bias[0], jnp.zeros_like(self_bias[0]), self_bias[1]])
    projected = low(low_back(matmul(low(target_row), self_qkv) + qkv_shift))
    queries = projected[:, :model_width].reshape(TGT_LEN, HEADS, HEAD)
    keys_self = projected[:, model_width:2 * model_width].reshape(TGT_LEN, HEADS, HEAD)
    values_self = projected[:, 2 * model_width:].reshape(TGT_LEN, HEADS, HEAD)
    scores = low_back(jnp.einsum('thd,uhd->htu', queries, keys_self, precision=precise) * score_scale)
    places = jnp.arange(TGT_LEN, dtype=jnp.int32)
    self_allowed = (target_seg[:, None] == target_seg[None, :]) & (places[None, :] <= places[:, None])
    self_probs = softmax_rows(scores, self_allowed[None])
    self_mixed = jnp.einsum('htu,uhd->thd', low(self_probs), values_self, precision=precise).reshape(TGT_LEN, model_width)
    self_mixed = low(low_back(self_mixed))
    self_branch = low_back(matmul(self_mixed, self_out) + self_bias[2])
    after_self = layer_norm(target_row + self_branch, norm_gains[0], norm_biases[0])
    cross_queries = low(low_back(matmul(low(after_self), cross_query) + cross_bias[0])).reshape(TGT_LEN, HEADS, HEAD)
    memory_kv = low(low_back(matmul(low(memory_row), cross_kv)))
    memory_keys = memory_kv[:, :model_width].reshape(SRC_LEN, HEADS, HEAD)
    memory_values = memory_kv[:, model_width:].reshape(SRC_LEN, HEADS, HEAD)
    cross_scores = low_back(jnp.einsum('thd,jhd->htj', cross_queries, memory_keys, precision=precise) * score_scale)
    cross_allowed = target_seg[:, None] == source_seg[None, :]
    cross_probs = softmax_rows(cross_scores, cross_allowed[None])
    cross_mixed = jnp.einsum('htj,jhd->thd', cross_probs, memory_values, precision=precise).reshape(TGT_LEN, model_width)
    cross_mixed = low(low_back(cross_mixed + cross_bias[1]))
    cross_branch = low_back(matmul(cross_mixed, cross_out) + cross_bias[2])
    after_cross = layer_norm(after_self + cross_branch, norm_gains[1], norm_biases[1])
    ffn_inner = low_back(matmul(low(after_cross), ffn_up) + ffn_up_bias)
    activated = low(jax.nn.silu(ffn_inner))
    ffn_branch = low_back(matmul(activated, ffn_down) + ffn_down_bias)
    return layer_norm(after_cross + ffn_branch, norm_gains[2], norm_biases[2])

def reference(target, memory, target_lengths, source_lengths, cotangent, self_qkv, self_bias, self_out, cross_query, cross_kv, cross_bias, cross_out, ffn_up, ffn_up_bias, ffn_down, ffn_down_bias, norm_gains, norm_biases):
    params = tuple((weight.astype(jnp.float32) for weight in (self_qkv, self_bias, self_out, cross_query, cross_kv, cross_bias, cross_out, ffn_up, ffn_up_bias, ffn_down, ffn_down_bias, norm_gains, norm_biases)))
    checked_row = jax.checkpoint(row_layer)

    def forward(targets, memories, weights):

        def one_row(row_items):
            return checked_row(row_items[0], row_items[1], row_items[2], row_items[3], weights)
        return lax.map(one_row, (targets, memories, target_lengths, source_lengths))
    output, pullback = jax.vjp(forward, target.astype(jnp.float32), memory.astype(jnp.float32), params)
    target_grad, memory_grad, weight_grads = pullback(cotangent.astype(jnp.float32))
    return (output.astype(jnp.bfloat16), target_grad, memory_grad, weight_grads[0], weight_grads[1], weight_grads[2], weight_grads[3], weight_grads[4], weight_grads[5], weight_grads[6], weight_grads[7], weight_grads[8], weight_grads[9], weight_grads[10], weight_grads[11], weight_grads[12])
```

```python
import functools

import jax
import jax.numpy as jnp
from jax import lax
from jax.sharding import PartitionSpec as P

HEADS = 8
BLOCK = 128
very_negative = -1e30
epsilon = 1e-05
f32 = jnp.float32
bf16 = jnp.bfloat16


def mm(left, right):
    return jnp.dot(left, right, preferred_element_type=f32)


def mm_tn(left, right):
    return lax.dot_general(left, right, (((0,), (0,)), ((), ())), preferred_element_type=f32)


def mm_nt(left, right):
    return lax.dot_general(left, right, (((1,), (1,)), ((), ())), preferred_element_type=f32)


def norm_forward(hidden, gain_row, shift_row):
    center = hidden - jnp.mean(hidden, axis=-1, keepdims=True)
    scaled = lax.rsqrt(jnp.mean(center * center, axis=-1, keepdims=True) + epsilon)
    normed = center * scaled
    return normed * gain_row + shift_row, normed, scaled


def norm_backward(upstream, normed, scaled, gain_row):
    gained = upstream * gain_row
    gained_mean = jnp.mean(gained, axis=-1, keepdims=True)
    mean_cross = jnp.mean(gained * normed, axis=-1, keepdims=True)
    return (
        scaled * (gained - gained_mean - normed * mean_cross),
        jnp.sum(upstream * normed, axis=0),
        jnp.sum(upstream, axis=0),
    )


def segment_ids(lengths, count):
    ends = jnp.cumsum(lengths)
    places = jnp.arange(count, dtype=jnp.int32)
    return jnp.sum((places[:, None] >= ends[None, :]).astype(jnp.int32), axis=1)


def softmax_parts(scores, allowed):
    masked = jnp.where(allowed, scores, very_negative)
    top = jnp.max(masked, axis=-1, keepdims=True)
    terms = jnp.exp(masked - top)
    total = jnp.sum(terms, axis=-1, keepdims=True)
    return terms / total


class Axis:
    def __init__(self, name, size):
        self.name, self.size = name, size
        self.index = lax.axis_index(name)
        self.bits = [1 << k for k in range(size.bit_length() - 1)]

    def bit(self, b):
        return (self.index // b) % 2

    def swap(self, value, b):
        return lax.ppermute(value, self.name, [(i, i ^ b) for i in range(self.size)])


def half(value, which, dim):
    return lax.dynamic_index_in_dim(value, which, dim, keepdims=False)


def ordered(own, other, bit, dim):
    return jnp.where(
        bit == 0, jnp.concatenate([own, other], dim), jnp.concatenate([other, own], dim)
    )


def gather_pieces(axis, value):
    pieces = {0: value}
    for b in reversed(axis.bits):
        keys = sorted(pieces)
        stacked = jnp.stack([pieces[k] for k in keys]) if len(keys) > 1 else pieces[0][None]
        got = axis.swap(stacked, b)
        pieces.update({k ^ b: got[i] for i, k in enumerate(keys)})
    return pieces


def place(axis, pieces):
    stacked = jnp.stack([pieces[b] for b in range(axis.size)])
    order = jnp.bitwise_xor(jnp.arange(axis.size), axis.index)
    return jnp.take(stacked, order, axis=0)


def reduce_weights(dp, mem, packed, mem_bits):
    rows, columns = packed.shape[1:]
    value = packed
    for b in mem_bits:
        parts = value.reshape(value.shape[:-1] + (2, value.shape[-1] // 2))
        keep, send = half(parts, mem.bit(b), parts.ndim - 2), half(parts, 1 - mem.bit(b), parts.ndim - 2)
        value = (keep.astype(f32) + mem.swap(send, b).astype(f32)).astype(bf16)
    value = value.reshape((2,) * len(dp.bits) + value.shape[1:])
    for b in reversed(dp.bits):
        keep, send = half(value, dp.bit(b), 0), half(value, 1 - dp.bit(b), 0)
        value = (keep.astype(f32) + dp.swap(send, b).astype(f32)).astype(bf16)
    return value


def widen(mem, value, mem_bits):
    for b in reversed(mem_bits):
        value = ordered(value, mem.swap(value, b), mem.bit(b), value.ndim - 1)
    return value


def on_device(
    dp_size,
    mem_size,
    target,
    memory,
    target_lengths,
    source_lengths,
    cotangent,
    self_qkv,
    self_bias,
    self_out,
    cross_query,
    cross_kv,
    cross_bias,
    cross_out,
    ffn_up,
    ffn_up_bias,
    ffn_down,
    ffn_down_bias,
    norm_gains,
    norm_biases,
):
    dp, mem = Axis("dp", dp_size), Axis("mem", mem_size)
    target, memory, cotangent = target[0], memory[0], cotangent[0]
    target_lengths, source_lengths = target_lengths[0], source_lengths[0]
    length, width = target.shape
    sources = memory.shape[0] * mem_size
    head = width // HEADS
    here = HEADS // mem_size
    own_width = here * head
    scale = head ** (-0.5)
    hidden = ffn_up.shape[1]
    own_blocks = length // (BLOCK * mem_size)
    gains, shifts = norm_gains.astype(f32), norm_biases.astype(f32)
    sb, cb = self_bias.astype(f32), cross_bias.astype(f32)
    ub, db = ffn_up_bias.astype(f32), ffn_down_bias.astype(f32)

    def own_tokens(array, b=0):
        parts = array.reshape((own_blocks, mem_size, BLOCK) + array.shape[1:])
        return lax.dynamic_index_in_dim(parts, mem.index ^ b, 1, keepdims=False).reshape(
            (own_blocks * BLOCK,) + array.shape[1:]
        )

    def all_tokens(pieces):
        parts = place(mem, pieces)
        parts = parts.reshape((mem_size, own_blocks, BLOCK) + parts.shape[2:])
        return jnp.swapaxes(parts, 0, 1).reshape((length,) + parts.shape[3:])

    memory_pieces = gather_pieces(mem, memory)

    target_seg = segment_ids(target_lengths, length)
    source_seg = segment_ids(source_lengths, sources)

    own_qkv = lax.dynamic_index_in_dim(
        self_qkv.reshape(width, 3, mem_size, own_width), mem.index, 2, keepdims=False
    )
    own_bias = lax.dynamic_index_in_dim(
        jnp.stack([sb[0], jnp.zeros_like(sb[0]), sb[1]]).reshape(3, mem_size, own_width),
        mem.index, 1, keepdims=False,
    )
    own_qkv2 = own_qkv.reshape(width, 3 * own_width)
    projected = (mm(target, own_qkv2) + own_bias.reshape(-1)).astype(bf16)
    q, k, v = (projected[:, i * own_width : (i + 1) * own_width].reshape(length, here, head) for i in range(3))
    places = jnp.arange(length)
    allowed = (target_seg[:, None] == target_seg[None, :]) & (places[None, :] <= places[:, None])
    scores = jnp.einsum("thd,uhd->htu", q, k, preferred_element_type=f32) * scale
    probs = softmax_parts(scores, allowed[None])
    mixed = jnp.einsum("htu,uhd->thd", probs.astype(bf16), v, preferred_element_type=f32)
    mixed = mixed.reshape(length, own_width).astype(bf16)
    mixed_pieces = {0: own_tokens(mixed)}
    for b in range(1, mem_size):
        mixed_pieces[b] = mem.swap(own_tokens(mixed, b), b)
    self_low = jnp.concatenate(list(place(mem, mixed_pieces)), axis=1)

    memory_all = place(mem, memory_pieces).reshape(sources, width)
    memory_kv = mm(memory_all, cross_kv).astype(bf16)
    mk = memory_kv[:, :width].reshape(sources, HEADS, head)
    mv = memory_kv[:, width:].reshape(sources, HEADS, head)

    count = own_blocks * BLOCK
    x = own_tokens(target).astype(f32)
    seg = own_tokens(target_seg)
    after_self, self_normed, self_scaled = norm_forward(x + mm(self_low, self_out) + sb[2], gains[0], shifts[0])
    after_self_low = after_self.astype(bf16)
    cq = (mm(after_self_low, cross_query) + cb[0]).astype(bf16).reshape(count, HEADS, head)
    cross_allowed = (seg[:, None] == source_seg[None, :])[None]
    cscores = jnp.einsum("thd,jhd->htj", cq, mk, preferred_element_type=f32) * scale
    cprobs = softmax_parts(cscores, cross_allowed)
    attended = jnp.einsum("htj,jhd->thd", cprobs.astype(bf16), mv, preferred_element_type=f32)
    cross_low = (attended.reshape(count, width) + cb[1]).astype(bf16)
    after_cross, cross_normed, cross_scaled = norm_forward(
        after_self + mm(cross_low, cross_out) + cb[2], gains[1], shifts[1]
    )
    after_cross_low = after_cross.astype(bf16)
    inner = mm(after_cross_low, ffn_up) + ub
    sig = jax.nn.sigmoid(inner)
    activated = (inner * sig).astype(bf16)
    layer_out, final_normed, final_scaled = norm_forward(
        after_cross + mm(activated, ffn_down) + db, gains[2], shifts[2]
    )
    grad_final, gain3, shift3 = norm_backward(own_tokens(cotangent).astype(f32), final_normed, final_scaled, gains[2])
    gfo = grad_final.astype(bf16)
    ginner = (mm_nt(gfo, ffn_down) * sig * (1.0 + inner * (1.0 - sig))).astype(bf16)
    up_grad = mm_tn(after_cross_low, ginner)
    down_grad = mm_tn(activated, gfo)
    grad_cross_norm, gain2, shift2 = norm_backward(grad_final + mm_nt(ginner, ffn_up), cross_normed, cross_scaled, gains[1])

    def per_dp(matrix):
        rows, columns = matrix.shape
        parts = matrix.astype(bf16).reshape(dp_size, rows // dp_size, columns // width, width)
        return jnp.swapaxes(parts, 1, 2).reshape(dp_size, -1, width)

    def from_dp(part, columns):
        rows = part.shape[0] * width // columns
        parts = part.reshape(columns // width, rows, width)
        return jnp.swapaxes(parts, 0, 1).reshape(rows, columns).astype(f32)

    ffn_packed = jnp.concatenate([per_dp(up_grad), per_dp(down_grad)], axis=1)
    ffn_sum = reduce_weights(dp, mem, ffn_packed, mem.bits)

    gcb = grad_cross_norm.astype(bf16)
    gcm = mm_nt(gcb, cross_out).astype(bf16)
    do = gcm.reshape(count, HEADS, head)
    dprobs = jnp.einsum("thd,jhd->htj", do, mv, preferred_element_type=f32)
    delta = jnp.sum(do.astype(f32) * attended, axis=-1).T[:, :, None]
    dscores = (cprobs * (dprobs - delta)).astype(bf16)
    gcq = (jnp.einsum("htj,jhd->thd", dscores, mk, preferred_element_type=f32) * scale).reshape(count, width).astype(bf16)
    gmk = jnp.einsum("htj,thd->jhd", dscores, cq, preferred_element_type=f32) * scale
    gmv = jnp.einsum("htj,thd->jhd", cprobs.astype(bf16), do, preferred_element_type=f32)
    gkv = jnp.concatenate([gmk.reshape(sources, width), gmv.reshape(sources, width)], axis=1).astype(bf16)
    grad_self_norm, gain1, shift1 = norm_backward(grad_cross_norm + mm_nt(gcq, cross_query), self_normed, self_scaled, gains[0])
    gsb = grad_self_norm.astype(bf16)
    gsm = mm_nt(gsb, self_out).astype(bf16)
    gsm_parts = gsm.reshape(count, mem_size, own_width)
    gsm_pieces = {}
    for b in range(mem_size):
        piece = lax.dynamic_index_in_dim(gsm_parts, mem.index ^ b, 1, keepdims=False)
        gsm_pieces[b] = mem.swap(piece, b) if b else piece

    memory_partial = mm_nt(gkv, cross_kv).astype(bf16).reshape(mem_size, -1, width)
    value = memory_partial.reshape((2,) * len(mem.bits) + memory_partial.shape[1:])
    for b in mem.bits:
        dim = len(value.shape) - 3
        keep, send = half(value, mem.bit(b), dim), half(value, 1 - mem.bit(b), dim)
        value = (keep.astype(f32) + mem.swap(send, b).astype(f32)).astype(bf16)
    memory_grad = value.astype(f32)

    sums = lambda a: jnp.sum(a.astype(f32), axis=0)
    vectors = jnp.stack(
        [sums(gsb), sums(gcq), sums(gcm), sums(gcb), gain1, gain2, gain3, shift1, shift2, shift3, sums(gfo)]
        + list(sums(ginner).reshape(-1, width))
    ).astype(bf16)
    vector_rows = vectors.shape[0]
    middle = [
        per_dp(mm_tn(cross_low, gcb)),
        per_dp(mm_tn(after_self_low, gcq)),
        per_dp(mm_tn(self_low, gsb)),
        per_dp(mm_tn(memory_all, gkv)),
        jnp.broadcast_to(vectors[None], (dp_size,) + vectors.shape),
    ]
    middle_packed = jnp.concatenate(middle, axis=1)
    middle_sum = reduce_weights(dp, mem, middle_packed, mem.bits)

    gso = all_tokens(gsm_pieces).reshape(length, here, head)
    dp_ = jnp.einsum("thd,uhd->htu", gso, v, preferred_element_type=f32)
    ds = (probs * (dp_ - jnp.sum(dp_ * probs, axis=-1, keepdims=True))).astype(bf16)
    gq = jnp.einsum("htu,uhd->thd", ds, k, preferred_element_type=f32) * scale
    gk = jnp.einsum("htu,thd->uhd", ds, q, preferred_element_type=f32) * scale
    gv = jnp.einsum("htu,thd->uhd", probs.astype(bf16), gso, preferred_element_type=f32)
    gproj = jnp.concatenate([a.reshape(length, own_width) for a in (gq, gk, gv)], axis=1).astype(bf16)
    qkv_grad = mm_tn(target, gproj)
    qkv_packed = jnp.concatenate(
        [qkv_grad.astype(bf16).reshape(dp_size, -1, 3 * own_width),
         jnp.broadcast_to(sums(gproj).astype(bf16)[None, None], (dp_size, 1, 3 * own_width))], axis=1)
    qkv_sum = reduce_weights(dp, mem, qkv_packed, [])
    partial = mm_nt(gproj, own_qkv2)
    partial = partial.reshape(own_blocks, mem_size, BLOCK, width)
    mine = lax.broadcasted_iota(jnp.int32, (1, mem_size, 1, 1), 1) == mem.index
    partial = partial + jnp.where(mine, grad_self_norm.reshape(own_blocks, 1, BLOCK, width), 0.0)
    parts = partial.astype(bf16).reshape(own_blocks * mem_size // 2, 2, BLOCK, width)
    value = (half(parts, mem.bit(1), 1).astype(f32) + mem.swap(half(parts, 1 - mem.bit(1), 1), 1).astype(f32)).astype(bf16)
    for b in mem.bits[1:]:
        value = (value.astype(f32) + mem.swap(value, b).astype(f32)).astype(bf16)
    target_grad = ordered(value[:, None], mem.swap(value, 1)[:, None], mem.bit(1), 1)
    target_grad = target_grad.reshape(length, width).astype(f32)

    layer_output = all_tokens(gather_pieces(mem, layer_out.astype(bf16)))

    ffn_all = widen(mem, ffn_sum, mem.bits)
    middle_all = widen(mem, middle_sum, mem.bits)
    qkv_pieces = gather_pieces(mem, qkv_sum)
    rows = width // dp_size
    qkv_all = place(mem, qkv_pieces).reshape(mem_size, rows + 1, 3, own_width)
    qkv_all = jnp.transpose(qkv_all, (1, 2, 0, 3)).reshape(rows + 1, 3, width)
    up_rows = rows * hidden // width
    up_all, down_all = ffn_all[:up_rows], ffn_all[up_rows:]
    cross_out_all, cross_query_all, self_out_all = (middle_all[i * rows : (i + 1) * rows] for i in range(3))
    kv_all = middle_all[3 * rows : 5 * rows]
    vec = middle_all[5 * rows : 5 * rows + vector_rows].astype(f32)

    def share(matrix):
        return lax.dynamic_slice_in_dim(matrix, dp.index * rows, rows, axis=1)

    qkv_vec = qkv_all[rows].astype(f32)
    self_bias_all = jnp.stack([qkv_vec[0], qkv_vec[2], vec[0]])
    return (
        layer_output[None],
        target_grad[None],
        memory_grad[None],
        qkv_all[:rows].reshape(rows, 3 * width).astype(f32),
        share(self_bias_all),
        self_out_all.astype(f32),
        cross_query_all.astype(f32),
        from_dp(kv_all, 2 * width),
        share(vec[1:4]),
        cross_out_all.astype(f32),
        from_dp(up_all, hidden),
        lax.dynamic_slice_in_dim(vec[11:].reshape(-1), dp.index * (hidden // dp_size), hidden // dp_size),
        down_all.astype(f32),
        share(vec[10:11])[0],
        share(vec[4:7]),
        share(vec[7:10]),
    )


def solution(mesh):
    row, whole = P("dp", None, None), P()
    in_specs = (row, P("dp", "mem", None), P("dp", None), P("dp", None), row) + (whole,) * 13
    out_specs = (
        row,
        row,
        P("dp", "mem", None),
        P("dp", None),
        P(None, "dp"),
        P("dp", None),
        P("dp", None),
        P("dp", None),
        P(None, "dp"),
        P("dp", None),
        P("dp", None),
        P("dp"),
        P("dp", None),
        P("dp"),
        P(None, "dp"),
        P(None, "dp"),
    )
    body = functools.partial(on_device, mesh.shape["dp"], mesh.shape["mem"])
    return jax.shard_map(body, mesh=mesh, in_specs=in_specs, out_specs=out_specs, check_vma=False)
```

```python
import functools

import jax
import jax.numpy as jnp
from jax import lax
from jax.experimental import pallas as pl
from jax.experimental.pallas import tpu as pltpu
from jax.sharding import PartitionSpec as P

HEADS = 8
SEG_MOST = 512
LANES = 128
HALF = 256
very_negative = -1e30
epsilon = 1e-05
SELF_BIAS, CROSS_BIAS, GAINS, SHIFTS, DOWN_BIAS, UP_BIAS = 0, 3, 6, 9, 12, 13
f32 = jnp.float32
bf16 = jnp.bfloat16


def mm(left, right):
    return jnp.dot(left, right, preferred_element_type=f32)


def mm_tn(left, right):
    return lax.dot_general(left, right, (((0,), (0,)), ((), ())), preferred_element_type=f32)


def mm_nt(left, right):
    return lax.dot_general(left, right, (((1,), (1,)), ((), ())), preferred_element_type=f32)


def norm_parts(hidden):
    center = hidden - jnp.mean(hidden, axis=-1, keepdims=True)
    scaled = lax.rsqrt(jnp.mean(center * center, axis=-1, keepdims=True) + epsilon)
    return center * scaled, scaled


def norm_backward(upstream, normed, scaled, gain_row):
    gained = upstream * gain_row
    gained_mean = jnp.mean(gained, axis=-1, keepdims=True)
    mean_cross = jnp.mean(gained * normed, axis=-1, keepdims=True)
    return scaled * (gained - gained_mean - normed * mean_cross)


def sums(matrix):
    return jnp.sum(matrix.astype(f32), axis=0, keepdims=True)


def started(lengths, places, ends, amounts):
    total = jnp.zeros(places.shape, jnp.int32)
    edge = jnp.int32(0)
    for j in range(lengths.shape[0]):
        if ends:
            edge = edge + lengths[j]
        total = total + jnp.where(places >= edge, amounts[j], 0)
        if not ends:
            edge = edge + lengths[j]
    return total


def head_lanes(value, h, head):
    if value.shape[-1] == head:
        return value
    lanes = lax.broadcasted_iota(jnp.int32, value.shape, 1)
    return jnp.where(lanes // head == h, value, jnp.zeros_like(value))


def self_bias(tlen_ref, begin, first, count):
    queries = begin + lax.broadcasted_iota(jnp.int32, (1, count), 1)
    start = started(tlen_ref, queries, True, tlen_ref)
    keys = first + lax.broadcasted_iota(jnp.int32, (begin + count - first, count), 0)
    return jnp.where((keys >= start) & (keys <= queries), 0.0, very_negative)


def self_forward_kernel(
    sizes, idx, tlen, target, qkv, vecs, q_out, k_out, v_out, kt_out, ot_out, lse_out, *rest
):
    mem, head = sizes
    pieces, (mixed, held, sem) = rest[:mem], rest[mem:]
    length = target.shape[0]
    wide = q_out.shape[1]
    share = length // mem
    weights = own_weights(idx, qkv, held, sem, wide)
    zero = jnp.zeros((1, wide), f32)
    block = lane_block(idx[0], wide)
    shift = [own_lanes(vecs.value()[i : i + 1, block], idx[0], wide) for i in (0, 1)]
    shift = jnp.concatenate([shift[0], zero, shift[1]], axis=1)
    for at in range(0, length, HALF):
        rows = slice(at, at + HALF)
        part = (mm(target[rows, :], weights) + shift).astype(bf16)
        q_out[rows, :] = part[:, :wide]
        k_out[rows, :] = part[:, wide : 2 * wide]
        v_out[rows, :] = part[:, 2 * wide :]
        kt_out[:, rows] = part[:, wide : 2 * wide].T
        mixed[rows, :] = part[:, 2 * wide :]
    for out in (q_out, k_out, v_out, kt_out):
        out.send()
    vt = mixed[...].T
    lse_out[...] = jnp.zeros(lse_out.shape, f32)
    for at in range(0, length, HALF):
        first = max(0, at - SEG_MOST)
        keys, cols = slice(first, at + HALF), slice(at, at + HALF)
        bias = self_bias(tlen, at, first, HALF)
        q = q_out[cols, :] * jnp.asarray(head**-0.5, bf16)
        for h in range(wide // head):
            scores = mm_nt(k_out[keys, :], head_lanes(q, h, head)) + bias
            top = jnp.max(scores, axis=0, keepdims=True)
            terms = jnp.exp(scores - top)
            total = jnp.sum(terms, axis=0, keepdims=True)
            part = mm(vt[h * head : (h + 1) * head, keys], terms.astype(bf16)) / total
            ot_out[h * head : (h + 1) * head, cols] = part
            lse_out[h : h + 1, cols] = top + jnp.log(total)
        mixed[cols, :] = ot_out[:, cols].T.astype(bf16)
    for b in range(mem):
        at = pl.multiple_of((idx[0] ^ b) * share, share)
        pieces[b][...] = mixed[pl.ds(at, share), :]


def memory_kernel(idx, *refs):
    pieces, (weights, all_out, k_out, v_out, kt_out, vt_out) = refs[:-6], refs[-6:]
    share, width = pieces[0].shape
    for b, piece in enumerate(pieces):
        at = pl.multiple_of((idx[0] ^ b) * share, share)
        all_out[pl.ds(at, share), :] = piece[...]
        both = mm(piece[...], weights[...]).astype(bf16)
        k_out[pl.ds(at, share), :] = both[:, :width]
        v_out[pl.ds(at, share), :] = both[:, width:]
        kt_out[:, pl.ds(at, share)] = both[:, :width].T
        vt_out[:, pl.ds(at, share)] = both[:, width:].T


def cross_bias_of(idx, tlen, slen, count, keys):
    queries = idx[0] * count + lax.broadcasted_iota(jnp.int32, (1, count), 1)
    low = started(tlen, queries, True, slen)
    high = started(tlen, queries, False, slen)
    places = lax.broadcasted_iota(jnp.int32, (keys, count), 0)
    return jnp.where((places >= low) & (places < high), 0.0, very_negative)


def column_of(row, count):
    return jnp.broadcast_to(row, (count, row.shape[1])).T


def token_kernel(
    sizes, idx, tlen, slen, target, cotangent, wo, vecs, cq, keys, vt, co, up, down, *rest,
):
    mem, dp, head = sizes
    pieces = rest[:mem]
    (lo_out, up_keep, up_send, down_keep, down_send, h0_out, mixed_out, q_out, cmt_out, att_out, lse_out, gcn_out,
     vec_out, x, ct, bias, act, fac, gi, gfo_s, acl_s, sem) = rest[mem:]
    count, width = lo_out.shape
    wide = width // mem
    hidden = up.shape[1]
    share = pl.ds(pl.multiple_of(idx[0] * count, count), count)
    copies = [
        pltpu.make_async_copy(target.at[share, :], x, sem.at[0]),
        pltpu.make_async_copy(cotangent.at[share, :], ct, sem.at[1]),
    ]
    for copy in copies:
        copy.start()
    bias[...] = cross_bias_of(idx, tlen, slen, count, keys.shape[0])
    row = lambda i: vecs[i : i + 1, :]
    copies[0].wait()
    h0 = x[...].astype(f32) + row(SELF_BIAS + 2)
    for b in range(mem):
        at = pl.multiple_of((idx[0] ^ b) * wide, wide)
        h0 = h0 + mm(pieces[b][...], wo.value()[pl.ds(at, wide), :])
        mixed_out[:, b * wide : (b + 1) * wide] = pieces[b][...]
    h0_out[...] = h0
    mixed_out.send()
    h0_out.send()
    normed0, _ = norm_parts(h0)
    after_self = normed0 * row(GAINS) + row(SHIFTS)
    q = (mm(after_self.astype(bf16), cq[...]) + row(CROSS_BIAS)).astype(bf16)
    q_out[...] = q
    q_out.send()
    q = q * jnp.asarray(head**-0.5, bf16)
    for h in range(HEADS):
        pair = slice(h * head // LANES * LANES, h * head // LANES * LANES + LANES)
        scores = mm_nt(keys[:, pair], head_lanes(q[:, pair], h % (LANES // head), head)) + bias[...]
        top = jnp.max(scores, axis=0, keepdims=True)
        terms = jnp.exp(scores - top)
        total = jnp.sum(terms, axis=0, keepdims=True)
        own = slice(h * head, (h + 1) * head)
        att_out[own, :] = mm(vt[own, :], terms.astype(bf16)) / total
        lse_out[h : h + 1, :] = top + jnp.log(total)
    cmt = (att_out[...] + column_of(row(CROSS_BIAS + 1), count)).astype(bf16)
    cmt_out[...] = cmt
    for out in (att_out, lse_out, cmt_out):
        out.send()
    normed1, scaled1 = norm_parts(after_self + mm_tn(cmt, co[...]) + row(CROSS_BIAS + 2))
    after_cross = normed1 * row(GAINS + 1) + row(SHIFTS + 1)
    acl = after_cross.astype(bf16)
    acl_s[...] = acl
    step = width
    h2 = after_cross + row(DOWN_BIAS)
    for i, at in enumerate(range(0, hidden, step)):
        cols = slice(at, at + step)
        inner = mm(acl, up[:, cols]) + row(UP_BIAS + i)
        sig = jax.nn.sigmoid(inner)
        part = (inner * sig).astype(bf16)
        act[:, cols] = part
        fac[:, cols] = sig * (1.0 + inner * (1.0 - sig))
        h2 = h2 + mm(part, down[cols, :])
    normed2, scaled2 = norm_parts(h2)
    lo_out[...] = (normed2 * row(GAINS + 2) + row(SHIFTS + 2)).astype(bf16)
    copies[1].wait()
    cot = ct[...].astype(f32)
    gf = norm_backward(cot, normed2, scaled2, row(GAINS + 2))
    gfo = gf.astype(bf16)
    gfo_s[...] = gfo
    u1 = gf
    vec_out[...] = jnp.zeros(vec_out.shape, f32)
    for i, at in enumerate(range(0, hidden, step)):
        cols = slice(at, at + step)
        part = (mm_nt(gfo, down[cols, :]) * fac[:, cols]).astype(bf16)
        gi[:, cols] = part
        u1 = u1 + mm_nt(part, up[:, cols])
        vec_out[5 + i : 6 + i, :] = sums(part)
    gcn_out[...] = norm_backward(u1, normed1, scaled1, row(GAINS + 1))
    for i, part in enumerate((u1 * normed1, u1, cot * normed2, cot, gfo)):
        vec_out[i : i + 1, :] = sums(part)
    gcn_out.send()
    vec_out.send()
    rows, hrows = width // dp, hidden // dp
    some = width // hrows
    for up_out, down_out, side in ((up_send, down_send, 1 - idx[0] % 2), (up_keep, down_keep, idx[0] % 2)):
        start = side * HALF
        cols = pl.ds(pl.multiple_of(start, HALF), HALF)
        for i in range(hidden // width):
            part = mm_tn(act[:, i * width : (i + 1) * width], gfo_s[:, cols]).astype(bf16)
            down_out[i * some : (i + 1) * some] = part.reshape(some, hrows, HALF)
        for i in range(hidden // width):
            cols = pl.ds(pl.multiple_of(start + i * width, HALF), HALF)
            part = mm_tn(acl_s[...], gi[:, cols]).astype(bf16)
            up_out[:, i * rows : (i + 1) * rows, :] = part.reshape(dp, rows, HALF)


def cross_backward_kernel(
    sizes, idx, tlen, slen, gcn, co, q_ref, lse, att, keys, values, kt, cq, vecs, h0, wo,
    gk_out, gv_out, gcq_out, gcb_out, gsb_out, gsn_out, vec_out, *rest,
):
    mem, head = sizes
    pieces, (bias, gcqt) = rest[:mem], rest[mem:]
    count, width = gcn.shape
    wide = width // mem
    bias[...] = cross_bias_of(idx, tlen, slen, count, keys.shape[0])
    gcb = gcn[...].astype(bf16)
    gcb_out[...] = gcb
    gcb_out.send()
    gcm = mm_nt(gcb, co[...]).astype(bf16)
    gcmt = mm_nt(co[...], gcb).astype(bf16)
    scale = head**-0.5
    q = q_ref[...] * jnp.asarray(scale, bf16)
    for p in range(width // LANES):
        pair = slice(p * LANES, (p + 1) * LANES)
        gk = gv = 0.0
        for i in range(LANES // head):
            h = p * (LANES // head) + i
            own = slice(h * head, (h + 1) * head)
            delta = jnp.sum(gcmt[own, :].astype(f32) * att[own, :], axis=0, keepdims=True)
            qh, gh = head_lanes(q[:, pair], i, head), head_lanes(gcm[:, pair], i, head)
            probs = jnp.exp(mm_nt(keys[:, pair], qh) + bias[...] - lse[h : h + 1, :])
            ds = (probs * (mm_nt(values[:, pair], gh) - delta)).astype(bf16)
            gv = gv + mm(probs.astype(bf16), gh)
            gk = gk + mm(ds, qh)
            gcqt[own, :] = mm(kt[own, :], ds) * scale
        gk_out[:, pair] = gk.astype(bf16)
        gv_out[:, pair] = gv.astype(bf16)
    gk_out.send()
    gv_out.send()
    gcq = gcqt[...].T.astype(bf16)
    gcq_out[...] = gcq
    gcq_out.send()
    u0 = gcn[...] + mm_nt(gcq, cq[...])
    normed0, scaled0 = norm_parts(h0[...])
    gsn = norm_backward(u0, normed0, scaled0, vecs[GAINS : GAINS + 1, :])
    gsn_out[...] = gsn
    gsb = gsn.astype(bf16)
    gsb_out[...] = gsb
    for b in range(mem):
        at = pl.multiple_of((idx[0] ^ b) * wide, wide)
        pieces[b][...] = mm_nt(gsb, wo.value()[pl.ds(at, wide), :]).astype(bf16)
    vec_out[...] = jnp.zeros(vec_out.shape, f32)
    for i, part in enumerate((gsb, gcq, gcm, gcb, u0 * normed0, u0)):
        vec_out[i : i + 1, :] = sums(part)


def middle_kernel(
    sizes, idx, gk, gv, memory, wkv, cmt, gcb, h0, vecs, gcq, mixed, gsb, vec1, vec2,
    keep_out, send_out, mkeep_out, msend_out,
):
    mem, dp = sizes
    count, width = gcb.shape
    wide, share = width // mem, memory.shape[0] // mem
    rows = width // dp
    for out, side in ((msend_out, 1 - idx[0] % 2), (mkeep_out, idx[0] % 2)):
        for i in range(mem // 2):
            at = pl.ds(pl.multiple_of((2 * i + side) * share, share), share)
            part = mm_nt(gk.value()[at, :], wkv[:, :width]) + mm_nt(gv.value()[at, :], wkv[:, width:])
            out[i] = part.astype(bf16)
    normed0, _ = norm_parts(h0[...])
    asl = (normed0 * vecs[GAINS : GAINS + 1, :] + vecs[SHIFTS : SHIFTS + 1, :]).astype(bf16)
    vec = jnp.concatenate([vec1[...], vec2[...]], axis=0).astype(bf16)
    some = wide // rows
    for out, side in ((send_out, 1 - idx[0] % 2), (keep_out, idx[0] % 2)):
        cols = pl.ds(pl.multiple_of(side * HALF, HALF), HALF)

        def put(at, matrix):
            out[:, at * rows : (at + 1) * rows, :] = matrix.astype(bf16).reshape(dp, rows, HALF)

        put(0, mm(cmt[...], gcb.value()[:, cols]))
        put(1, mm_tn(asl, gcq.value()[:, cols]))
        part = mm_tn(mixed[...], gsb.value()[:, cols]).astype(bf16)
        for b in range(mem):
            j = idx[0] ^ b
            out[pl.ds(j * some, some), 2 * rows : 3 * rows, :] = part[b * wide : (b + 1) * wide].reshape(some, rows, HALF)
        put(3, mm_tn(memory[...], gk.value()[:, cols]))
        put(4, mm_tn(memory[...], gv.value()[:, cols]))
        vrows = vec.shape[0]
        half = jnp.where(side == 0, vec[:, :HALF], vec[:, HALF:])
        out[:, 5 * rows : 5 * rows + vrows, :] = jnp.broadcast_to(half[None], (dp, vrows, HALF))


def self_backward_kernel(
    sizes, idx, tlen, q_ref, k_ref, v_ref, ot, lse, kt, target, qkv, gsn, *rest
):
    mem, dp, head = sizes
    pieces = rest[:mem]
    qkv_out, keep_out, send_out, go, gproj, gk, gv, gqt, held, sem = rest[mem:]
    length, wide = q_ref.shape
    share, width = gsn.shape
    copies = own_weights_copies(idx, qkv, held, sem, wide)
    for b in range(mem):
        at = pl.multiple_of((idx[0] ^ b) * share, share)
        go[pl.ds(at, share), :] = pieces[b][...]
    gk[...] = jnp.zeros_like(gk)
    gv[...] = jnp.zeros_like(gv)
    scale = head**-0.5
    for at in range(0, length, HALF):
        first = max(0, at - SEG_MOST)
        keys, cols = slice(first, at + HALF), slice(at, at + HALF)
        bias = self_bias(tlen, at, first, HALF)
        q = q_ref[cols, :] * jnp.asarray(scale, bf16)
        grad = go[cols, :]
        product = grad.astype(f32).T * ot[:, cols]
        for h in range(wide // head):
            own = slice(h * head, (h + 1) * head)
            delta = jnp.sum(product[own, :], axis=0, keepdims=True)
            qh, gh = head_lanes(q, h, head), head_lanes(grad, h, head)
            probs = jnp.exp(mm_nt(k_ref[keys, :], qh) + bias - lse[h : h + 1, cols])
            ds = (probs * (mm_nt(v_ref[keys, :], gh) - delta)).astype(bf16)
            gv[keys, :] += mm(probs.astype(bf16), gh)
            gk[keys, :] += mm(ds, qh)
            gqt[own, cols] = mm(kt[own, keys], ds) * scale
    gproj[:, :wide] = gqt[...].T.astype(bf16)
    gproj[:, wide : 2 * wide] = gk[...].astype(bf16)
    gproj[:, 2 * wide :] = gv[...].astype(bf16)
    rows = width // dp
    qkv_out[:, :rows, :] = mm_tn(target[...], gproj[...]).astype(bf16).reshape(dp, rows, 3 * wide)
    total = sums(gproj[...]).astype(bf16)
    pad = qkv_out.shape[1] - rows
    qkv_out[:, rows:, :] = jnp.broadcast_to(total[None], (dp, pad, 3 * wide))
    weights = own_weights_value(idx, copies, held, wide)
    for out, side in ((send_out, 1 - idx[0] % 2), (keep_out, idx[0] % 2)):
        for i in range(mem // 2):
            at = pl.multiple_of((2 * i + side) * share, share)
            out[i] = mm_nt(gproj[pl.ds(at, share), :], weights).astype(bf16)
    at = pl.multiple_of(idx[0] * share, share)
    part = mm_nt(gproj[pl.ds(at, share), :], weights) + gsn[...]
    keep_out[idx[0] // 2] = part.astype(bf16)


def own_weights_copies(idx, qkv, held, sem, wide):
    width, full = qkv.shape[0], qkv.shape[1] // 3
    lanes = max(wide, LANES)
    copies = []
    for c in range(3):
        at = pl.multiple_of(c * full + idx[0] * wide // LANES * LANES, LANES)
        copies.append(pltpu.make_async_copy(qkv.at[:, pl.ds(at, lanes)], held.at[c], sem.at[c]))
        copies[-1].start()
    return copies


def own_weights_value(idx, copies, held, wide):
    for copy in copies:
        copy.wait()
    return jnp.concatenate([own_lanes(held[c], idx[0], wide) for c in range(3)], axis=1)


def own_weights(idx, qkv, held, sem, wide):
    return own_weights_value(idx, own_weights_copies(idx, qkv, held, sem, wide), held, wide)


def split_kernel(axis_at, bit_at, dim, idx, keep, received, keep_out, send_out):
    bit = (idx[axis_at] >> bit_at) & 1
    if dim == keep.ndim - 1:
        total = keep[...].astype(f32) + received[...].astype(f32)
        middle = keep.shape[-1] // 2
        low, high = total[..., :middle], total[..., middle:]
        keep_out[...] = jnp.where(bit == 0, low, high).astype(bf16)
        send_out[...] = jnp.where(bit == 0, high, low).astype(bf16)
        return
    lead = (slice(None),) * dim
    for out, which in ((send_out, 1 - bit), (keep_out, bit)):
        out[...] = (keep[lead + (which,)].astype(f32) + received[lead + (which,)].astype(f32)).astype(bf16)


def add_kernel(*refs):
    out, pairs, at = refs[-1], refs[:-1], 0
    for keep, received in zip(pairs[::2], pairs[1::2]):
        part = keep[...].astype(f32) + received[...].astype(f32)
        out[at : at + part.shape[0]] = part.astype(out.dtype)
        at += part.shape[0]


def rows_kernel(idx, *refs):
    pieces, (out, sem) = refs[:-2], refs[-2:]
    share = pieces[0].shape[0]
    copies = []
    for b, piece in enumerate(pieces):
        at = pl.multiple_of((idx[0] ^ b) * share, share)
        copies.append(pltpu.make_async_copy(piece, out.at[pl.ds(at, share), :], sem.at[b]))
        copies[-1].start()
    for copy in copies:
        copy.wait()


def target_kernel(idx, own, other, out, held, sem):
    count, share = own.shape[:2]
    copies = []
    for i in range(count):
        for k, (ref, side) in enumerate(((own, idx[0] % 2), (other, 1 - idx[0] % 2))):
            n = 2 * i + k
            held[n] = ref[i].astype(f32)
            at = pl.multiple_of((2 * i + side) * share, share)
            copies.append(pltpu.make_async_copy(held.at[n], out.at[pl.ds(at, share), :], sem.at[n]))
            copies[-1].start()
    for copy in copies:
        copy.wait()


def column_at(idx, b):
    other = idx[0] ^ b
    return pl.multiple_of(other % 2 * HALF + other // 2 % 2 * LANES, LANES)


def ffn_out_kernel(idx, *refs):
    pieces, (up_out, down_out) = refs[:-2], refs[-2:]
    rows, width = up_out.shape[0], down_out.shape[1]
    blocks = up_out.shape[1] // width
    for b, piece in enumerate(pieces):
        at = column_at(idx, b)
        for i in range(blocks):
            part = piece[i * rows : (i + 1) * rows, :].astype(f32)
            up_out.held[:, pl.ds(pl.multiple_of(i * width + at, LANES), LANES)] = part
        down_out.held[:, pl.ds(at, LANES)] = piece[blocks * rows :, :].astype(f32)


def lanes_from(ref, first, count, at, wide):
    if wide % LANES == 0:
        return ref[pl.ds(first, count), pl.ds(pl.multiple_of(at, LANES), wide)]
    block = ref[pl.ds(first, count), pl.ds(pl.multiple_of(at // LANES * LANES, LANES), LANES)]
    result = block[:, :wide]
    for k in range(1, LANES // wide):
        result = jnp.where(at % LANES == k * wide, block[:, k * wide : (k + 1) * wide], result)
    return result


def middle_out_kernel(count, idx, *refs):
    pieces = refs[:-10]
    co_out, cq_out, so_out, kv_out, cb_out, ub_out, db_out, gain_out, shift_out, vec = refs[-10:]
    rows, width = co_out.shape
    for b, piece in enumerate(pieces):
        at = column_at(idx, b)
        cols = pl.ds(at, LANES)
        for i, out in enumerate((co_out, cq_out, so_out)):
            out.held[:, cols] = piece[i * rows : (i + 1) * rows, :].astype(f32)
        for i in range(2):
            part = piece[(3 + i) * rows : (4 + i) * rows, :].astype(f32)
            kv_out.held[:, pl.ds(pl.multiple_of(i * width + at, LANES), LANES)] = part
        vec[:, cols] = piece[5 * rows :, :].astype(f32)
    here = idx[1] * rows
    take = lambda first, count: lanes_from(vec, first, count, here, rows)
    cb_out[...] = take(17, 3)
    db_out[...] = take(4, 1)
    for out, places in ((gain_out, (20, 0, 2)), (shift_out, (21, 1, 3))):
        for i, first in enumerate(places):
            out[i : i + 1, :] = take(first, 1)
    per = ub_out.shape[1]
    first = idx[1] * per
    part = lanes_from(vec, 5, 1, first % width, per)
    for i in range(1, count):
        part = jnp.where(first // width == i, lanes_from(vec, 5 + i, 1, first % width, per), part)
    ub_out[...] = part


def qkv_out_kernel(idx, vec, *refs):
    pieces, (qkv_out, sb_out, full) = refs[:-3], refs[-3:]
    rows, width = qkv_out.shape[0], qkv_out.shape[1] // 3
    wide = pieces[0].shape[1] // 3

    def put(out, first, count):
        for c in range(3):
            lanes = slice(c * wide, (c + 1) * wide)
            parts = [piece[first : first + count, lanes].astype(f32) for piece in pieces]
            if wide < LANES:
                odd = idx[0] % 2
                parts = [
                    jnp.where(odd == 0, jnp.concatenate([a, b], 1), jnp.concatenate([b, a], 1))
                    for a, b in zip(parts[::2], parts[1::2])
                ]
            for b, part in enumerate(parts):
                j = idx[0] ^ b if wide >= LANES else (idx[0] // 2) ^ b
                at = pl.multiple_of(c * width + j * max(wide, LANES), LANES)
                out[:count, pl.ds(at, max(wide, LANES))] = part

    put(qkv_out.held, 0, rows)
    put(full, rows, full.shape[0])
    here = idx[1] * rows
    sb_out[0:1, :] = lanes_from(full, 0, 1, here, rows)
    sb_out[1:2, :] = lanes_from(full, 0, 1, 2 * width + here, rows)
    sb_out[2:3, :] = lanes_from(vec, 16, 1, here, rows)


class Staged:
    def __init__(self, source, held, sem):
        self.held, self.copy, self.shape, self.dtype = held, pltpu.make_async_copy(source, held, sem), held.shape, held.dtype
        self.copy.start()
        self.waited = False

    def wait(self):
        if not self.waited:
            self.copy.wait()
            self.waited = True

    def __getitem__(self, at):
        self.wait()
        return self.held[at]

    def value(self):
        self.wait()
        return self.held


class Result:
    def __init__(self, place, held, sem):
        self.held, self.shape, self.dtype = held, held.shape, held.dtype
        self.copy, self.sent = pltpu.make_async_copy(held, place, sem), False

    def __getitem__(self, at):
        return self.held[at]

    def __setitem__(self, at, value):
        self.held[at] = value

    def send(self):
        if not self.sent:
            self.copy.start()
            self.sent = True


def call(kernel, ins, outs, scratch=(), vmem=32):
    spaces = {"s": pltpu.SMEM, "v": pltpu.VMEM, "h": pltpu.HBM, "r": pltpu.HBM}
    held = [(x.shape, x.dtype) for x, mode in ins if mode == "h"]
    held += [(shape, dtype) for shape, dtype, mode in outs if mode == "h"]
    modes = [mode for _, mode in ins] + [mode for _, _, mode in outs]

    def body(*refs):
        count = len(modes)
        own = refs[count + len(held) : len(refs) - 1 if held else len(refs)]
        spare, sems = iter(refs[count : count + len(held)]), refs[-1]
        given, place = [], 0
        for i, mode in enumerate(modes):
            ref = refs[i]
            if mode == "h":
                ref = (Staged if i < len(ins) else Result)(ref, next(spare), sems.at[place])
                place += 1
            given.append(ref)
        kernel(*given, *own)
        for ref in given:
            if isinstance(ref, Staged):
                ref.wait()
            if isinstance(ref, Result):
                ref.send()
        for ref in given:
            if isinstance(ref, Result):
                ref.copy.wait()

    held_scratch = [pltpu.VMEM(shape, dtype) for shape, dtype in held]
    sems = [pltpu.SemaphoreType.DMA((len(held),))] if held else []
    return pl.pallas_call(
        body,
        out_shape=[jax.ShapeDtypeStruct(shape, dtype) for shape, dtype, _ in outs],
        in_specs=[pl.BlockSpec(memory_space=spaces[mode]) for _, mode in ins],
        out_specs=[pl.BlockSpec(memory_space=spaces[mode]) for _, _, mode in outs],
        scratch_shapes=held_scratch + list(scratch) + sems,
        compiler_params=pltpu.CompilerParams(vmem_limit_bytes=vmem * 1024 * 1024),
    )(*[x for x, _ in ins])


def own_lanes(block, which, wide):
    if wide % LANES == 0:
        return block
    return jnp.where(which % 2 == 0, block[:, :wide], block[:, wide : 2 * wide])


def lane_block(which, wide):
    return pl.ds(pl.multiple_of(which * wide // LANES * LANES, LANES), max(wide, LANES))


class Axis:
    def __init__(self, name, size, place):
        self.name, self.size, self.place = name, size, place
        self.index = lax.axis_index(name)
        self.bits = [1 << k for k in range(size.bit_length() - 1)]

    def bit(self, b):
        return (self.index // b) % 2

    def swap(self, value, b):
        return lax.ppermute(value, self.name, [(i, i ^ b) for i in range(self.size)])


def gather_pieces(axis, value, bits):
    pieces = {0: value}
    for b in reversed(bits):
        for k in sorted(pieces):
            pieces[k ^ b] = axis.swap(pieces[k], b)
    return [pieces[k] for k in range(len(pieces))]


def widen(mem, value):
    for b in reversed(mem.bits[2:]):
        other = mem.swap(value, b)
        value = jnp.where(
            mem.bit(b) == 0, jnp.concatenate([value, other], 1), jnp.concatenate([other, value], 1)
        )
    return gather_pieces(mem, value, mem.bits[:2])


def split(idx, axis, b, keep, received, dim):
    shape = list(keep.shape)
    if dim == keep.ndim - 1:
        shape[dim] //= 2
    else:
        del shape[dim]
    kernel = functools.partial(split_kernel, axis.place, b.bit_length() - 1, dim)
    return call(
        kernel, [(idx, "s"), (keep, "v"), (received, "v")], [(shape, bf16, "v")] * 2
    )


def chain(idx, keep, received, stages, axes):
    left = {axis.name: list(reversed(axis.bits)) for axis in axes}
    for axis, b in stages:
        if axis.name == "mem":
            dim = keep.ndim - 1
        else:
            dim = left[axis.name].index(b)
            left[axis.name].remove(b)
        keep, send = split(idx, axis, b, keep, received, dim)
        received = axis.swap(send, b)
    return keep, received


def total(pairs, dtype=bf16, mode="v"):
    shape = (sum(keep.shape[0] for keep, _ in pairs),) + pairs[0][0].shape[1:]
    return call(add_kernel, [(x, "v") for pair in pairs for x in pair], [(shape, dtype, mode)])[0]


def on_device(
    dp_size,
    mem_size,
    target,
    memory,
    target_lengths,
    source_lengths,
    cotangent,
    self_qkv,
    self_bias_,
    self_out,
    cross_query,
    cross_kv,
    cross_bias,
    cross_out,
    ffn_up,
    ffn_up_bias,
    ffn_down,
    ffn_down_bias,
    norm_gains,
    norm_biases,
):
    mem, dp = Axis("mem", mem_size, 0), Axis("dp", dp_size, 1)
    target, memory, cotangent = target[0], memory[0], cotangent[0]
    tlen, slen = target_lengths[0], source_lengths[0]
    length, width = target.shape
    share = memory.shape[0]
    sources = share * mem_size
    head = width // HEADS
    wide = width // mem_size
    hidden = ffn_up.shape[1]
    count = length // mem_size
    rows = width // dp_size
    idx = jnp.stack([mem.index, dp.index]).astype(jnp.int32)
    vecs = jnp.concatenate(
        [self_bias_, cross_bias, norm_gains, norm_biases, ffn_down_bias.reshape(1, width),
         ffn_up_bias.reshape(-1, width), jnp.zeros((7, width), bf16)]
    ).astype(f32)

    memory_pieces = gather_pieces(mem, memory, mem.bits)

    weights_held = [pltpu.VMEM((3, width, max(wide, LANES)), bf16)]
    q, k, v, kt, ot, lse, *mixed = call(
        functools.partial(self_forward_kernel, (mem_size, head)),
        [(idx, "s"), (tlen, "s"), (target, "h"), (self_qkv, "r"), (vecs, "h")],
        [((length, wide), bf16, "h")] * 3
        + [((wide, length), bf16, "h"), ((wide, length), f32, "h"), ((8, length), f32, "h")]
        + [((count, wide), bf16, "v")] * mem_size,
        [pltpu.VMEM((length, wide), bf16)] + weights_held + [pltpu.SemaphoreType.DMA((3,))],
    )
    mixed = [mem.swap(piece, b) if b else piece for b, piece in enumerate(mixed)]

    memory_all, mk, mv, mkt, mvt = call(
        memory_kernel,
        [(idx, "s"), (memory, "h")] + [(x, "v") for x in memory_pieces[1:]] + [(cross_kv, "h")],
        [((sources, width), bf16, "h")] * 3 + [((width, sources), bf16, "h")] * 2,
    )

    up_rows, down_rows = hidden // width * rows, hidden // dp_size
    (layer_own, up_keep, up_send, down_keep, down_send, h0, mixed_all, cq, cmt, att, clse, gcn, vec1) = call(
        functools.partial(token_kernel, (mem_size, dp_size, head)),
        [(idx, "s"), (tlen, "s"), (slen, "s"), (target, "r"), (cotangent, "r"), (self_out, "h"), (vecs, "h"),
         (cross_query, "h"), (mk, "h"), (mvt, "h"), (cross_out, "h"), (ffn_up, "h"), (ffn_down, "h")]
        + [(x, "v") for x in mixed],
        [((count, width), bf16, "v")] + [((dp_size, up_rows, HALF), bf16, "v")] * 2
        + [((dp_size, down_rows, HALF), bf16, "v")] * 2
        + [((count, width), f32, "h"), ((count, width), bf16, "h"), ((count, width), bf16, "h"),
           ((width, count), bf16, "h"), ((width, count), f32, "h"), ((8, count), f32, "h"),
           ((count, width), f32, "h"), ((16, width), f32, "h")],
        [pltpu.VMEM((count, width), bf16), pltpu.VMEM((count, width), bf16), pltpu.VMEM((sources, count), f32),
         pltpu.VMEM((count, hidden), bf16), pltpu.VMEM((count, hidden), f32), pltpu.VMEM((count, hidden), bf16),
         pltpu.VMEM((count, width), bf16), pltpu.VMEM((count, width), bf16), pltpu.SemaphoreType.DMA((2,))],
    )
    dims = (2,) * len(dp.bits)
    high = [(mem, b) for b in mem.bits[1:]]
    up_chain = chain(
        idx, up_keep.reshape(dims + up_keep.shape[1:]), mem.swap(up_send, 1).reshape(dims + up_keep.shape[1:]),
        [(dp, b) for b in dp.bits] + high, [dp, mem],
    )
    down_chain = chain(
        idx, down_keep.reshape(dims + down_keep.shape[1:]), mem.swap(down_send, 1).reshape(dims + down_keep.shape[1:]),
        [(dp, b) for b in dp.bits[1:] + dp.bits[:1]] + high, [dp, mem],
    )

    gk, gv, gcq, gcb, gsb, gsn, vec2, *gsm = call(
        functools.partial(cross_backward_kernel, (mem_size, head)),
        [(idx, "s"), (tlen, "s"), (slen, "s"), (gcn, "h"), (cross_out, "h"), (cq, "h"), (clse, "h"), (att, "h"),
         (mk, "h"), (mv, "h"), (mkt, "h"), (cross_query, "h"), (vecs, "h"), (h0, "h"), (self_out, "h")],
        [((sources, width), bf16, "h")] * 2 + [((count, width), bf16, "h")] * 3
        + [((count, width), f32, "h"), ((16, width), f32, "h")] + [((count, wide), bf16, "v")] * mem_size,
        [pltpu.VMEM((sources, count), f32), pltpu.VMEM((width, count), f32)],
    )
    gsm = [mem.swap(piece, b) if b else piece for b, piece in enumerate(gsm)]

    middle_rows = 5 * rows + vec1.shape[0] + vec2.shape[0]
    middle_keep, middle_send, memory_keep, memory_send = call(
        functools.partial(middle_kernel, (mem_size, dp_size)),
        [(x, "s" if i == 0 else "h") for i, x in enumerate(
            [idx, gk, gv, memory_all, cross_kv, cmt, gcb, h0, vecs, gcq, mixed_all, gsb, vec1, vec2])],
        [((dp_size, middle_rows, HALF), bf16, "v")] * 2 + [((mem_size // 2, share, width), bf16, "v")] * 2,
    )
    gsm[0], middle_send, memory_send = lax.optimization_barrier((gsm[0], middle_send, memory_send))
    middle_chain = chain(
        idx, middle_keep.reshape(dims + middle_keep.shape[1:]),
        mem.swap(middle_send, 1).reshape(dims + middle_keep.shape[1:]),
        high + [(dp, b) for b in dp.bits], [dp, mem],
    )
    memory_dims = (2,) * (len(mem.bits) - 1) + (share, width)
    keep, received = memory_keep.reshape(memory_dims), mem.swap(memory_send, 1).reshape(memory_dims)
    for b in reversed(mem.bits[1:]):
        keep, send = split(idx, mem, b, keep, received, 0)
        received = mem.swap(send, b)
    memory_grad = total([(keep, received)], f32, "h")

    qkv_packed, target_keep, target_send = call(
        functools.partial(self_backward_kernel, (mem_size, dp_size, head)),
        [(idx, "s"), (tlen, "s"), (q, "h"), (k, "h"), (v, "h"), (ot, "h"), (lse, "h"), (kt, "h"), (target, "h"),
         (self_qkv, "r"), (gsn, "h")] + [(x, "v") for x in gsm],
        [((dp_size, rows + 16, 3 * wide), bf16, "v")] + [((mem_size // 2, count, width), bf16, "v")] * 2,
        [pltpu.VMEM((length, wide), bf16), pltpu.VMEM((length, 3 * wide), bf16), pltpu.VMEM((length, wide), f32),
         pltpu.VMEM((length, wide), f32), pltpu.VMEM((wide, length), f32)] + weights_held
        + [pltpu.SemaphoreType.DMA((3,))],
    )
    value = qkv_packed.reshape(dims + qkv_packed.shape[1:])
    first = dp.bits[0]
    at = len(dims) - 1
    keep = lax.dynamic_index_in_dim(value, dp.bit(first), at, keepdims=False)
    received = dp.swap(lax.dynamic_index_in_dim(value, 1 - dp.bit(first), at, keepdims=False), first)
    for n, b in enumerate(dp.bits[1:]):
        keep, send = split(idx, dp, b, keep, received, len(dims) - 2 - n)
        received = dp.swap(send, b)
    qkv_sum = total([(keep, received)])

    value = total([(target_keep, mem.swap(target_send, 1))])
    for b in mem.bits[1:]:
        value = total([(value, mem.swap(value, b))])
    target_grad = call(
        target_kernel,
        [(idx, "s"), (value, "v"), (mem.swap(value, 1), "v")],
        [((length, width), f32, "r")],
        [pltpu.VMEM((mem_size, count, width), f32), pltpu.SemaphoreType.DMA((mem_size,))],
    )[0]

    layer_output = call(
        rows_kernel,
        [(idx, "s")] + [(x, "v") for x in gather_pieces(mem, layer_own, mem.bits)],
        [((length, width), bf16, "r")],
        [pltpu.SemaphoreType.DMA((mem_size,))],
    )[0]

    up_grad, down_grad = call(
        ffn_out_kernel,
        [(idx, "s")] + [(x, "v") for x in widen(mem, total([up_chain, down_chain]))],
        [((rows, hidden), f32, "h"), ((down_rows, width), f32, "h")],
    )
    co_grad, cq_grad, so_grad, kv_grad, cb_grad, ub_grad, db_grad, gain_grad, shift_grad, vec = call(
        functools.partial(middle_out_kernel, hidden // width),
        [(idx, "s")] + [(x, "v") for x in widen(mem, total([middle_chain]))],
        [((rows, width), f32, "h")] * 3 + [((rows, 2 * width), f32, "h"), ((3, rows), f32, "v"),
         ((1, hidden // dp_size), f32, "v"), ((1, rows), f32, "v"), ((3, rows), f32, "v"), ((3, rows), f32, "v"),
         ((32, width), f32, "v")],
    )
    qkv_grad, sb_grad = call(
        qkv_out_kernel,
        [(idx, "s"), (vec, "v")] + [(x, "v") for x in gather_pieces(mem, qkv_sum, mem.bits)],
        [((rows, 3 * width), f32, "h"), ((3, rows), f32, "v")],
        [pltpu.VMEM((8, 3 * width), f32)],
    )
    return (
        layer_output[None],
        target_grad[None],
        memory_grad[None],
        qkv_grad,
        sb_grad,
        so_grad,
        cq_grad,
        kv_grad,
        cb_grad,
        co_grad,
        up_grad,
        ub_grad.reshape(-1),
        down_grad,
        db_grad.reshape(-1),
        gain_grad,
        shift_grad,
    )


def solution(mesh):
    row, whole = P("dp", None, None), P()
    in_specs = (row, P("dp", "mem", None), P("dp", None), P("dp", None), row) + (whole,) * 13
    out_specs = (
        row,
        row,
        P("dp", "mem", None),
        P("dp", None),
        P(None, "dp"),
        P("dp", None),
        P("dp", None),
        P("dp", None),
        P(None, "dp"),
        P("dp", None),
        P("dp", None),
        P("dp"),
        P("dp", None),
        P("dp"),
        P(None, "dp"),
        P(None, "dp"),
    )
    body = functools.partial(on_device, mesh.shape["dp"], mesh.shape["mem"])
    return jax.shard_map(body, mesh=mesh, in_specs=in_specs, out_specs=out_specs, check_vma=False)
```

```python
import functools

import jax
import jax.numpy as jnp
from jax import lax
from jax.experimental import pallas as pl
from jax.experimental.pallas import tpu as pltpu
from jax.sharding import PartitionSpec as P

HEADS = 8
SEG_MOST = 512
LANES = 128
HALF = 256
very_negative = -1e30
epsilon = 1e-05
SELF_BIAS, CROSS_BIAS, GAINS, SHIFTS, DOWN_BIAS, UP_BIAS = 0, 3, 6, 9, 12, 13
f32 = jnp.float32
bf16 = jnp.bfloat16


def mm(left, right):
    return jnp.dot(left, right, preferred_element_type=f32)


def mm_tn(left, right):
    return lax.dot_general(left, right, (((0,), (0,)), ((), ())), preferred_element_type=f32)


def mm_nt(left, right):
    return lax.dot_general(left, right, (((1,), (1,)), ((), ())), preferred_element_type=f32)


def norm_parts(hidden):
    center = hidden - jnp.mean(hidden, axis=-1, keepdims=True)
    scaled = lax.rsqrt(jnp.mean(center * center, axis=-1, keepdims=True) + epsilon)
    return center * scaled, scaled


def norm_backward(upstream, normed, scaled, gain_row):
    gained = upstream * gain_row
    gained_mean = jnp.mean(gained, axis=-1, keepdims=True)
    mean_cross = jnp.mean(gained * normed, axis=-1, keepdims=True)
    return scaled * (gained - gained_mean - normed * mean_cross)


def sums(matrix):
    return jnp.sum(matrix.astype(f32), axis=0, keepdims=True)


def started(lengths, places, ends, amounts):
    total = jnp.zeros(places.shape, jnp.int32)
    edge = jnp.int32(0)
    for j in range(lengths.shape[0]):
        if ends:
            edge = edge + lengths[j]
        total = total + jnp.where(places >= edge, amounts[j], 0)
        if not ends:
            edge = edge + lengths[j]
    return total


def head_lanes(value, h, head):
    if value.shape[-1] == head:
        return value
    lanes = lax.broadcasted_iota(jnp.int32, value.shape, 1)
    return jnp.where(lanes // head == h, value, jnp.zeros_like(value))


def self_bias(tlen_ref, begin, first, count):
    queries = begin + lax.broadcasted_iota(jnp.int32, (1, count), 1)
    start = started(tlen_ref, queries, True, tlen_ref)
    keys = first + lax.broadcasted_iota(jnp.int32, (begin + count - first, count), 0)
    return jnp.where((keys >= start) & (keys <= queries), 0.0, very_negative)


def self_forward_kernel(
    sizes, idx, tlen, target, qkv, shifts, q_out, k_out, v_out, kt_out, ot_out, lse_out, *rest
):
    mem, head = sizes
    pieces, (mixed, held, sem) = rest[:mem], rest[mem:]
    length = target.shape[0]
    wide = q_out.shape[1]
    share = length // mem
    weights = own_weights(idx, qkv, held, sem, wide)
    zero = jnp.zeros((1, wide), f32)
    block = lane_block(idx[0], wide)
    shift = [own_lanes(shifts.value()[i : i + 1, block].astype(f32), idx[0], wide) for i in (0, 1)]
    shift = jnp.concatenate([shift[0], zero, shift[1]], axis=1)
    for at in range(0, length, HALF):
        rows = slice(at, at + HALF)
        part = (mm(target[rows, :], weights) + shift).astype(bf16)
        q_out[rows, :] = part[:, :wide]
        k_out[rows, :] = part[:, wide : 2 * wide]
        v_out[rows, :] = part[:, 2 * wide :]
        kt_out[:, rows] = part[:, wide : 2 * wide].T
        mixed[rows, :] = part[:, 2 * wide :]
    for out in (q_out, k_out, v_out, kt_out):
        out.send()
    vt = mixed[...].T
    lse_out[...] = jnp.zeros(lse_out.shape, f32)
    for at in range(0, length, HALF):
        first = max(0, at - SEG_MOST)
        keys, cols = slice(first, at + HALF), slice(at, at + HALF)
        bias = self_bias(tlen, at, first, HALF)
        q = q_out[cols, :] * jnp.asarray(head**-0.5, bf16)
        for h in range(wide // head):
            scores = mm_nt(k_out[keys, :], head_lanes(q, h, head)) + bias
            top = jnp.max(scores, axis=0, keepdims=True)
            terms = jnp.exp(scores - top)
            total = jnp.sum(terms, axis=0, keepdims=True)
            part = mm(vt[h * head : (h + 1) * head, keys], terms.astype(bf16)) / total
            ot_out[h * head : (h + 1) * head, cols] = part
            lse_out[h : h + 1, cols] = top + jnp.log(total)
        mixed[cols, :] = ot_out[:, cols].T.astype(bf16)
    for b in range(mem):
        at = pl.multiple_of((idx[0] ^ b) * share, share)
        pieces[b][...] = mixed[pl.ds(at, share), :]


def memory_kernel(idx, *refs):
    pieces, (weights, all_out, k_out, v_out, kt_out, vt_out) = refs[:-6], refs[-6:]
    share, width = pieces[0].shape
    for b, piece in enumerate(pieces):
        at = pl.multiple_of((idx[0] ^ b) * share, share)
        all_out[pl.ds(at, share), :] = piece[...]
        both = mm(piece[...], weights[...]).astype(bf16)
        k_out[pl.ds(at, share), :] = both[:, :width]
        v_out[pl.ds(at, share), :] = both[:, width:]
        kt_out[:, pl.ds(at, share)] = both[:, :width].T
        vt_out[:, pl.ds(at, share)] = both[:, width:].T


def cross_bias_of(idx, tlen, slen, count, keys):
    queries = idx[0] * count + lax.broadcasted_iota(jnp.int32, (1, count), 1)
    low = started(tlen, queries, True, slen)
    high = started(tlen, queries, False, slen)
    places = lax.broadcasted_iota(jnp.int32, (keys, count), 0)
    return jnp.where((places >= low) & (places < high), 0.0, very_negative)


def column_of(row, count):
    return jnp.broadcast_to(row, (count, row.shape[1])).T


def token_kernel(
    sizes, idx, tlen, slen, target, cotangent, wo, vecs, cq, keys, vt, co, up, down, *rest,
):
    mem, dp, head = sizes
    pieces = rest[:mem]
    (lo_out, up_keep, up_send, down_keep, down_send, h0_out, mixed_out, q_out, att_out, lse_out, gcn_out,
     vec_out, x, ct, bias, act, fac, gi, gfo_s, acl_s, gcb_s, sem) = rest[mem:]
    count, width = lo_out.shape
    wide = width // mem
    hidden = up.shape[1]
    share = pl.ds(pl.multiple_of(idx[0] * count, count), count)
    copies = [
        pltpu.make_async_copy(target.at[share, :], x, sem.at[0]),
        pltpu.make_async_copy(cotangent.at[share, :], ct, sem.at[1]),
    ]
    for copy in copies:
        copy.start()
    bias[...] = cross_bias_of(idx, tlen, slen, count, keys.shape[0])
    row = lambda i: vecs[i : i + 1, :]
    copies[0].wait()
    h0 = x[...].astype(f32) + row(SELF_BIAS + 2)
    for b in range(mem):
        at = pl.multiple_of((idx[0] ^ b) * wide, wide)
        h0 = h0 + mm(pieces[b][...], wo.value()[pl.ds(at, wide), :])
        mixed_out[:, b * wide : (b + 1) * wide] = pieces[b][...]
    h0_out[...] = h0
    mixed_out.send()
    h0_out.send()
    normed0, _ = norm_parts(h0)
    after_self = normed0 * row(GAINS) + row(SHIFTS)
    q = (mm(after_self.astype(bf16), cq[...]) + row(CROSS_BIAS)).astype(bf16)
    q_out[...] = q
    q_out.send()
    q = q * jnp.asarray(head**-0.5, bf16)
    for h in range(HEADS):
        pair = slice(h * head // LANES * LANES, h * head // LANES * LANES + LANES)
        scores = mm_nt(keys[:, pair], head_lanes(q[:, pair], h % (LANES // head), head)) + bias[...]
        top = jnp.max(scores, axis=0, keepdims=True)
        terms = jnp.exp(scores - top)
        total = jnp.sum(terms, axis=0, keepdims=True)
        own = slice(h * head, (h + 1) * head)
        att_out[own, :] = mm(vt[own, :], terms.astype(bf16)) / total
        lse_out[h : h + 1, :] = top + jnp.log(total)
    cmt = (att_out[...] + column_of(row(CROSS_BIAS + 1), count)).astype(bf16)
    for out in (att_out, lse_out):
        out.send()
    normed1, scaled1 = norm_parts(after_self + mm_tn(cmt, co[...]) + row(CROSS_BIAS + 2))
    after_cross = normed1 * row(GAINS + 1) + row(SHIFTS + 1)
    acl = after_cross.astype(bf16)
    acl_s[...] = acl
    step = width
    h2 = after_cross + row(DOWN_BIAS)
    for i, at in enumerate(range(0, hidden, step)):
        cols = slice(at, at + step)
        inner = mm(acl, up[:, cols]) + row(UP_BIAS + i)
        sig = jax.nn.sigmoid(inner)
        part = (inner * sig).astype(bf16)
        act[:, cols] = part
        fac[:, cols] = sig * (1.0 + inner * (1.0 - sig))
        h2 = h2 + mm(part, down[cols, :])
    normed2, scaled2 = norm_parts(h2)
    lo_out[...] = (normed2 * row(GAINS + 2) + row(SHIFTS + 2)).astype(bf16)
    copies[1].wait()
    cot = ct[...].astype(f32)
    gf = norm_backward(cot, normed2, scaled2, row(GAINS + 2))
    gfo = gf.astype(bf16)
    gfo_s[...] = gfo
    u1 = gf
    vec_out[...] = jnp.zeros(vec_out.shape, f32)
    for i, at in enumerate(range(0, hidden, step)):
        cols = slice(at, at + step)
        part = (mm_nt(gfo, down[cols, :]) * fac[:, cols]).astype(bf16)
        gi[:, cols] = part
        u1 = u1 + mm_nt(part, up[:, cols])
        vec_out[5 + i : 6 + i, :] = sums(part)
    gcn = norm_backward(u1, normed1, scaled1, row(GAINS + 1))
    gcn_out[...] = gcn
    gcb_s[...] = gcn.astype(bf16)
    for i, part in enumerate((u1 * normed1, u1, cot * normed2, cot, gfo)):
        vec_out[i : i + 1, :] = sums(part)
    gcn_out.send()
    vec_out.send()
    rows, hrows = width // dp, hidden // dp
    some = width // hrows
    for up_out, down_out, side in ((up_send, down_send, 1 - idx[0] % 2), (up_keep, down_keep, idx[0] % 2)):
        start = side * HALF
        cols = pl.ds(pl.multiple_of(start, HALF), HALF)
        for i in range(hidden // width):
            part = mm_tn(act[:, i * width : (i + 1) * width], gfo_s[:, cols]).astype(bf16)
            down_out[i * some : (i + 1) * some] = part.reshape(some, hrows, HALF)
        part = mm(cmt, gcb_s[:, cols]).astype(bf16)
        last = hidden // width * rows
        up_out[:, last : last + rows, :] = part.reshape(dp, rows, HALF)
        for i in range(hidden // width):
            cols = pl.ds(pl.multiple_of(start + i * width, HALF), HALF)
            part = mm_tn(acl_s[...], gi[:, cols]).astype(bf16)
            up_out[:, i * rows : (i + 1) * rows, :] = part.reshape(dp, rows, HALF)


def cross_backward_kernel(
    sizes, idx, tlen, slen, gcn, co, q_ref, lse, att, keys, values, kt, cq, vecs, h0, wo,
    gk_out, gv_out, gcq_out, gsb_out, gsn_out, vec_out, *rest,
):
    mem, head = sizes
    pieces, (bias, gcqt) = rest[:mem], rest[mem:]
    count, width = gcn.shape
    wide = width // mem
    bias[...] = cross_bias_of(idx, tlen, slen, count, keys.shape[0])
    gcb = gcn[...].astype(bf16)
    gcm = mm_nt(gcb, co[...]).astype(bf16)
    gcmt = mm_nt(co[...], gcb).astype(bf16)
    scale = head**-0.5
    q = q_ref[...] * jnp.asarray(scale, bf16)
    for p in range(width // LANES):
        pair = slice(p * LANES, (p + 1) * LANES)
        gk = gv = 0.0
        for i in range(LANES // head):
            h = p * (LANES // head) + i
            own = slice(h * head, (h + 1) * head)
            delta = jnp.sum(gcmt[own, :].astype(f32) * att[own, :], axis=0, keepdims=True)
            qh, gh = head_lanes(q[:, pair], i, head), head_lanes(gcm[:, pair], i, head)
            probs = jnp.exp(mm_nt(keys[:, pair], qh) + bias[...] - lse[h : h + 1, :])
            ds = (probs * (mm_nt(values[:, pair], gh) - delta)).astype(bf16)
            gv = gv + mm(probs.astype(bf16), gh)
            gk = gk + mm(ds, qh)
            gcqt[own, :] = mm(kt[own, :], ds) * scale
        gk_out[:, pair] = gk.astype(bf16)
        gv_out[:, pair] = gv.astype(bf16)
    gk_out.send()
    gv_out.send()
    gcq = gcqt[...].T.astype(bf16)
    gcq_out[...] = gcq
    gcq_out.send()
    u0 = gcn[...] + mm_nt(gcq, cq[...])
    normed0, scaled0 = norm_parts(h0[...])
    gsn = norm_backward(u0, normed0, scaled0, vecs[GAINS : GAINS + 1, :])
    gsn_out[...] = gsn
    gsb = gsn.astype(bf16)
    gsb_out[...] = gsb
    for b in range(mem):
        at = pl.multiple_of((idx[0] ^ b) * wide, wide)
        pieces[b][...] = mm_nt(gsb, wo.value()[pl.ds(at, wide), :]).astype(bf16)
    vec_out[...] = jnp.zeros(vec_out.shape, f32)
    for i, part in enumerate((gsb, gcq, gcm, gcb, u0 * normed0, u0)):
        vec_out[i : i + 1, :] = sums(part)


def middle_kernel(
    sizes, idx, gk, gv, memory, wkv, h0, vecs, gcq, mixed, gsb, vec1, vec2,
    keep_out, send_out,
):
    mem, dp = sizes
    width = gsb.shape[1]
    wide, share = width // mem, memory.shape[0] // mem
    rows = width // dp
    place = keep_out.shape[0] - mem // 2 * 2 * share
    for out, side in ((send_out, 1 - idx[0] % 2), (keep_out, idx[0] % 2)):
        for i in range(mem // 2):
            at = pl.ds(pl.multiple_of((2 * i + side) * share, share), share)
            part = mm_nt(gk.value()[at, :], wkv[:, :width]) + mm_nt(gv.value()[at, :], wkv[:, width:])
            for k in range(2):
                rest = place + (2 * i + k) * share
                out[rest : rest + share, :] = part[:, k * HALF : (k + 1) * HALF].astype(bf16)
    normed0, _ = norm_parts(h0[...])
    asl = (normed0 * vecs[GAINS : GAINS + 1, :] + vecs[SHIFTS : SHIFTS + 1, :]).astype(bf16)
    vec = jnp.concatenate([vec1[...], vec2[...]], axis=0).astype(bf16)
    some, per = wide // rows, 4 * rows + vec.shape[0]
    for out, side in ((send_out, 1 - idx[0] % 2), (keep_out, idx[0] % 2)):
        cols = pl.ds(pl.multiple_of(side * HALF, HALF), HALF)

        def put(at, matrix):
            for d in range(dp):
                first = d * per + at * rows
                out[first : first + rows, :] = matrix[d * rows : (d + 1) * rows].astype(bf16)

        put(0, mm_tn(asl, gcq.value()[:, cols]))
        part = mm_tn(mixed[...], gsb.value()[:, cols]).astype(bf16)
        for b in range(mem):
            j = idx[0] ^ b
            for i in range(some):
                first = pl.multiple_of((j * some + i) * per + rows, 16)
                out[pl.ds(first, rows), :] = part[b * wide + i * rows : b * wide + (i + 1) * rows]
        put(2, mm_tn(memory[...], gk.value()[:, cols]))
        put(3, mm_tn(memory[...], gv.value()[:, cols]))
        vrows = vec.shape[0]
        half = jnp.where(side == 0, vec[:, :HALF], vec[:, HALF:])
        for d in range(dp):
            out[(d + 1) * per - vrows : (d + 1) * per, :] = half


def self_backward_kernel(
    sizes, idx, tlen, q_ref, k_ref, v_ref, ot, lse, kt, target, qkv, gsn, *rest
):
    mem, dp, head = sizes
    pieces = rest[:mem]
    qkv_keep, qkv_send, keep_out, send_out, go, gproj, gk, gv, gqt, qkv_out, held, sem = rest[mem:]
    length, wide = q_ref.shape
    share, width = gsn.shape
    copies = own_weights_copies(idx, qkv, held, sem, wide)
    for b in range(mem):
        at = pl.multiple_of((idx[0] ^ b) * share, share)
        go[pl.ds(at, share), :] = pieces[b][...]
    gk[...] = jnp.zeros_like(gk)
    gv[...] = jnp.zeros_like(gv)
    scale = head**-0.5
    for at in range(0, length, HALF):
        first = max(0, at - SEG_MOST)
        keys, cols = slice(first, at + HALF), slice(at, at + HALF)
        bias = self_bias(tlen, at, first, HALF)
        q = q_ref[cols, :] * jnp.asarray(scale, bf16)
        grad = go[cols, :]
        product = grad.astype(f32).T * ot[:, cols]
        for h in range(wide // head):
            own = slice(h * head, (h + 1) * head)
            delta = jnp.sum(product[own, :], axis=0, keepdims=True)
            qh, gh = head_lanes(q, h, head), head_lanes(grad, h, head)
            probs = jnp.exp(mm_nt(k_ref[keys, :], qh) + bias - lse[h : h + 1, cols])
            ds = (probs * (mm_nt(v_ref[keys, :], gh) - delta)).astype(bf16)
            gv[keys, :] += mm(probs.astype(bf16), gh)
            gk[keys, :] += mm(ds, qh)
            gqt[own, cols] = mm(kt[own, keys], ds) * scale
    gproj[:, :wide] = gqt[...].T.astype(bf16)
    gproj[:, wide : 2 * wide] = gk[...].astype(bf16)
    gproj[:, 2 * wide :] = gv[...].astype(bf16)
    rows = width // dp
    qkv_out[:, :rows, :] = mm_tn(target[...], gproj[...]).astype(bf16).reshape(dp, rows, 3 * wide)
    total = sums(gproj[...]).astype(bf16)
    pad = qkv_out.shape[1] - rows
    qkv_out[:, rows:, :] = jnp.broadcast_to(total[None], (dp, pad, 3 * wide))
    for out, side in ((qkv_send, 1 - idx[1] % 2), (qkv_keep, idx[1] % 2)):
        for i in range(dp // 2):
            out[i] = qkv_out[2 * i + side]
    weights = own_weights_value(idx, copies, held, wide)
    for out, side in ((send_out, 1 - idx[0] % 2), (keep_out, idx[0] % 2)):
        for i in range(mem // 2):
            at = pl.multiple_of((2 * i + side) * share, share)
            out[i] = mm_nt(gproj[pl.ds(at, share), :], weights).astype(bf16)
    at = pl.multiple_of(idx[0] * share, share)
    part = mm_nt(gproj[pl.ds(at, share), :], weights) + gsn[...]
    keep_out[idx[0] // 2] = part.astype(bf16)


def own_weights_copies(idx, qkv, held, sem, wide):
    width, full = qkv.shape[0], qkv.shape[1] // 3
    lanes = max(wide, LANES)
    copies = []
    for c in range(3):
        at = pl.multiple_of(c * full + idx[0] * wide // LANES * LANES, LANES)
        copies.append(pltpu.make_async_copy(qkv.at[:, pl.ds(at, lanes)], held.at[c], sem.at[c]))
        copies[-1].start()
    return copies


def own_weights_value(idx, copies, held, wide):
    for copy in copies:
        copy.wait()
    return jnp.concatenate([own_lanes(held[c], idx[0], wide) for c in range(3)], axis=1)


def own_weights(idx, qkv, held, sem, wide):
    return own_weights_value(idx, own_weights_copies(idx, qkv, held, sem, wide), held, wide)


def split_kernel(axis_at, bit_at, dim, idx, keep, received, keep_out, send_out):
    bit = (idx[axis_at] >> bit_at) & 1
    if dim == keep.ndim - 1:
        total = keep[...].astype(f32) + received[...].astype(f32)
        middle = keep.shape[-1] // 2
        low, high = total[..., :middle], total[..., middle:]
        keep_out[...] = jnp.where(bit == 0, low, high).astype(bf16)
        send_out[...] = jnp.where(bit == 0, high, low).astype(bf16)
        return
    lead = (slice(None),) * dim
    for out, which in ((send_out, 1 - bit), (keep_out, bit)):
        out[...] = (keep[lead + (which,)].astype(f32) + received[lead + (which,)].astype(f32)).astype(bf16)


def add_kernel(idx, *refs):
    out, pairs, at = refs[-1], refs[:-1], 0
    for keep, received in zip(pairs[::2], pairs[1::2]):
        part = keep[...].astype(f32) + received[...].astype(f32)
        out[at : at + part.shape[0]] = part.astype(out.dtype)
        at += part.shape[0]


def join_kernel(parts, idx, keep, received, *refs):
    more, out = refs[:-1], refs[-1]
    for i in range(parts):
        out[i] = (keep[i].astype(f32) + received[i].astype(f32)).astype(bf16)
    at = parts
    for ref in more or (keep, received):
        if more:
            out[at] = ref[...]
            at += 1
            continue
        for i in range(parts, ref.shape[0]):
            out[at] = ref[i]
            at += 1


def rows_out_kernel(masks, idx, own, other, target_out, layer_out, held, sem):
    share = own.shape[1]
    copies = []
    blocks = own.shape[0] - len(masks)

    def send(source, out, at):
        at = pl.ds(pl.multiple_of(at * share, share), share)
        copies.append(pltpu.make_async_copy(source, out.at[at, :], sem.at[len(copies)]))
        copies[-1].start()

    for ref, flip in ((own, 0), (other, 1)):
        for i, mask in enumerate(masks):
            send(ref.at[blocks + i], layer_out, idx[0] ^ (mask + flip))
    for i in range(blocks):
        for k, ref in enumerate((own, other)):
            held[2 * i + k] = ref[i].astype(f32)
            send(held.at[2 * i + k], target_out, 2 * i + (idx[0] + k) % 2)
    for copy in copies:
        copy.wait()


def ffn_out_kernel(idx, own, other, up_out, down_out, co_out):
    rows, width = co_out.shape
    blocks = up_out.shape[1] // width
    for piece, side in ((own, idx[0] % 2), (other, 1 - idx[0] % 2)):
        for i in range(blocks):
            at = pl.multiple_of(i * width + side * HALF, HALF)
            up_out.held[:, pl.ds(at, HALF)] = piece[i * rows : (i + 1) * rows, :].astype(f32)
        cols = pl.ds(pl.multiple_of(side * HALF, HALF), HALF)
        co_out.held[:, cols] = piece[blocks * rows : (blocks + 1) * rows, :].astype(f32)
        down_out.held[:, cols] = piece[(blocks + 1) * rows :, :].astype(f32)


def lanes_from(ref, first, count, at, wide):
    if wide % LANES == 0:
        return ref[pl.ds(first, count), pl.ds(pl.multiple_of(at, LANES), wide)]
    block = ref[pl.ds(first, count), pl.ds(pl.multiple_of(at // LANES * LANES, LANES), LANES)]
    result = block[:, :wide]
    for k in range(1, LANES // wide):
        result = jnp.where(at % LANES == k * wide, block[:, k * wide : (k + 1) * wide], result)
    return result


def middle_out_kernel(count, idx, qkv_sums, *refs):
    pieces = refs[:-10]
    cq_out, so_out, kv_out, cb_out, ub_out, db_out, gain_out, shift_out, sb_out, vec = refs[-10:]
    rows, width = cq_out.shape
    for b, piece in enumerate(pieces):
        other = idx[0] ^ b
        at = other % 2 * HALF + other // 2 % 2 * LANES
        cols = pl.ds(pl.multiple_of(at, LANES), LANES)
        for i, out in enumerate((cq_out, so_out)):
            out.held[:, cols] = piece[i * rows : (i + 1) * rows, :].astype(f32)
        for i in range(2):
            part = piece[(2 + i) * rows : (3 + i) * rows, :].astype(f32)
            kv_out.held[:, pl.ds(pl.multiple_of(i * width + at, LANES), LANES)] = part
        vec[:, cols] = piece[4 * rows :, :].astype(f32)
    here = idx[1] * rows
    take = lambda first, count: lanes_from(vec, first, count, here, rows)
    cb_out[...] = take(17, 3)
    db_out[...] = take(4, 1)
    for out, places in ((gain_out, (20, 0, 2)), (shift_out, (21, 1, 3))):
        for i, first in enumerate(places):
            out[i : i + 1, :] = take(first, 1)
    per = ub_out.shape[1]
    first = idx[1] * per
    part = lanes_from(vec, 5, 1, first % width, per)
    for i in range(1, count):
        part = jnp.where(first // width == i, lanes_from(vec, 5 + i, 1, first % width, per), part)
    ub_out[...] = part
    for i, (ref, at) in enumerate(((qkv_sums, 0), (qkv_sums, 2 * width), (vec, 0))):
        sb_out[i : i + 1, :] = lanes_from(ref, 16 if ref is vec else 0, 1, at + here, rows)


def qkv_out_kernel(idx, *refs):
    pieces, (qkv_out, full) = refs[:-2], refs[-2:]
    rows, width = qkv_out.shape[0], qkv_out.shape[1] // 3
    wide = pieces[0].shape[1] // 3

    def put(out, first, count):
        for c in range(3):
            lanes = slice(c * wide, (c + 1) * wide)
            parts = [piece[first : first + count, lanes].astype(f32) for piece in pieces]
            if wide < LANES:
                odd = idx[0] % 2
                parts = [
                    jnp.where(odd == 0, jnp.concatenate([a, b], 1), jnp.concatenate([b, a], 1))
                    for a, b in zip(parts[::2], parts[1::2])
                ]
            for b, part in enumerate(parts):
                j = idx[0] ^ b if wide >= LANES else (idx[0] // 2) ^ b
                at = pl.multiple_of(c * width + j * max(wide, LANES), LANES)
                out[:count, pl.ds(at, max(wide, LANES))] = part

    put(qkv_out.held, 0, rows)
    put(full, rows, full.shape[0])


def middle_columns_kernel(bit_at, count, idx, keep, received, keep_out, memory_out, send_out):
    bit = (idx[0] >> bit_at) & 1
    per = keep_out.shape[1]
    for d in range(keep_out.shape[0]):
        at = slice(d * per, (d + 1) * per)
        total = keep[at, :].astype(f32) + received[at, :].astype(f32)
        low, high = total[:, :LANES], total[:, LANES:]
        keep_out[d] = jnp.where(bit == 0, low, high).astype(bf16)
        send_out[at, :] = jnp.where(bit == 0, high, low).astype(bf16)
    place = keep_out.shape[0] * per
    share = memory_out.shape[1]
    for i in range(memory_out.shape[0]):
        for k in range(2):
            for which in (0, 1):
                side = bit if which else 1 - bit
                at = pl.ds(pl.multiple_of(place + ((2 * i + side) * 2 + k) * share, 16), share)
                total = (keep[at, :].astype(f32) + received[at, :].astype(f32)).astype(bf16)
                if which:
                    memory_out[i, :, k * HALF : (k + 1) * HALF] = total
                    continue
                for n in range(HALF // LANES):
                    rest = place + ((i * 2 + k) * 2 + n) * share
                    send_out[rest : rest + share, :] = total[:, n * LANES : (n + 1) * LANES]


def middle_rows_kernel(bit_at, idx, keep, memory, received, keep_out, send_out, memory_out):
    bit = (idx[1] >> bit_at) & 1
    per = keep.shape[2]
    for out, side in ((send_out, 1 - bit), (keep_out, bit)):
        for i in range(keep.shape[0]):
            at = pl.ds(pl.multiple_of((2 * i + side) * per, 16), per)
            out[i] = (keep[i, side].astype(f32) + received[at, :].astype(f32)).astype(bf16)
    place = keep.shape[0] * 2 * per
    share = memory.shape[1]
    for i in range(memory.shape[0]):
        for k in range(memory.shape[2] // LANES):
            cols = slice(k * LANES, (k + 1) * LANES)
            rest = place + (i * (memory.shape[2] // LANES) + k) * share
            total = memory[i, :, cols].astype(f32) + received[rest : rest + share, :].astype(f32)
            memory_out[i * share : (i + 1) * share, cols] = total.astype(memory_out.dtype)


class Staged:
    def __init__(self, source, held, sem):
        self.held, self.shape, self.dtype = held, held.shape, held.dtype
        self.copy = pltpu.make_async_copy(source, held, sem)
        self.copy.start()
        self.waited = False

    def wait(self):
        if not self.waited:
            self.copy.wait()
            self.waited = True

    def __getitem__(self, at):
        self.wait()
        return self.held[at]

    def value(self):
        self.wait()
        return self.held


class Result:
    def __init__(self, place, held, sem):
        self.held, self.shape, self.dtype = held, held.shape, held.dtype
        self.copy, self.sent = pltpu.make_async_copy(held, place, sem), False

    def __getitem__(self, at):
        return self.held[at]

    def __setitem__(self, at, value):
        self.held[at] = value

    def send(self):
        if not self.sent:
            self.copy.start()
            self.sent = True


class Plain:
    def __init__(self, ref):
        self.held, self.shape, self.dtype = ref, ref.shape, ref.dtype

    def __getitem__(self, at):
        return self.held[at]

    def __setitem__(self, at, value):
        self.held[at] = value

    def value(self):
        return self.held

    def send(self):
        pass


def call(kernel, ins, outs, scratch=(), vmem=16, us=1.0):
    ins = [(pltpu.with_memory_space_constraint(x, pltpu.HBM) if mode in "hr" else x, mode) for x, mode in ins]
    spaces = {"s": pltpu.SMEM, "v": pltpu.VMEM, "w": pltpu.VMEM, "h": pltpu.HBM, "r": pltpu.HBM}
    held = [(x.shape, x.dtype) for x, mode in ins if mode == "h"]
    held += [(shape, dtype) for shape, dtype, mode in outs if mode == "h"]
    modes = [mode for _, mode in ins] + [mode for _, _, mode in outs]

    def body(*refs):
        count = len(modes)
        own = refs[count + len(held) : len(refs) - 1 if held else len(refs)]
        spare, sems = iter(refs[count : count + len(held)]), refs[-1]
        given, place = [], 0
        for i, mode in enumerate(modes):
            ref = refs[i]
            if mode == "h":
                ref = (Staged if i < len(ins) else Result)(ref, next(spare), sems.at[place])
                place += 1
            if mode == "w":
                ref = Plain(ref)
            given.append(ref)
        kernel(*given, *own)
        for ref in given:
            if isinstance(ref, Staged):
                ref.wait()
            if isinstance(ref, Result):
                ref.send()
        for ref in given:
            if isinstance(ref, Result):
                ref.copy.wait()

    held_scratch = [pltpu.VMEM(shape, dtype) for shape, dtype in held]
    sems = [pltpu.SemaphoreType.DMA((len(held),))] if held else []
    return pl.pallas_call(
        body,
        out_shape=[
            (pltpu.HBM if mode in "hr" else jax.ShapeDtypeStruct)(shape, dtype) for shape, dtype, mode in outs
        ],
        in_specs=[pl.BlockSpec(memory_space=spaces[mode]) for _, mode in ins],
        out_specs=[pl.BlockSpec(memory_space=spaces[mode]) for _, _, mode in outs],
        scratch_shapes=held_scratch + list(scratch) + sems,
        compiler_params=pltpu.CompilerParams(vmem_limit_bytes=vmem * 1024 * 1024),
        cost_estimate=pl.CostEstimate(
            flops=int(us * 1.1e9), bytes_accessed=int(us * 1e6), transcendentals=0
        ),
    )(*[x for x, _ in ins])


def own_lanes(block, which, wide):
    if wide % LANES == 0:
        return block
    return jnp.where(which % 2 == 0, block[:, :wide], block[:, wide : 2 * wide])


def lane_block(which, wide):
    return pl.ds(pl.multiple_of(which * wide // LANES * LANES, LANES), max(wide, LANES))


class Axis:
    def __init__(self, name, size, place):
        self.name, self.size, self.place = name, size, place
        self.index = lax.axis_index(name)
        self.bits = [1 << k for k in range(size.bit_length() - 1)]

    def bit(self, b):
        return (self.index // b) % 2

    def swap(self, value, b):
        return lax.ppermute(value, self.name, [(i, i ^ b) for i in range(self.size)])


def gather_pieces(axis, value, bits):
    pieces = {0: value}
    for b in reversed(bits):
        for k in sorted(pieces):
            pieces[k ^ b] = axis.swap(pieces[k], b)
    return [pieces[k] for k in sorted(pieces)]


class Order:
    def __init__(self, idx):
        self.idx, self.token = idx, None

    def call(self, kernel, ins, outs, scratch=(), vmem=16, us=1.0):
        idx = self.idx if self.token is None else lax.optimization_barrier((self.idx, self.token))[0]
        results = call(kernel, [(idx, "s")] + ins, outs, scratch, vmem, us)
        self.token = results[0]
        return results

    def split(self, axis, b, keep, received, dim):
        shape = list(keep.shape)
        if dim == keep.ndim - 1:
            shape[dim] //= 2
        else:
            del shape[dim]
        kernel = functools.partial(split_kernel, axis.place, b.bit_length() - 1, dim)
        return self.call(kernel, [(keep, "v"), (received, "v")], [(shape, bf16, "v")] * 2)

    def total(self, pairs, dtype=bf16, mode="v"):
        shape = (sum(keep.shape[0] for keep, _ in pairs),) + pairs[0][0].shape[1:]
        return self.call(add_kernel, [(x, "v") for pair in pairs for x in pair], [(shape, dtype, mode)])[0]


class Chain:
    def __init__(self, order, keep, received, bits):
        self.order, self.keep, self.received = order, keep, received
        self.left = list(reversed(bits))

    def step(self, axis, b):
        dim = self.keep.ndim - 1
        if axis.name == "dp":
            dim = self.left.index(b)
            self.left.remove(b)
        self.keep, send = self.order.split(axis, b, self.keep, self.received, dim)
        self.received = axis.swap(send, b)

    def last(self):
        return self.keep, self.received


def on_device(
    dp_size,
    mem_size,
    target,
    memory,
    target_lengths,
    source_lengths,
    cotangent,
    self_qkv,
    self_bias_,
    self_out,
    cross_query,
    cross_kv,
    cross_bias,
    cross_out,
    ffn_up,
    ffn_up_bias,
    ffn_down,
    ffn_down_bias,
    norm_gains,
    norm_biases,
):
    mem, dp = Axis("mem", mem_size, 0), Axis("dp", dp_size, 1)
    target, memory, cotangent = target[0], memory[0], cotangent[0]
    tlen, slen = target_lengths[0], source_lengths[0]
    length, width = target.shape
    share = memory.shape[0]
    sources = share * mem_size
    head = width // HEADS
    wide = width // mem_size
    hidden = ffn_up.shape[1]
    count = length // mem_size
    rows = width // dp_size
    idx = jnp.stack([mem.index, dp.index]).astype(jnp.int32)
    vecs = jnp.concatenate(
        [self_bias_, cross_bias, norm_gains, norm_biases, ffn_down_bias.reshape(1, width),
         ffn_up_bias.reshape(-1, width), jnp.zeros((7, width), bf16)]
    ).astype(f32)

    far_pieces = gather_pieces(mem, memory, mem.bits[1:])

    weights_held = [pltpu.VMEM((3, width, max(wide, LANES)), bf16)]
    order = Order(idx)
    q, k, v, kt, ot, lse, *mixed = order.call(
        functools.partial(self_forward_kernel, (mem_size, head)),
        [(tlen, "s"), (target, "h"), (self_qkv, "r"), (self_bias_, "w")],
        [((length, wide), bf16, "h")] * 3
        + [((wide, length), bf16, "h"), ((wide, length), f32, "h"), ((8, length), f32, "h")]
        + [((count, wide), bf16, "v")] * mem_size,
        [pltpu.VMEM((length, wide), bf16)] + weights_held + [pltpu.SemaphoreType.DMA((3,))],
        us=5,
    )
    *far_pieces, mixed[0] = lax.optimization_barrier((*far_pieces, mixed[0]))
    near_pieces = [mem.swap(piece, 1) for piece in far_pieces]
    memory_pieces = [piece for pair in zip(far_pieces, near_pieces) for piece in pair]
    mixed = [mem.swap(piece, b) if b else piece for b, piece in enumerate(mixed)]

    memory_all, mk, mv, mkt, mvt = order.call(
        memory_kernel,
        [(memory, "w")] + [(x, "v") for x in memory_pieces[1:]] + [(cross_kv, "w")],
        [((sources, width), bf16, "w")] * 3 + [((width, sources), bf16, "w")] * 2,
        us=2.5,
    )

    up_rows, down_rows = (hidden // width + 1) * rows, hidden // dp_size
    (layer_own, up_keep, up_send, down_keep, down_send, h0, mixed_all, cq, att, clse, gcn, vec1) = order.call(
        functools.partial(token_kernel, (mem_size, dp_size, head)),
        [(tlen, "s"), (slen, "s"), (target, "r"), (cotangent, "r"), (self_out, "w"), (vecs, "w"),
         (cross_query, "w"), (mk, "w"), (mvt, "w"), (cross_out, "w"), (ffn_up, "w"), (ffn_down, "w")]
        + [(x, "v") for x in mixed],
        [((count, width), bf16, "v")] + [((dp_size, up_rows, HALF), bf16, "v")] * 2
        + [((dp_size, down_rows, HALF), bf16, "v")] * 2
        + [((count, width), f32, "w"), ((count, width), bf16, "w"), ((count, width), bf16, "w"),
           ((width, count), f32, "w"), ((8, count), f32, "w"),
           ((count, width), f32, "w"), ((16, width), f32, "w")],
        [pltpu.VMEM((count, width), bf16), pltpu.VMEM((count, width), bf16), pltpu.VMEM((sources, count), f32),
         pltpu.VMEM((count, hidden), bf16), pltpu.VMEM((count, hidden), f32), pltpu.VMEM((count, hidden), bf16),
         pltpu.VMEM((count, width), bf16), pltpu.VMEM((count, width), bf16), pltpu.VMEM((count, width), bf16), pltpu.SemaphoreType.DMA((2,))],
        us=14,
        vmem=20,
    )
    dims = (2,) * len(dp.bits)
    shaped = lambda x: x.reshape(dims + x.shape[1:])
    up = Chain(order, shaped(up_keep), shaped(mem.swap(up_send, 1)), dp.bits)
    down = Chain(order, shaped(down_keep), shaped(mem.swap(down_send, 1)), dp.bits)

    gk, gv, gcq, gsb, gsn, vec2, *gsm = order.call(
        functools.partial(cross_backward_kernel, (mem_size, head)),
        [(tlen, "s"), (slen, "s"), (gcn, "w"), (cross_out, "w"), (cq, "w"), (clse, "w"), (att, "w"),
         (mk, "w"), (mv, "w"), (mkt, "w"), (cross_query, "w"), (vecs, "w"), (h0, "w"), (self_out, "w")],
        [((sources, width), bf16, "w")] * 2 + [((count, width), bf16, "w")] * 2
        + [((count, width), f32, "w"), ((16, width), f32, "w")] + [((count, wide), bf16, "v")] * mem_size,
        [pltpu.VMEM((sources, count), f32), pltpu.VMEM((width, count), f32)],
        us=9,
    )
    gsm = [mem.swap(piece, b) if b else piece for b, piece in enumerate(gsm)]

    up.step(dp, dp.bits[0])
    down.step(dp, dp.bits[1])
    middle_rows = 4 * rows + vec1.shape[0] + vec2.shape[0]
    joint_rows = dp_size * middle_rows + mem_size // 2 * 2 * share
    middle_keep, middle_send = order.call(
        functools.partial(middle_kernel, (mem_size, dp_size)),
        [(x, "w") for x in (gk, gv, memory_all, cross_kv, h0, vecs, gcq, mixed_all, gsb, vec1, vec2)],
        [((joint_rows, HALF), bf16, "v")] * 2,
        us=5,
    )
    middle_send, gsm[1] = lax.optimization_barrier((middle_send, gsm[1]))
    middle_keep, memory_keep, middle_send = order.call(
        functools.partial(middle_columns_kernel, 1, middle_rows),
        [(middle_keep, "v"), (mem.swap(middle_send, 1), "v")],
        [((dp_size, middle_rows, LANES), bf16, "v"), ((mem_size // 4, share, width), bf16, "v"),
         ((joint_rows, LANES), bf16, "v")],
    )
    middle_received = mem.swap(middle_send, mem.bits[1])

    qkv_keep, qkv_send, target_keep, target_send = order.call(
        functools.partial(self_backward_kernel, (mem_size, dp_size, head)),
        [(tlen, "s"), (q, "h"), (k, "h"), (v, "h"), (ot, "h"), (lse, "h"), (kt, "h"), (target, "h"),
         (self_qkv, "r"), (gsn, "w")] + [(x, "v") for x in gsm],
        [((dp_size // 2, rows + 16, 3 * wide), bf16, "v")] * 2 + [((mem_size // 2, count, width), bf16, "v")] * 2,
        [pltpu.VMEM((length, wide), bf16), pltpu.VMEM((length, 3 * wide), bf16), pltpu.VMEM((length, wide), f32),
         pltpu.VMEM((length, wide), f32), pltpu.VMEM((wide, length), f32),
         pltpu.VMEM((dp_size, rows + 16, 3 * wide), bf16)] + weights_held
        + [pltpu.SemaphoreType.DMA((3,))],
        us=6,
    )
    half_dims = dims[1:] + qkv_keep.shape[1:]
    qkv = Chain(order, qkv_keep.reshape(half_dims), dp.swap(qkv_send, 1).reshape(half_dims), dp.bits[1:])

    blocks = mem_size // 2
    last = len(dp.bits) - 1
    middle = None
    for n in range(1, len(dp.bits)):
        up.step(dp, dp.bits[n])
        if n < last:
            down.step(dp, dp.bits[n + 1])
        if n == 1:
            grad = order.call(
                functools.partial(join_kernel, blocks),
                [(target_keep, "v"), (mem.swap(target_send, 1), "v"), (layer_own, "v")],
                [((blocks + 1, count, width), bf16, "v")],
            )[0]
            grad_far = mem.swap(grad, mem.bits[1])
        if middle is None:
            keep, send, memory_grad = order.call(
                functools.partial(middle_rows_kernel, 0),
                [(middle_keep.reshape(dp_size // 2, 2, middle_rows, LANES), "v"), (memory_keep, "v"), (middle_received, "v")],
                [((dp_size // 2, middle_rows, LANES), bf16, "v")] * 2
                + [((mem_size // 4 * share, width), f32 if mem_size == 4 else bf16, "h")],
            )
            shape = dims[1:] + (middle_rows, LANES)
            middle = Chain(order, keep.reshape(shape), dp.swap(send, 1).reshape(shape), dp.bits[1:])
        else:
            middle.step(dp, dp.bits[n - 1])
        qkv.step(dp, dp.bits[n])
    for b in mem.bits[2:]:
        parts = memory_grad.reshape(-1, 2, share, width)
        keep, send = (lax.dynamic_index_in_dim(parts, x, 1, keepdims=False) for x in (mem.bit(b), 1 - mem.bit(b)))
        memory_grad = keep.astype(f32) + mem.swap(send, b).astype(f32)
        if b != mem.bits[-1]:
            memory_grad = memory_grad.astype(bf16)
    memory_grad = memory_grad.reshape(share, width)
    down.step(dp, dp.bits[0])
    masks = [0]
    for b in mem.bits[1:]:
        masks = masks + [mask + b for mask in masks]
        grad = order.call(
            functools.partial(join_kernel, blocks),
            [(grad, "v"), (grad_far, "v")],
            [((blocks + len(masks), count, width), bf16, "v")],
        )[0]
        if b != mem.bits[-1]:
            grad_far = mem.swap(grad, 2 * b)
    middle.step(dp, dp.bits[last])
    qkv_pieces = gather_pieces(mem, order.total([qkv.last()]), mem.bits)
    ffn = order.total([up.last(), down.last()])
    ffn_far = mem.swap(ffn, mem.bits[1])
    target_grad, layer_output = order.call(
        functools.partial(rows_out_kernel, masks),
        [(grad, "v"), (mem.swap(grad, 1), "v")],
        [((length, width), f32, "r"), ((length, width), bf16, "r")],
        [pltpu.VMEM((mem_size, count, width), f32), pltpu.SemaphoreType.DMA((2 * mem_size,))],
    )
    mid = order.total([middle.last()])
    for b in mem.bits[2:]:
        mid = order.total([(mid, mem.swap(mid, b))])
    middle_pieces = gather_pieces(mem, mid, mem.bits[:2])
    for b in mem.bits[1:]:
        ffn = order.total([(ffn, ffn_far)])
        if b != mem.bits[-1]:
            ffn_far = mem.swap(ffn, 2 * b)
    qkv_grad, qkv_sums = order.call(
        qkv_out_kernel,
        [(x, "v") for x in qkv_pieces],
        [((rows, 3 * width), f32, "h"), ((8, 3 * width), f32, "v")],
    )
    up_grad, down_grad, co_grad = order.call(
        ffn_out_kernel,
        [(ffn, "v"), (mem.swap(ffn, 1), "v")],
        [((rows, hidden), f32, "h"), ((down_rows, width), f32, "h"), ((rows, width), f32, "h")],
    )
    cq_grad, so_grad, kv_grad, cb_grad, ub_grad, db_grad, gain_grad, shift_grad, sb_grad = order.call(
        functools.partial(middle_out_kernel, hidden // width),
        [(qkv_sums, "v")] + [(x, "v") for x in middle_pieces],
        [((rows, width), f32, "h")] * 2 + [((rows, 2 * width), f32, "h"), ((3, rows), f32, "v"),
         ((1, hidden // dp_size), f32, "v"), ((1, rows), f32, "v")] + [((3, rows), f32, "v")] * 3,
        [pltpu.VMEM((32, width), f32)],
    )
    return (
        layer_output[None],
        target_grad[None],
        memory_grad[None],
        qkv_grad,
        sb_grad,
        so_grad,
        cq_grad,
        kv_grad,
        cb_grad,
        co_grad,
        up_grad,
        ub_grad.reshape(-1),
        down_grad,
        db_grad.reshape(-1),
        gain_grad,
        shift_grad,
    )


def solution(mesh):
    row, whole = P("dp", None, None), P()
    in_specs = (row, P("dp", "mem", None), P("dp", None), P("dp", None), row) + (whole,) * 13
    out_specs = (
        row,
        row,
        P("dp", "mem", None),
        P("dp", None),
        P(None, "dp"),
        P("dp", None),
        P("dp", None),
        P("dp", None),
        P(None, "dp"),
        P("dp", None),
        P("dp", None),
        P("dp"),
        P("dp", None),
        P("dp"),
        P(None, "dp"),
        P(None, "dp"),
    )
    body = functools.partial(on_device, mesh.shape["dp"], mesh.shape["mem"])
    return jax.shard_map(body, mesh=mesh, in_specs=in_specs, out_specs=out_specs, check_vma=False)
```

```python
import functools

import jax
import jax.numpy as jnp
from jax import lax
from jax.experimental import pallas as pl
from jax.experimental.pallas import tpu as pltpu
from jax.sharding import PartitionSpec as P

HEADS = 8
SEG_MOST = 512
LANES = 128
HALF = 256
very_negative = -1e30
epsilon = 1e-05
SELF_BIAS, CROSS_BIAS, GAINS, SHIFTS, DOWN_BIAS, UP_BIAS = 0, 3, 6, 9, 12, 13
f32 = jnp.float32
bf16 = jnp.bfloat16


def mm(left, right):
    return jnp.dot(left, right, preferred_element_type=f32)


def mm_tn(left, right):
    return lax.dot_general(left, right, (((0,), (0,)), ((), ())), preferred_element_type=f32)


def mm_nt(left, right):
    return lax.dot_general(left, right, (((1,), (1,)), ((), ())), preferred_element_type=f32)


def norm_parts(hidden):
    center = hidden - jnp.mean(hidden, axis=-1, keepdims=True)
    scaled = lax.rsqrt(jnp.mean(center * center, axis=-1, keepdims=True) + epsilon)
    return center * scaled, scaled


def norm_backward(upstream, normed, scaled, gain_row):
    gained = upstream * gain_row
    gained_mean = jnp.mean(gained, axis=-1, keepdims=True)
    mean_cross = jnp.mean(gained * normed, axis=-1, keepdims=True)
    return scaled * (gained - gained_mean - normed * mean_cross)


def sums(matrix):
    return jnp.sum(matrix.astype(f32), axis=0, keepdims=True)


def started(lengths, places, ends, amounts):
    total = jnp.zeros(places.shape, jnp.int32)
    edge = jnp.int32(0)
    for j in range(lengths.shape[0]):
        if ends:
            edge = edge + lengths[j]
        total = total + jnp.where(places >= edge, amounts[j], 0)
        if not ends:
            edge = edge + lengths[j]
    return total


def head_lanes(value, h, head):
    if value.shape[-1] == head:
        return value
    lanes = lax.broadcasted_iota(jnp.int32, value.shape, 1)
    return jnp.where(lanes // head == h, value, jnp.zeros_like(value))


def self_bias(tlen_ref, begin, first, count):
    queries = begin + lax.broadcasted_iota(jnp.int32, (1, count), 1)
    start = started(tlen_ref, queries, True, tlen_ref)
    keys = first + lax.broadcasted_iota(jnp.int32, (begin + count - first, count), 0)
    return jnp.where((keys >= start) & (keys <= queries), 0.0, very_negative)


def self_forward_kernel(
    sizes, idx, tlen, target, qkv, shifts, q_out, k_out, v_out, kt_out, ot_out, lse_out, *rest
):
    mem, head = sizes
    pieces, (mixed, held, sem) = rest[:mem], rest[mem:]
    length = target.shape[0]
    wide = q_out.shape[1]
    share = length // mem
    weights = own_weights(idx, qkv, held, sem, wide)
    zero = jnp.zeros((1, wide), f32)
    block = lane_block(idx[0], wide)
    shift = [own_lanes(shifts.value()[i : i + 1, block].astype(f32), idx[0], wide) for i in (0, 1)]
    shift = jnp.concatenate([shift[0], zero, shift[1]], axis=1)
    for at in range(0, length, HALF):
        rows = slice(at, at + HALF)
        part = (mm(target[rows, :], weights) + shift).astype(bf16)
        q_out[rows, :] = part[:, :wide]
        k_out[rows, :] = part[:, wide : 2 * wide]
        v_out[rows, :] = part[:, 2 * wide :]
        kt_out[:, rows] = part[:, wide : 2 * wide].T
        mixed[rows, :] = part[:, 2 * wide :]
    for out in (q_out, k_out, v_out, kt_out):
        out.send()
    vt = mixed[...].T
    lse_out[...] = jnp.zeros(lse_out.shape, f32)
    for at in range(0, length, HALF):
        first = max(0, at - SEG_MOST)
        keys, cols = slice(first, at + HALF), slice(at, at + HALF)
        bias = self_bias(tlen, at, first, HALF)
        q = q_out[cols, :] * jnp.asarray(head**-0.5, bf16)
        for h in range(wide // head):
            scores = mm_nt(k_out[keys, :], head_lanes(q, h, head)) + bias
            top = jnp.max(scores, axis=0, keepdims=True)
            terms = jnp.exp(scores - top)
            total = jnp.sum(terms, axis=0, keepdims=True)
            part = mm(vt[h * head : (h + 1) * head, keys], terms.astype(bf16)) / total
            ot_out[h * head : (h + 1) * head, cols] = part
            lse_out[h : h + 1, cols] = top + jnp.log(total)
        mixed[cols, :] = ot_out[:, cols].T.astype(bf16)
    for b in range(mem):
        at = pl.multiple_of((idx[0] ^ b) * share, share)
        pieces[b][...] = mixed[pl.ds(at, share), :]


def memory_kernel(idx, *refs):
    pieces, (weights, all_out, k_out, v_out, kt_out, vt_out) = refs[:-6], refs[-6:]
    share, width = pieces[0].shape
    for b, piece in enumerate(pieces):
        at = pl.multiple_of((idx[0] ^ b) * share, share)
        all_out[pl.ds(at, share), :] = piece[...]
        both = mm(piece[...], weights[...]).astype(bf16)
        k_out[pl.ds(at, share), :] = both[:, :width]
        v_out[pl.ds(at, share), :] = both[:, width:]
        kt_out[:, pl.ds(at, share)] = both[:, :width].T
        vt_out[:, pl.ds(at, share)] = both[:, width:].T


def cross_bias_of(idx, tlen, slen, count, keys):
    queries = idx[0] * count + lax.broadcasted_iota(jnp.int32, (1, count), 1)
    low = started(tlen, queries, True, slen)
    high = started(tlen, queries, False, slen)
    places = lax.broadcasted_iota(jnp.int32, (keys, count), 0)
    return jnp.where((places >= low) & (places < high), 0.0, very_negative)


def column_of(row, count):
    return jnp.broadcast_to(row, (count, row.shape[1])).T


def token_kernel(
    sizes, idx, tlen, slen, target, cotangent, wo, vecs, cq, keys, vt, co, up, down, *rest,
):
    mem, dp, head = sizes
    pieces = rest[:mem]
    (lo_out, up_keep, up_send, down_keep, down_send, h0_out, mixed_out, q_out, att_out, lse_out, gcn_out,
     vec_out, x, ct, bias, act, fac, gi, gfo_s, acl_s, gcb_s, sem) = rest[mem:]
    count, width = lo_out.shape
    wide = width // mem
    hidden = up.shape[1]
    share = pl.ds(pl.multiple_of(idx[0] * count, count), count)
    copies = [
        pltpu.make_async_copy(target.at[share, :], x, sem.at[0]),
        pltpu.make_async_copy(cotangent.at[share, :], ct, sem.at[1]),
    ]
    for copy in copies:
        copy.start()
    bias[...] = cross_bias_of(idx, tlen, slen, count, keys.shape[0])
    row = lambda i: vecs[i : i + 1, :]
    copies[0].wait()
    h0 = x[...].astype(f32) + row(SELF_BIAS + 2)
    for b in range(mem):
        at = pl.multiple_of((idx[0] ^ b) * wide, wide)
        h0 = h0 + mm(pieces[b][...], wo.value()[pl.ds(at, wide), :])
        mixed_out[:, b * wide : (b + 1) * wide] = pieces[b][...]
    h0_out[...] = h0
    mixed_out.send()
    h0_out.send()
    normed0, _ = norm_parts(h0)
    after_self = normed0 * row(GAINS) + row(SHIFTS)
    q = (mm(after_self.astype(bf16), cq[...]) + row(CROSS_BIAS)).astype(bf16)
    q_out[...] = q
    q_out.send()
    q = q * jnp.asarray(head**-0.5, bf16)
    for h in range(HEADS):
        pair = slice(h * head // LANES * LANES, h * head // LANES * LANES + LANES)
        scores = mm_nt(keys[:, pair], head_lanes(q[:, pair], h % (LANES // head), head)) + bias[...]
        top = jnp.max(scores, axis=0, keepdims=True)
        terms = jnp.exp(scores - top)
        total = jnp.sum(terms, axis=0, keepdims=True)
        own = slice(h * head, (h + 1) * head)
        att_out[own, :] = mm(vt[own, :], terms.astype(bf16)) / total
        lse_out[h : h + 1, :] = top + jnp.log(total)
    cmt = (att_out[...] + column_of(row(CROSS_BIAS + 1), count)).astype(bf16)
    for out in (att_out, lse_out):
        out.send()
    normed1, scaled1 = norm_parts(after_self + mm_tn(cmt, co[...]) + row(CROSS_BIAS + 2))
    after_cross = normed1 * row(GAINS + 1) + row(SHIFTS + 1)
    acl = after_cross.astype(bf16)
    acl_s[...] = acl
    step = width
    h2 = after_cross + row(DOWN_BIAS)
    for i, at in enumerate(range(0, hidden, step)):
        cols = slice(at, at + step)
        inner = mm(acl, up[:, cols]) + row(UP_BIAS + i)
        sig = jax.nn.sigmoid(inner)
        part = (inner * sig).astype(bf16)
        act[:, cols] = part
        fac[:, cols] = sig * (1.0 + inner * (1.0 - sig))
        h2 = h2 + mm(part, down[cols, :])
    normed2, scaled2 = norm_parts(h2)
    lo_out[...] = (normed2 * row(GAINS + 2) + row(SHIFTS + 2)).astype(bf16)
    copies[1].wait()
    cot = ct[...].astype(f32)
    gf = norm_backward(cot, normed2, scaled2, row(GAINS + 2))
    gfo = gf.astype(bf16)
    gfo_s[...] = gfo
    u1 = gf
    vec_out[...] = jnp.zeros(vec_out.shape, f32)
    for i, at in enumerate(range(0, hidden, step)):
        cols = slice(at, at + step)
        part = (mm_nt(gfo, down[cols, :]) * fac[:, cols]).astype(bf16)
        gi[:, cols] = part
        u1 = u1 + mm_nt(part, up[:, cols])
        vec_out[5 + i : 6 + i, :] = sums(part)
    gcn = norm_backward(u1, normed1, scaled1, row(GAINS + 1))
    gcn_out[...] = gcn
    gcb_s[...] = gcn.astype(bf16)
    for i, part in enumerate((u1 * normed1, u1, cot * normed2, cot, gfo)):
        vec_out[i : i + 1, :] = sums(part)
    gcn_out.send()
    vec_out.send()
    rows, hrows = width // dp, hidden // dp
    some = width // hrows
    for up_out, down_out, side in ((up_send, down_send, 1 - idx[0] % 2), (up_keep, down_keep, idx[0] % 2)):
        start = side * HALF
        cols = pl.ds(pl.multiple_of(start, HALF), HALF)
        for i in range(hidden // width):
            part = mm_tn(act[:, i * width : (i + 1) * width], gfo_s[:, cols]).astype(bf16)
            down_out[i * some : (i + 1) * some] = part.reshape(some, hrows, HALF)
        part = mm(cmt, gcb_s[:, cols]).astype(bf16)
        last = hidden // width * rows
        up_out[:, last : last + rows, :] = part.reshape(dp, rows, HALF)
        for i in range(hidden // width):
            cols = pl.ds(pl.multiple_of(start + i * width, HALF), HALF)
            part = mm_tn(acl_s[...], gi[:, cols]).astype(bf16)
            up_out[:, i * rows : (i + 1) * rows, :] = part.reshape(dp, rows, HALF)


def cross_backward_kernel(
    sizes, idx, tlen, slen, gcn, co, q_ref, lse, att, keys, values, kt, cq, vecs, h0, wo,
    gk_out, gv_out, gcq_out, gsb_out, gsn_out, vec_out, *rest,
):
    mem, head = sizes
    pieces, (bias, gcqt) = rest[:mem], rest[mem:]
    count, width = gcn.shape
    wide = width // mem
    bias[...] = cross_bias_of(idx, tlen, slen, count, keys.shape[0])
    gcb = gcn[...].astype(bf16)
    gcm = mm_nt(gcb, co[...]).astype(bf16)
    gcmt = mm_nt(co[...], gcb).astype(bf16)
    scale = head**-0.5
    q = q_ref[...] * jnp.asarray(scale, bf16)
    for p in range(width // LANES):
        pair = slice(p * LANES, (p + 1) * LANES)
        gk = gv = 0.0
        for i in range(LANES // head):
            h = p * (LANES // head) + i
            own = slice(h * head, (h + 1) * head)
            delta = jnp.sum(gcmt[own, :].astype(f32) * att[own, :], axis=0, keepdims=True)
            qh, gh = head_lanes(q[:, pair], i, head), head_lanes(gcm[:, pair], i, head)
            probs = jnp.exp(mm_nt(keys[:, pair], qh) + bias[...] - lse[h : h + 1, :])
            ds = (probs * (mm_nt(values[:, pair], gh) - delta)).astype(bf16)
            gv = gv + mm(probs.astype(bf16), gh)
            gk = gk + mm(ds, qh)
            gcqt[own, :] = mm(kt[own, :], ds) * scale
        gk_out[:, pair] = gk.astype(bf16)
        gv_out[:, pair] = gv.astype(bf16)
    gk_out.send()
    gv_out.send()
    gcq = gcqt[...].T.astype(bf16)
    gcq_out[...] = gcq
    gcq_out.send()
    u0 = gcn[...] + mm_nt(gcq, cq[...])
    normed0, scaled0 = norm_parts(h0[...])
    gsn = norm_backward(u0, normed0, scaled0, vecs[GAINS : GAINS + 1, :])
    gsn_out[...] = gsn
    gsb = gsn.astype(bf16)
    gsb_out[...] = gsb
    for b in range(mem):
        at = pl.multiple_of((idx[0] ^ b) * wide, wide)
        pieces[b][...] = mm_nt(gsb, wo.value()[pl.ds(at, wide), :]).astype(bf16)
    vec_out[...] = jnp.zeros(vec_out.shape, f32)
    for i, part in enumerate((gsb, gcq, gcm, gcb, u0 * normed0, u0)):
        vec_out[i : i + 1, :] = sums(part)


def middle_kernel(
    sizes, idx, gk, gv, memory, wkv, h0, vecs, gcq, mixed, gsb, vec1, vec2,
    keep_out, send_out,
):
    mem, dp = sizes
    width = gsb.shape[1]
    wide, share = width // mem, memory.shape[0] // mem
    rows = width // dp
    place = keep_out.shape[0] - mem // 2 * 2 * share
    for out, side in ((send_out, 1 - idx[0] % 2), (keep_out, idx[0] % 2)):
        for i in range(mem // 2):
            at = pl.ds(pl.multiple_of((2 * i + side) * share, share), share)
            part = mm_nt(gk.value()[at, :], wkv[:, :width]) + mm_nt(gv.value()[at, :], wkv[:, width:])
            for k in range(2):
                rest = place + (2 * i + k) * share
                out[rest : rest + share, :] = part[:, k * HALF : (k + 1) * HALF].astype(bf16)
    normed0, _ = norm_parts(h0[...])
    asl = (normed0 * vecs[GAINS : GAINS + 1, :] + vecs[SHIFTS : SHIFTS + 1, :]).astype(bf16)
    vec = jnp.concatenate([vec1[...], vec2[...]], axis=0).astype(bf16)
    some, per = wide // rows, 4 * rows + vec.shape[0]
    for out, side in ((send_out, 1 - idx[0] % 2), (keep_out, idx[0] % 2)):
        cols = pl.ds(pl.multiple_of(side * HALF, HALF), HALF)

        def put(at, matrix):
            for d in range(dp):
                first = d * per + at * rows
                out[first : first + rows, :] = matrix[d * rows : (d + 1) * rows].astype(bf16)

        put(0, mm_tn(asl, gcq.value()[:, cols]))
        part = mm_tn(mixed[...], gsb.value()[:, cols]).astype(bf16)
        for b in range(mem):
            j = idx[0] ^ b
            for i in range(some):
                first = pl.multiple_of((j * some + i) * per + rows, 16)
                out[pl.ds(first, rows), :] = part[b * wide + i * rows : b * wide + (i + 1) * rows]
        put(2, mm_tn(memory[...], gk.value()[:, cols]))
        put(3, mm_tn(memory[...], gv.value()[:, cols]))
        vrows = vec.shape[0]
        half = jnp.where(side == 0, vec[:, :HALF], vec[:, HALF:])
        for d in range(dp):
            out[(d + 1) * per - vrows : (d + 1) * per, :] = half


def self_backward_kernel(
    sizes, idx, tlen, q_ref, k_ref, v_ref, ot, lse, kt, target, qkv, gsn, *rest
):
    mem, dp, head = sizes
    pieces = rest[:mem]
    qkv_keep, qkv_send, keep_out, send_out, go, gproj, gk, gv, gqt, qkv_out, held, sem = rest[mem:]
    length, wide = q_ref.shape
    share, width = gsn.shape
    copies = own_weights_copies(idx, qkv, held, sem, wide)
    for b in range(mem):
        at = pl.multiple_of((idx[0] ^ b) * share, share)
        go[pl.ds(at, share), :] = pieces[b][...]
    gk[...] = jnp.zeros_like(gk)
    gv[...] = jnp.zeros_like(gv)
    scale = head**-0.5
    for at in range(0, length, HALF):
        first = max(0, at - SEG_MOST)
        keys, cols = slice(first, at + HALF), slice(at, at + HALF)
        bias = self_bias(tlen, at, first, HALF)
        q = q_ref[cols, :] * jnp.asarray(scale, bf16)
        grad = go[cols, :]
        product = grad.astype(f32).T * ot[:, cols]
        for h in range(wide // head):
            own = slice(h * head, (h + 1) * head)
            delta = jnp.sum(product[own, :], axis=0, keepdims=True)
            qh, gh = head_lanes(q, h, head), head_lanes(grad, h, head)
            probs = jnp.exp(mm_nt(k_ref[keys, :], qh) + bias - lse[h : h + 1, cols])
            ds = (probs * (mm_nt(v_ref[keys, :], gh) - delta)).astype(bf16)
            gv[keys, :] += mm(probs.astype(bf16), gh)
            gk[keys, :] += mm(ds, qh)
            gqt[own, cols] = mm(kt[own, keys], ds) * scale
    gproj[:, :wide] = gqt[...].T.astype(bf16)
    gproj[:, wide : 2 * wide] = gk[...].astype(bf16)
    gproj[:, 2 * wide :] = gv[...].astype(bf16)
    rows = width // dp
    qkv_out[:, :rows, :] = mm_tn(target[...], gproj[...]).astype(bf16).reshape(dp, rows, 3 * wide)
    total = sums(gproj[...]).astype(bf16)
    pad = qkv_out.shape[1] - rows
    qkv_out[:, rows:, :] = jnp.broadcast_to(total[None], (dp, pad, 3 * wide))
    for out, side in ((qkv_send, 1 - idx[1] % 2), (qkv_keep, idx[1] % 2)):
        for i in range(dp // 2):
            out[i] = qkv_out[2 * i + side]
    weights = own_weights_value(idx, copies, held, wide)
    for out, side in ((send_out, 1 - idx[0] % 2), (keep_out, idx[0] % 2)):
        for i in range(mem // 2):
            at = pl.multiple_of((2 * i + side) * share, share)
            out[i] = mm_nt(gproj[pl.ds(at, share), :], weights).astype(bf16)
    at = pl.multiple_of(idx[0] * share, share)
    part = mm_nt(gproj[pl.ds(at, share), :], weights) + gsn[...]
    keep_out[idx[0] // 2] = part.astype(bf16)


def own_weights_copies(idx, qkv, held, sem, wide):
    width, full = qkv.shape[0], qkv.shape[1] // 3
    lanes = max(wide, LANES)
    copies = []
    for c in range(3):
        at = pl.multiple_of(c * full + idx[0] * wide // LANES * LANES, LANES)
        copies.append(pltpu.make_async_copy(qkv.at[:, pl.ds(at, lanes)], held.at[c], sem.at[c]))
        copies[-1].start()
    return copies


def own_weights_value(idx, copies, held, wide):
    for copy in copies:
        copy.wait()
    return jnp.concatenate([own_lanes(held[c], idx[0], wide) for c in range(3)], axis=1)


def own_weights(idx, qkv, held, sem, wide):
    return own_weights_value(idx, own_weights_copies(idx, qkv, held, sem, wide), held, wide)


def split_kernel(axis_at, bit_at, dim, idx, keep, received, keep_out, send_out):
    bit = (idx[axis_at] >> bit_at) & 1
    if dim == keep.ndim - 1:
        total = keep[...].astype(f32) + received[...].astype(f32)
        middle = keep.shape[-1] // 2
        low, high = total[..., :middle], total[..., middle:]
        keep_out[...] = jnp.where(bit == 0, low, high).astype(bf16)
        send_out[...] = jnp.where(bit == 0, high, low).astype(bf16)
        return
    lead = (slice(None),) * dim
    for out, which in ((send_out, 1 - bit), (keep_out, bit)):
        out[...] = (keep[lead + (which,)].astype(f32) + received[lead + (which,)].astype(f32)).astype(bf16)


def add_kernel(idx, *refs):
    out, pairs, at = refs[-1], refs[:-1], 0
    for keep, received in zip(pairs[::2], pairs[1::2]):
        part = keep[...].astype(f32) + received[...].astype(f32)
        out[at : at + part.shape[0]] = part.astype(out.dtype)
        at += part.shape[0]


def join_kernel(parts, idx, keep, received, *refs):
    more, out = refs[:-1], refs[-1]
    for i in range(parts):
        out[i] = (keep[i].astype(f32) + received[i].astype(f32)).astype(bf16)
    at = parts
    for ref in more or (keep, received):
        if more:
            out[at] = ref[...]
            at += 1
            continue
        for i in range(parts, ref.shape[0]):
            out[at] = ref[i]
            at += 1


def rows_out_kernel(masks, idx, own, other, target_out, layer_out, held, sem):
    share = own.shape[1]
    copies = []
    blocks = own.shape[0] - len(masks)

    def send(source, out, at):
        at = pl.ds(pl.multiple_of(at * share, share), share)
        copies.append(pltpu.make_async_copy(source, out.at[at, :], sem.at[len(copies)]))
        copies[-1].start()

    for ref, flip in ((own, 0), (other, 1)):
        for i, mask in enumerate(masks):
            send(ref.at[blocks + i], layer_out, idx[0] ^ (mask + flip))
    for i in range(blocks):
        for k, ref in enumerate((own, other)):
            held[2 * i + k] = ref[i].astype(f32)
            send(held.at[2 * i + k], target_out, 2 * i + (idx[0] + k) % 2)
    for copy in copies:
        copy.wait()


def ffn_out_kernel(idx, own, other, up_out, down_out, co_out):
    rows, width = co_out.shape
    blocks = up_out.shape[1] // width
    for piece, side in ((own, idx[0] % 2), (other, 1 - idx[0] % 2)):
        for i in range(blocks):
            at = pl.multiple_of(i * width + side * HALF, HALF)
            up_out.held[:, pl.ds(at, HALF)] = piece[i * rows : (i + 1) * rows, :].astype(f32)
        cols = pl.ds(pl.multiple_of(side * HALF, HALF), HALF)
        co_out.held[:, cols] = piece[blocks * rows : (blocks + 1) * rows, :].astype(f32)
        down_out.held[:, cols] = piece[(blocks + 1) * rows :, :].astype(f32)


def lanes_from(ref, first, count, at, wide):
    if wide % LANES == 0:
        return ref[pl.ds(first, count), pl.ds(pl.multiple_of(at, LANES), wide)]
    block = ref[pl.ds(first, count), pl.ds(pl.multiple_of(at // LANES * LANES, LANES), LANES)]
    result = block[:, :wide]
    for k in range(1, LANES // wide):
        result = jnp.where(at % LANES == k * wide, block[:, k * wide : (k + 1) * wide], result)
    return result


def middle_out_kernel(count, idx, qkv_sums, *refs):
    pieces = refs[:-10]
    cq_out, so_out, kv_out, cb_out, ub_out, db_out, gain_out, shift_out, sb_out, vec = refs[-10:]
    rows, width = cq_out.shape
    for b, piece in enumerate(pieces):
        other = idx[0] ^ b
        at = other % 2 * HALF + other // 2 % 2 * LANES
        cols = pl.ds(pl.multiple_of(at, LANES), LANES)
        for i, out in enumerate((cq_out, so_out)):
            out.held[:, cols] = piece[i * rows : (i + 1) * rows, :].astype(f32)
        for i in range(2):
            part = piece[(2 + i) * rows : (3 + i) * rows, :].astype(f32)
            kv_out.held[:, pl.ds(pl.multiple_of(i * width + at, LANES), LANES)] = part
        vec[:, cols] = piece[4 * rows :, :].astype(f32)
    here = idx[1] * rows
    take = lambda first, count: lanes_from(vec, first, count, here, rows)
    cb_out[...] = take(17, 3)
    db_out[...] = take(4, 1)
    for out, places in ((gain_out, (20, 0, 2)), (shift_out, (21, 1, 3))):
        for i, first in enumerate(places):
            out[i : i + 1, :] = take(first, 1)
    per = ub_out.shape[1]
    first = idx[1] * per
    part = lanes_from(vec, 5, 1, first % width, per)
    for i in range(1, count):
        part = jnp.where(first // width == i, lanes_from(vec, 5 + i, 1, first % width, per), part)
    ub_out[...] = part
    for i, (ref, at) in enumerate(((qkv_sums, 0), (qkv_sums, 2 * width), (vec, 0))):
        sb_out[i : i + 1, :] = lanes_from(ref, 16 if ref is vec else 0, 1, at + here, rows)


def qkv_out_kernel(idx, *refs):
    pieces, (qkv_out, full) = refs[:-2], refs[-2:]
    rows, width = qkv_out.shape[0], qkv_out.shape[1] // 3
    wide = pieces[0].shape[1] // 3

    def put(out, first, count):
        for c in range(3):
            lanes = slice(c * wide, (c + 1) * wide)
            parts = [piece[first : first + count, lanes].astype(f32) for piece in pieces]
            if wide < LANES:
                odd = idx[0] % 2
                parts = [
                    jnp.where(odd == 0, jnp.concatenate([a, b], 1), jnp.concatenate([b, a], 1))
                    for a, b in zip(parts[::2], parts[1::2])
                ]
            for b, part in enumerate(parts):
                j = idx[0] ^ b if wide >= LANES else (idx[0] // 2) ^ b
                at = pl.multiple_of(c * width + j * max(wide, LANES), LANES)
                out[:count, pl.ds(at, max(wide, LANES))] = part

    put(qkv_out.held, 0, rows)
    put(full, rows, full.shape[0])


def middle_columns_kernel(bit_at, count, idx, keep, received, keep_out, memory_out, send_out):
    bit = (idx[0] >> bit_at) & 1
    per = keep_out.shape[1]
    for d in range(keep_out.shape[0]):
        at = slice(d * per, (d + 1) * per)
        total = keep[at, :].astype(f32) + received[at, :].astype(f32)
        low, high = total[:, :LANES], total[:, LANES:]
        keep_out[d] = jnp.where(bit == 0, low, high).astype(bf16)
        send_out[at, :] = jnp.where(bit == 0, high, low).astype(bf16)
    place = keep_out.shape[0] * per
    share = memory_out.shape[1]
    for i in range(memory_out.shape[0]):
        for k in range(2):
            for which in (0, 1):
                side = bit if which else 1 - bit
                at = pl.ds(pl.multiple_of(place + ((2 * i + side) * 2 + k) * share, 16), share)
                total = (keep[at, :].astype(f32) + received[at, :].astype(f32)).astype(bf16)
                if which:
                    memory_out[i, :, k * HALF : (k + 1) * HALF] = total
                    continue
                for n in range(HALF // LANES):
                    rest = place + ((i * 2 + k) * 2 + n) * share
                    send_out[rest : rest + share, :] = total[:, n * LANES : (n + 1) * LANES]


def middle_rows_kernel(bit_at, idx, keep, memory, received, keep_out, send_out, memory_out):
    bit = (idx[1] >> bit_at) & 1
    per = keep.shape[2]
    for out, side in ((send_out, 1 - bit), (keep_out, bit)):
        for i in range(keep.shape[0]):
            at = pl.ds(pl.multiple_of((2 * i + side) * per, 16), per)
            out[i] = (keep[i, side].astype(f32) + received[at, :].astype(f32)).astype(bf16)
    place = keep.shape[0] * 2 * per
    share = memory.shape[1]
    for i in range(memory.shape[0]):
        for k in range(memory.shape[2] // LANES):
            cols = slice(k * LANES, (k + 1) * LANES)
            rest = place + (i * (memory.shape[2] // LANES) + k) * share
            total = memory[i, :, cols].astype(f32) + received[rest : rest + share, :].astype(f32)
            memory_out[i * share : (i + 1) * share, cols] = total.astype(memory_out.dtype)


class Staged:
    def __init__(self, source, held, sem):
        self.held, self.shape, self.dtype = held, held.shape, held.dtype
        self.copy = pltpu.make_async_copy(source, held, sem)
        self.copy.start()
        self.waited = False

    def wait(self):
        if not self.waited:
            self.copy.wait()
            self.waited = True

    def __getitem__(self, at):
        self.wait()
        return self.held[at]

    def value(self):
        self.wait()
        return self.held


class Result:
    def __init__(self, place, held, sem):
        self.held, self.shape, self.dtype = held, held.shape, held.dtype
        self.copy, self.sent = pltpu.make_async_copy(held, place, sem), False

    def __getitem__(self, at):
        return self.held[at]

    def __setitem__(self, at, value):
        self.held[at] = value

    def send(self):
        if not self.sent:
            self.copy.start()
            self.sent = True


class Plain:
    def __init__(self, ref):
        self.held, self.shape, self.dtype = ref, ref.shape, ref.dtype

    def __getitem__(self, at):
        return self.held[at]

    def __setitem__(self, at, value):
        self.held[at] = value

    def value(self):
        return self.held

    def send(self):
        pass


def call(kernel, ins, outs, scratch=(), vmem=16, us=1.0):
    ins = [(pltpu.with_memory_space_constraint(x, pltpu.HBM) if mode in "hr" else x, mode) for x, mode in ins]
    spaces = {"s": pltpu.SMEM, "v": pltpu.VMEM, "w": pltpu.VMEM, "h": pltpu.HBM, "r": pltpu.HBM}
    held = [(x.shape, x.dtype) for x, mode in ins if mode == "h"]
    held += [(shape, dtype) for shape, dtype, mode in outs if mode == "h"]
    modes = [mode for _, mode in ins] + [mode for _, _, mode in outs]

    def body(*refs):
        count = len(modes)
        own = refs[count + len(held) : len(refs) - 1 if held else len(refs)]
        spare, sems = iter(refs[count : count + len(held)]), refs[-1]
        given, place = [], 0
        for i, mode in enumerate(modes):
            ref = refs[i]
            if mode == "h":
                ref = (Staged if i < len(ins) else Result)(ref, next(spare), sems.at[place])
                place += 1
            if mode == "w":
                ref = Plain(ref)
            given.append(ref)
        kernel(*given, *own)
        for ref in given:
            if isinstance(ref, Staged):
                ref.wait()
            if isinstance(ref, Result):
                ref.send()
        for ref in given:
            if isinstance(ref, Result):
                ref.copy.wait()

    held_scratch = [pltpu.VMEM(shape, dtype) for shape, dtype in held]
    sems = [pltpu.SemaphoreType.DMA((len(held),))] if held else []
    return pl.pallas_call(
        body,
        out_shape=[
            (pltpu.HBM if mode in "hr" else jax.ShapeDtypeStruct)(shape, dtype) for shape, dtype, mode in outs
        ],
        in_specs=[pl.BlockSpec(memory_space=spaces[mode]) for _, mode in ins],
        out_specs=[pl.BlockSpec(memory_space=spaces[mode]) for _, _, mode in outs],
        scratch_shapes=held_scratch + list(scratch) + sems,
        compiler_params=pltpu.CompilerParams(vmem_limit_bytes=vmem * 1024 * 1024),
        cost_estimate=pl.CostEstimate(
            flops=int(us * 1.1e9), bytes_accessed=int(us * 1e6), transcendentals=0
        ),
    )(*[x for x, _ in ins])


def own_lanes(block, which, wide):
    if wide % LANES == 0:
        return block
    return jnp.where(which % 2 == 0, block[:, :wide], block[:, wide : 2 * wide])


def lane_block(which, wide):
    return pl.ds(pl.multiple_of(which * wide // LANES * LANES, LANES), max(wide, LANES))


class Axis:
    def __init__(self, name, size, place):
        self.name, self.size, self.place = name, size, place
        self.index = lax.axis_index(name)
        self.bits = [1 << k for k in range(size.bit_length() - 1)]

    def bit(self, b):
        return (self.index // b) % 2

    def swap(self, value, b):
        return lax.ppermute(value, self.name, [(i, i ^ b) for i in range(self.size)])


def gather_pieces(axis, value, bits):
    pieces = {0: value}
    for b in reversed(bits):
        for k in sorted(pieces):
            pieces[k ^ b] = axis.swap(pieces[k], b)
    return [pieces[k] for k in sorted(pieces)]


class Order:
    def __init__(self, idx):
        self.idx, self.before, self.now = idx, [], []

    def call(self, kernel, ins, outs, scratch=(), vmem=16, us=2.0, alone=True):
        if alone:
            self.next()
        idx = lax.optimization_barrier((self.idx, *self.before))[0] if self.before else self.idx
        results = call(kernel, [(idx, "s")] + ins, outs, scratch, vmem, us)
        self.now.append(results[0])
        return results

    def next(self):
        if self.now:
            self.before, self.now = self.now, []

    def split(self, axis, b, keep, received, dim):
        shape = list(keep.shape)
        if dim == keep.ndim - 1:
            shape[dim] //= 2
        else:
            del shape[dim]
        kernel = functools.partial(split_kernel, axis.place, b.bit_length() - 1, dim)
        return self.call(kernel, [(keep, "v"), (received, "v")], [(shape, bf16, "v")] * 2, alone=False)

    def total(self, pairs, dtype=bf16, mode="v"):
        shape = (sum(keep.shape[0] for keep, _ in pairs),) + pairs[0][0].shape[1:]
        return self.call(add_kernel, [(x, "v") for pair in pairs for x in pair], [(shape, dtype, mode)], alone=False)[0]


class Chain:
    def __init__(self, order, keep, received, bits):
        self.order, self.keep, self.received = order, keep, received
        self.left = list(reversed(bits))

    def step(self, axis, b):
        dim = self.keep.ndim - 1
        if axis.name == "dp":
            dim = self.left.index(b)
            self.left.remove(b)
        self.keep, send = self.order.split(axis, b, self.keep, self.received, dim)
        self.received = axis.swap(send, b)

    def last(self):
        return self.keep, self.received


def on_device(
    dp_size,
    mem_size,
    target,
    memory,
    target_lengths,
    source_lengths,
    cotangent,
    self_qkv,
    self_bias_,
    self_out,
    cross_query,
    cross_kv,
    cross_bias,
    cross_out,
    ffn_up,
    ffn_up_bias,
    ffn_down,
    ffn_down_bias,
    norm_gains,
    norm_biases,
):
    mem, dp = Axis("mem", mem_size, 0), Axis("dp", dp_size, 1)
    target, memory, cotangent = target[0], memory[0], cotangent[0]
    tlen, slen = target_lengths[0], source_lengths[0]
    length, width = target.shape
    share = memory.shape[0]
    sources = share * mem_size
    head = width // HEADS
    wide = width // mem_size
    hidden = ffn_up.shape[1]
    count = length // mem_size
    rows = width // dp_size
    idx = jnp.stack([mem.index, dp.index]).astype(jnp.int32)
    vecs = jnp.concatenate(
        [self_bias_, cross_bias, norm_gains, norm_biases, ffn_down_bias.reshape(1, width),
         ffn_up_bias.reshape(-1, width), jnp.zeros((7, width), bf16)]
    ).astype(f32)

    far_pieces = gather_pieces(mem, memory, mem.bits[1:])

    weights_held = [pltpu.VMEM((3, width, max(wide, LANES)), bf16)]
    order = Order(idx)
    q, k, v, kt, ot, lse, *mixed = order.call(
        functools.partial(self_forward_kernel, (mem_size, head)),
        [(tlen, "s"), (target, "h"), (self_qkv, "r"), (self_bias_, "w")],
        [((length, wide), bf16, "h")] * 3
        + [((wide, length), bf16, "h"), ((wide, length), f32, "h"), ((8, length), f32, "h")]
        + [((count, wide), bf16, "v")] * mem_size,
        [pltpu.VMEM((length, wide), bf16)] + weights_held + [pltpu.SemaphoreType.DMA((3,))],
        us=5,
    )
    *far_pieces, mixed[0] = lax.optimization_barrier((*far_pieces, mixed[0]))
    near_pieces = [mem.swap(piece, 1) for piece in far_pieces]
    memory_pieces = [piece for pair in zip(far_pieces, near_pieces) for piece in pair]
    mixed = [mem.swap(piece, b) if b else piece for b, piece in enumerate(mixed)]

    memory_all, mk, mv, mkt, mvt = order.call(
        memory_kernel,
        [(memory, "w")] + [(x, "v") for x in memory_pieces[1:]] + [(cross_kv, "w")],
        [((sources, width), bf16, "w")] * 3 + [((width, sources), bf16, "w")] * 2,
        us=2.5,
    )

    up_rows, down_rows = (hidden // width + 1) * rows, hidden // dp_size
    (layer_own, up_keep, up_send, down_keep, down_send, h0, mixed_all, cq, att, clse, gcn, vec1) = order.call(
        functools.partial(token_kernel, (mem_size, dp_size, head)),
        [(tlen, "s"), (slen, "s"), (target, "r"), (cotangent, "r"), (self_out, "w"), (vecs, "w"),
         (cross_query, "w"), (mk, "w"), (mvt, "w"), (cross_out, "w"), (ffn_up, "w"), (ffn_down, "w")]
        + [(x, "v") for x in mixed],
        [((count, width), bf16, "v")] + [((dp_size, up_rows, HALF), bf16, "v")] * 2
        + [((dp_size, down_rows, HALF), bf16, "v")] * 2
        + [((count, width), f32, "w"), ((count, width), bf16, "w"), ((count, width), bf16, "w"),
           ((width, count), f32, "w"), ((8, count), f32, "w"),
           ((count, width), f32, "w"), ((16, width), f32, "w")],
        [pltpu.VMEM((count, width), bf16), pltpu.VMEM((count, width), bf16), pltpu.VMEM((sources, count), f32),
         pltpu.VMEM((count, hidden), bf16), pltpu.VMEM((count, hidden), f32), pltpu.VMEM((count, hidden), bf16),
         pltpu.VMEM((count, width), bf16), pltpu.VMEM((count, width), bf16), pltpu.VMEM((count, width), bf16), pltpu.SemaphoreType.DMA((2,))],
        us=14,
        vmem=20,
    )
    dims = (2,) * len(dp.bits)
    shaped = lambda x: x.reshape(dims + x.shape[1:])
    up = Chain(order, shaped(up_keep), shaped(mem.swap(up_send, 1)), dp.bits)
    down = Chain(order, shaped(down_keep), shaped(mem.swap(down_send, 1)), dp.bits)

    gk, gv, gcq, gsb, gsn, vec2, *gsm = order.call(
        functools.partial(cross_backward_kernel, (mem_size, head)),
        [(tlen, "s"), (slen, "s"), (gcn, "w"), (cross_out, "w"), (cq, "w"), (clse, "w"), (att, "w"),
         (mk, "w"), (mv, "w"), (mkt, "w"), (cross_query, "w"), (vecs, "w"), (h0, "w"), (self_out, "w")],
        [((sources, width), bf16, "w")] * 2 + [((count, width), bf16, "w")] * 2
        + [((count, width), f32, "w"), ((16, width), f32, "w")] + [((count, wide), bf16, "v")] * mem_size,
        [pltpu.VMEM((sources, count), f32), pltpu.VMEM((width, count), f32)],
        us=9,
    )
    gsm = [mem.swap(piece, b) if b else piece for b, piece in enumerate(gsm)]

    up.step(dp, dp.bits[0])
    down.step(dp, dp.bits[1])
    middle_rows = 4 * rows + vec1.shape[0] + vec2.shape[0]
    joint_rows = dp_size * middle_rows + mem_size // 2 * 2 * share
    middle_keep, middle_send = order.call(
        functools.partial(middle_kernel, (mem_size, dp_size)),
        [(x, "w") for x in (gk, gv, memory_all, cross_kv, h0, vecs, gcq, mixed_all, gsb, vec1, vec2)],
        [((joint_rows, HALF), bf16, "v")] * 2,
        us=5,
    )
    middle_send, gsm[1] = lax.optimization_barrier((middle_send, gsm[1]))
    middle_keep, memory_keep, middle_send = order.call(
        functools.partial(middle_columns_kernel, 1, middle_rows),
        [(middle_keep, "v"), (mem.swap(middle_send, 1), "v")],
        [((dp_size, middle_rows, LANES), bf16, "v"), ((mem_size // 4, share, width), bf16, "v"),
         ((joint_rows, LANES), bf16, "v")],
    )
    middle_received = mem.swap(middle_send, mem.bits[1])

    qkv_keep, qkv_send, target_keep, target_send = order.call(
        functools.partial(self_backward_kernel, (mem_size, dp_size, head)),
        [(tlen, "s"), (q, "h"), (k, "h"), (v, "h"), (ot, "h"), (lse, "h"), (kt, "h"), (target, "h"),
         (self_qkv, "r"), (gsn, "w")] + [(x, "v") for x in gsm],
        [((dp_size // 2, rows + 16, 3 * wide), bf16, "v")] * 2 + [((mem_size // 2, count, width), bf16, "v")] * 2,
        [pltpu.VMEM((length, wide), bf16), pltpu.VMEM((length, 3 * wide), bf16), pltpu.VMEM((length, wide), f32),
         pltpu.VMEM((length, wide), f32), pltpu.VMEM((wide, length), f32),
         pltpu.VMEM((dp_size, rows + 16, 3 * wide), bf16)] + weights_held
        + [pltpu.SemaphoreType.DMA((3,))],
        us=6,
    )
    half_dims = dims[1:] + qkv_keep.shape[1:]
    qkv = Chain(order, qkv_keep.reshape(half_dims), dp.swap(qkv_send, 1).reshape(half_dims), dp.bits[1:])

    blocks = mem_size // 2
    last = len(dp.bits) - 1
    free = functools.partial(order.call, alone=False)
    order.next()
    grad = free(
        functools.partial(join_kernel, blocks),
        [(target_keep, "v"), (mem.swap(target_send, 1), "v"), (layer_own, "v")],
        [((blocks + 1, count, width), bf16, "v")],
    )[0]
    grad_far = mem.swap(grad, mem.bits[1])
    middle = None
    for n in range(1, len(dp.bits)):
        up.step(dp, dp.bits[n])
        if n < last:
            down.step(dp, dp.bits[n + 1])
        else:
            down.step(dp, dp.bits[0])
        if middle is None:
            keep, send, memory_grad = free(
                functools.partial(middle_rows_kernel, 0),
                [(middle_keep.reshape(dp_size // 2, 2, middle_rows, LANES), "v"), (memory_keep, "v"), (middle_received, "v")],
                [((dp_size // 2, middle_rows, LANES), bf16, "v")] * 2
                + [((mem_size // 4 * share, width), f32 if mem_size == 4 else bf16, "h")],
            )
            shape = dims[1:] + (middle_rows, LANES)
            middle = Chain(order, keep.reshape(shape), dp.swap(send, 1).reshape(shape), dp.bits[1:])
        else:
            middle.step(dp, dp.bits[n - 1])
        qkv.step(dp, dp.bits[n])
        order.next()
    for b in mem.bits[2:]:
        parts = memory_grad.reshape(-1, 2, share, width)
        keep, send = (lax.dynamic_index_in_dim(parts, x, 1, keepdims=False) for x in (mem.bit(b), 1 - mem.bit(b)))
        memory_grad = keep.astype(f32) + mem.swap(send, b).astype(f32)
        if b != mem.bits[-1]:
            memory_grad = memory_grad.astype(bf16)
    memory_grad = memory_grad.reshape(share, width)
    qkv_pieces = gather_pieces(mem, order.total([qkv.last()]), mem.bits)
    middle.step(dp, dp.bits[last])
    ffn = order.total([up.last(), down.last()])
    ffn_far = mem.swap(ffn, mem.bits[1])
    masks = [0]
    for b in mem.bits[1:]:
        masks = masks + [mask + b for mask in masks]
        grad = free(
            functools.partial(join_kernel, blocks),
            [(grad, "v"), (grad_far, "v")],
            [((blocks + len(masks), count, width), bf16, "v")],
        )[0]
        if b != mem.bits[-1]:
            grad_far = mem.swap(grad, 2 * b)
    order.next()
    mid = order.total([middle.last()])
    for b in mem.bits[2:]:
        mid = order.total([(mid, mem.swap(mid, b))])
    middle_pieces = gather_pieces(mem, mid, mem.bits[:2])
    for b in mem.bits[1:]:
        ffn = order.total([(ffn, ffn_far)])
        if b != mem.bits[-1]:
            ffn_far = mem.swap(ffn, 2 * b)
    target_grad, layer_output = free(
        functools.partial(rows_out_kernel, masks),
        [(grad, "v"), (mem.swap(grad, 1), "v")],
        [((length, width), f32, "r"), ((length, width), bf16, "r")],
        [pltpu.VMEM((mem_size, count, width), f32), pltpu.SemaphoreType.DMA((2 * mem_size,))],
    )
    qkv_grad, qkv_sums = free(
        qkv_out_kernel,
        [(x, "v") for x in qkv_pieces],
        [((rows, 3 * width), f32, "h"), ((8, 3 * width), f32, "v")],
    )
    order.next()
    up_grad, down_grad, co_grad = free(
        ffn_out_kernel,
        [(ffn, "v"), (mem.swap(ffn, 1), "v")],
        [((rows, hidden), f32, "h"), ((down_rows, width), f32, "h"), ((rows, width), f32, "h")],
    )
    cq_grad, so_grad, kv_grad, cb_grad, ub_grad, db_grad, gain_grad, shift_grad, sb_grad = free(
        functools.partial(middle_out_kernel, hidden // width),
        [(qkv_sums, "v")] + [(x, "v") for x in middle_pieces],
        [((rows, width), f32, "h")] * 2 + [((rows, 2 * width), f32, "h"), ((3, rows), f32, "v"),
         ((1, hidden // dp_size), f32, "v"), ((1, rows), f32, "v")] + [((3, rows), f32, "v")] * 3,
        [pltpu.VMEM((32, width), f32)],
    )
    return (
        layer_output[None],
        target_grad[None],
        memory_grad[None],
        qkv_grad,
        sb_grad,
        so_grad,
        cq_grad,
        kv_grad,
        cb_grad,
        co_grad,
        up_grad,
        ub_grad.reshape(-1),
        down_grad,
        db_grad.reshape(-1),
        gain_grad,
        shift_grad,
    )


def solution(mesh):
    row, whole = P("dp", None, None), P()
    in_specs = (row, P("dp", "mem", None), P("dp", None), P("dp", None), row) + (whole,) * 13
    out_specs = (
        row,
        row,
        P("dp", "mem", None),
        P("dp", None),
        P(None, "dp"),
        P("dp", None),
        P("dp", None),
        P("dp", None),
        P(None, "dp"),
        P("dp", None),
        P("dp", None),
        P("dp"),
        P("dp", None),
        P("dp"),
        P(None, "dp"),
        P(None, "dp"),
    )
    body = functools.partial(on_device, mesh.shape["dp"], mesh.shape["mem"])
    return jax.shard_map(body, mesh=mesh, in_specs=in_specs, out_specs=out_specs, check_vma=False)
```

```python
import functools

import jax
import jax.numpy as jnp
from jax import lax
from jax.experimental import pallas as pl
from jax.experimental.pallas import tpu as pltpu
from jax.sharding import PartitionSpec as P

HEADS = 8
SEG_MOST = 512
LANES = 128
HALF = 256
very_negative = -1e30
epsilon = 1e-05
SELF_BIAS, CROSS_BIAS, GAINS, SHIFTS, DOWN_BIAS, UP_BIAS = 0, 3, 6, 9, 12, 13
f32 = jnp.float32
bf16 = jnp.bfloat16


def mm(left, right):
    return jnp.dot(left, right, preferred_element_type=f32)


def mm_tn(left, right):
    return lax.dot_general(left, right, (((0,), (0,)), ((), ())), preferred_element_type=f32)


def mm_nt(left, right):
    return lax.dot_general(left, right, (((1,), (1,)), ((), ())), preferred_element_type=f32)


def norm_parts(hidden):
    center = hidden - jnp.mean(hidden, axis=-1, keepdims=True)
    scaled = lax.rsqrt(jnp.mean(center * center, axis=-1, keepdims=True) + epsilon)
    return center * scaled, scaled


def norm_backward(upstream, normed, scaled, gain_row):
    gained = upstream * gain_row
    gained_mean = jnp.mean(gained, axis=-1, keepdims=True)
    mean_cross = jnp.mean(gained * normed, axis=-1, keepdims=True)
    return scaled * (gained - gained_mean - normed * mean_cross)


def sums(matrix):
    return jnp.sum(matrix.astype(f32), axis=0, keepdims=True)


def started(lengths, places, ends, amounts):
    total = jnp.zeros(places.shape, jnp.int32)
    edge = jnp.int32(0)
    for j in range(lengths.shape[0]):
        if ends:
            edge = edge + lengths[j]
        total = total + jnp.where(places >= edge, amounts[j], 0)
        if not ends:
            edge = edge + lengths[j]
    return total


def head_lanes(value, h, head):
    if value.shape[-1] == head:
        return value
    lanes = lax.broadcasted_iota(jnp.int32, value.shape, 1)
    return jnp.where(lanes // head == h, value, jnp.zeros_like(value))


def self_bias(tlen_ref, begin, first, count):
    queries = begin + lax.broadcasted_iota(jnp.int32, (1, count), 1)
    start = started(tlen_ref, queries, True, tlen_ref)
    keys = first + lax.broadcasted_iota(jnp.int32, (begin + count - first, count), 0)
    return jnp.where((keys >= start) & (keys <= queries), 0.0, very_negative)


def self_forward_kernel(
    sizes, idx, tlen, target, qkv, shifts, q_out, k_out, v_out, kt_out, ot_out, lse_out, *rest
):
    mem, head = sizes
    pieces, (mixed, held, sem, lengths, lengths_sem) = rest[:mem], rest[mem:]
    known = pltpu.make_async_copy(tlen, lengths, lengths_sem)
    known.start()
    tlen = lengths
    length = target.shape[0]
    wide = q_out.shape[1]
    share = length // mem
    weights = own_weights(idx, qkv, held, sem, wide)
    zero = jnp.zeros((1, wide), f32)
    block = lane_block(idx[0], wide)
    shift = [own_lanes(shifts.value()[i : i + 1, block].astype(f32), idx[0], wide) for i in (0, 1)]
    shift = jnp.concatenate([shift[0], zero, shift[1]], axis=1)
    for at in range(0, length, HALF):
        rows = slice(at, at + HALF)
        part = (mm(target[rows, :], weights) + shift).astype(bf16)
        q_out[rows, :] = part[:, :wide]
        k_out[rows, :] = part[:, wide : 2 * wide]
        v_out[rows, :] = part[:, 2 * wide :]
        kt_out[:, rows] = part[:, wide : 2 * wide].T
        mixed[rows, :] = part[:, 2 * wide :]
    for out in (q_out, k_out, v_out, kt_out):
        out.send()
    known.wait()
    vt = mixed[...].T
    lse_out[...] = jnp.zeros(lse_out.shape, f32)
    work = [(at, h) for at in range(0, length, HALF) for h in range(wide // head)]

    def score(at, h):
        first = max(0, at - SEG_MOST)
        q = q_out[at : at + HALF, :] * jnp.asarray(head**-0.5, bf16)
        return mm_nt(k_out[first : at + HALF, :], head_lanes(q, h, head)) + self_bias(tlen, at, first, HALF)

    later = score(*work[0])
    for n, (at, h) in enumerate(work):
        scores, later = later, score(*work[n + 1]) if n + 1 < len(work) else None
        keys, cols = slice(max(0, at - SEG_MOST), at + HALF), slice(at, at + HALF)
        own = slice(h * head, (h + 1) * head)
        top = jnp.max(scores, axis=0, keepdims=True)
        terms = jnp.exp(scores - top)
        total = jnp.sum(terms, axis=0, keepdims=True)
        ot_out[own, cols] = mm(vt[own, keys], terms.astype(bf16)) / total
        lse_out[h : h + 1, cols] = top + jnp.log(total)
        if h == wide // head - 1:
            mixed[cols, :] = ot_out[:, cols].T.astype(bf16)
    for b in range(mem):
        at = pl.multiple_of((idx[0] ^ b) * share, share)
        pieces[b][...] = mixed[pl.ds(at, share), :]


def memory_kernel(idx, *refs):
    pieces, (weights, all_out, k_out, v_out, kt_out, vt_out) = refs[:-6], refs[-6:]
    share, width = pieces[0].shape
    for b, piece in enumerate(pieces):
        at = pl.multiple_of((idx[0] ^ b) * share, share)
        all_out[pl.ds(at, share), :] = piece[...]
        both = mm(piece[...], weights[...]).astype(bf16)
        k_out[pl.ds(at, share), :] = both[:, :width]
        v_out[pl.ds(at, share), :] = both[:, width:]
        kt_out[:, pl.ds(at, share)] = both[:, :width].T
        vt_out[:, pl.ds(at, share)] = both[:, width:].T


def cross_bias_of(idx, tlen, slen, count, keys):
    queries = idx[0] * count + lax.broadcasted_iota(jnp.int32, (1, count), 1)
    low = started(tlen, queries, True, slen)
    high = started(tlen, queries, False, slen)
    places = lax.broadcasted_iota(jnp.int32, (keys, count), 0)
    return jnp.where((places >= low) & (places < high), 0.0, very_negative)


def column_of(row, count):
    return jnp.broadcast_to(row, (count, row.shape[1])).T


def token_kernel(
    sizes, idx, tlen, slen, target, cotangent, wo, vecs, cq, keys, vt, co, up, down, *rest,
):
    mem, dp, head = sizes
    pieces, far, near, rest = rest[:mem], rest[mem : mem + 7], rest[mem + 19 : mem + 26], rest[mem + 7 :]
    rest = rest[:12] + rest[19:]
    (lo_out, up_keep, up_send, down_keep, down_send, h0_out, mixed_out, q_out, att_out, lse_out, gcn_out,
     vec_out, x, ct, bias, act, fac, gi, gfo_s, acl_s, gcb_s, sem, far_sem) = rest
    brought = [pltpu.make_async_copy(x, y, far_sem.at[i]) for i, (x, y) in enumerate(zip(far, near))]
    count, width = lo_out.shape
    wide = width // mem
    hidden = up.shape[1]
    share = pl.ds(pl.multiple_of(idx[0] * count, count), count)
    copies = [
        pltpu.make_async_copy(target.at[share, :], x, sem.at[0]),
        pltpu.make_async_copy(cotangent.at[share, :], ct, sem.at[1]),
    ]
    for copy in copies + brought:
        copy.start()
    bias[...] = cross_bias_of(idx, tlen, slen, count, keys.shape[0])
    row = lambda i: vecs[i : i + 1, :]
    h0 = row(SELF_BIAS + 2)
    for b in range(mem):
        at = pl.multiple_of((idx[0] ^ b) * wide, wide)
        h0 = h0 + mm(pieces[b][...], wo.value()[pl.ds(at, wide), :])
        mixed_out[:, b * wide : (b + 1) * wide] = pieces[b][...]
    copies[0].wait()
    h0 = h0 + x[...].astype(f32)
    h0_out[...] = h0
    mixed_out.send()
    h0_out.send()
    normed0, _ = norm_parts(h0)
    after_self = normed0 * row(GAINS) + row(SHIFTS)
    q = (mm(after_self.astype(bf16), cq[...]) + row(CROSS_BIAS)).astype(bf16)
    q_out[...] = q
    q_out.send()
    q = q * jnp.asarray(head**-0.5, bf16)

    def score(h):
        pair = slice(h * head // LANES * LANES, h * head // LANES * LANES + LANES)
        return mm_nt(keys[:, pair], head_lanes(q[:, pair], h % (LANES // head), head)) + bias[...]

    later = score(0)
    for h in range(HEADS):
        scores, later = later, score(h + 1) if h + 1 < HEADS else None
        top = jnp.max(scores, axis=0, keepdims=True)
        terms = jnp.exp(scores - top)
        total = jnp.sum(terms, axis=0, keepdims=True)
        own = slice(h * head, (h + 1) * head)
        att_out[own, :] = mm(vt[own, :], terms.astype(bf16)) / total
        lse_out[h : h + 1, :] = top + jnp.log(total)
    cmt = (att_out[...] + column_of(row(CROSS_BIAS + 1), count)).astype(bf16)
    for out in (att_out, lse_out):
        out.send()
    normed1, scaled1 = norm_parts(after_self + mm_tn(cmt, co[...]) + row(CROSS_BIAS + 2))
    after_cross = normed1 * row(GAINS + 1) + row(SHIFTS + 1)
    acl = after_cross.astype(bf16)
    acl_s[...] = acl
    step = width
    h2 = after_cross + row(DOWN_BIAS)
    chunks = [slice(at, at + step) for at in range(0, hidden, step)]
    later = mm(acl, up[:, chunks[0]])
    for i, cols in enumerate(chunks):
        inner = later + row(UP_BIAS + i)
        later = mm(acl, up[:, chunks[i + 1]]) if i + 1 < len(chunks) else None
        sig = jax.nn.sigmoid(inner)
        part = (inner * sig).astype(bf16)
        act[:, cols] = part
        fac[:, cols] = sig * (1.0 + inner * (1.0 - sig))
        h2 = h2 + mm(part, down[cols, :])
    normed2, scaled2 = norm_parts(h2)
    lo_out[...] = (normed2 * row(GAINS + 2) + row(SHIFTS + 2)).astype(bf16)
    copies[1].wait()
    cot = ct[...].astype(f32)
    gf = norm_backward(cot, normed2, scaled2, row(GAINS + 2))
    gfo = gf.astype(bf16)
    gfo_s[...] = gfo
    u1 = gf
    vec_out[...] = jnp.zeros(vec_out.shape, f32)
    later = mm_nt(gfo, down[chunks[0], :])
    for i, cols in enumerate(chunks):
        part = (later * fac[:, cols]).astype(bf16)
        later = mm_nt(gfo, down[chunks[i + 1], :]) if i + 1 < len(chunks) else None
        gi[:, cols] = part
        u1 = u1 + mm_nt(part, up[:, cols])
        vec_out[5 + i : 6 + i, :] = sums(part)
    rows, hrows = width // dp, hidden // dp
    some = width // hrows
    sides = ((up_send, down_send, 1 - idx[0] % 2), (up_keep, down_keep, idx[0] % 2))
    own_cols = lambda side, at: pl.ds(pl.multiple_of(side * HALF + at, HALF), HALF)
    for i in range(hidden // width):
        actt = act[:, i * width : (i + 1) * width].T
        for _, down_out, side in sides:
            part = mm(actt, gfo_s[:, own_cols(side, 0)]).astype(bf16)
            down_out[i * some : (i + 1) * some] = part.reshape(some, hrows, HALF)
    gcn = norm_backward(u1, normed1, scaled1, row(GAINS + 1))
    gcn_out[...] = gcn
    gcb_s[...] = gcn.astype(bf16)
    aclt = acl_s[...].T
    for i in range(hidden // width):
        for up_out, _, side in sides:
            part = mm(aclt, gi[:, own_cols(side, i * width)]).astype(bf16)
            up_out[:, i * rows : (i + 1) * rows, :] = part.reshape(dp, rows, HALF)
    for i, part in enumerate((u1 * normed1, u1, cot * normed2, cot, gfo)):
        vec_out[i : i + 1, :] = sums(part)
    last = hidden // width * rows
    for up_out, _, side in sides:
        part = mm(cmt, gcb_s[:, own_cols(side, 0)]).astype(bf16)
        up_out[:, last : last + rows, :] = part.reshape(dp, rows, HALF)
    for copy in brought:
        copy.wait()


def cross_backward_kernel(
    sizes, idx, tlen, slen, gcn, co, q_ref, lse, att, keys, values, kt, cq, vecs, h0, wo,
    gk_out, gv_out, gcq_out, gsb_out, gsn_out, vec_out, *rest,
):
    mem, head = sizes
    pieces, (bias, gcqt) = rest[:mem], rest[mem:]
    count, width = gcn.shape
    wide = width // mem
    bias[...] = cross_bias_of(idx, tlen, slen, count, keys.shape[0])
    gcb = gcn[...].astype(bf16)
    gcm = mm_nt(gcb, co[...]).astype(bf16)
    gcmt = mm_nt(co[...], gcb).astype(bf16)
    scale = head**-0.5
    q = q_ref[...] * jnp.asarray(scale, bf16)
    per = LANES // head

    def products(h):
        pair = slice(h // per * LANES, (h // per + 1) * LANES)
        qh, gh = head_lanes(q[:, pair], h % per, head), head_lanes(gcm[:, pair], h % per, head)
        scores = mm_nt(keys[:, pair], qh) + bias[...] - lse[h : h + 1, :]
        return qh, gh, scores, mm_nt(values[:, pair], gh)

    later = products(0)
    for h in range(width // head):
        (qh, gh, scores, grads), later = later, products(h + 1) if h + 1 < width // head else None
        pair, own = slice(h // per * LANES, (h // per + 1) * LANES), slice(h * head, (h + 1) * head)
        delta = jnp.sum(gcmt[own, :].astype(f32) * att[own, :], axis=0, keepdims=True)
        probs = jnp.exp(scores)
        ds = (probs * (grads - delta)).astype(bf16)
        gv_part, gk_part = mm(probs.astype(bf16), gh), mm(ds, qh)
        gcqt[own, :] = mm(kt[own, :], ds) * scale
        gv, gk = (gv_part, gk_part) if h % per == 0 else (gv + gv_part, gk + gk_part)
        if h % per == per - 1:
            gk_out[:, pair] = gk.astype(bf16)
            gv_out[:, pair] = gv.astype(bf16)
    gk_out.send()
    gv_out.send()
    gcq = gcqt[...].T.astype(bf16)
    gcq_out[...] = gcq
    gcq_out.send()
    u0 = gcn[...] + mm_nt(gcq, cq[...])
    normed0, scaled0 = norm_parts(h0[...])
    gsn = norm_backward(u0, normed0, scaled0, vecs[GAINS : GAINS + 1, :])
    gsn_out[...] = gsn
    gsb = gsn.astype(bf16)
    gsb_out[...] = gsb
    for b in range(mem):
        at = pl.multiple_of((idx[0] ^ b) * wide, wide)
        pieces[b][...] = mm_nt(gsb, wo.value()[pl.ds(at, wide), :]).astype(bf16)
    vec_out[...] = jnp.zeros(vec_out.shape, f32)
    for i, part in enumerate((gsb, gcq, gcm, gcb, u0 * normed0, u0)):
        vec_out[i : i + 1, :] = sums(part)


def middle_kernel(
    sizes, idx, gk, gv, memory, wkv, h0, vecs, gcq, mixed, gsb, vec1, vec2, keep_out, send_out
):
    mem, dp = sizes
    width = gsb.shape[1]
    wide, share = width // mem, memory.shape[0] // mem
    rows = width // dp
    place = keep_out.shape[0] - mem // 2 * 2 * share
    for out, side in ((send_out, 1 - idx[0] % 2), (keep_out, idx[0] % 2)):
        for i in range(mem // 2):
            at = pl.ds(pl.multiple_of((2 * i + side) * share, share), share)
            part = mm_nt(gk.value()[at, :], wkv[:, :width]) + mm_nt(gv.value()[at, :], wkv[:, width:])
            for k in range(2):
                rest = place + (2 * i + k) * share
                out[rest : rest + share, :] = part[:, k * HALF : (k + 1) * HALF].astype(bf16)
    normed0, _ = norm_parts(h0[...])
    asl = (normed0 * vecs[GAINS : GAINS + 1, :] + vecs[SHIFTS : SHIFTS + 1, :]).astype(bf16)
    vec = jnp.concatenate([vec1[...], vec2[...]], axis=0).astype(bf16)
    some, per = wide // rows, 4 * rows + vec.shape[0]
    for out, side in ((send_out, 1 - idx[0] % 2), (keep_out, idx[0] % 2)):
        cols = pl.ds(pl.multiple_of(side * HALF, HALF), HALF)

        def put(at, matrix):
            for d in range(dp):
                first = d * per + at * rows
                out[first : first + rows, :] = matrix[d * rows : (d + 1) * rows].astype(bf16)

        put(0, mm_tn(asl, gcq.value()[:, cols]))
        part = mm_tn(mixed[...], gsb.value()[:, cols]).astype(bf16)
        for b in range(mem):
            j = idx[0] ^ b
            for i in range(some):
                first = pl.multiple_of((j * some + i) * per + rows, 16)
                out[pl.ds(first, rows), :] = part[b * wide + i * rows : b * wide + (i + 1) * rows]
        put(2, mm_tn(memory[...], gk.value()[:, cols]))
        put(3, mm_tn(memory[...], gv.value()[:, cols]))
        vrows = vec.shape[0]
        half = jnp.where(side == 0, vec[:, :HALF], vec[:, HALF:])
        for d in range(dp):
            out[(d + 1) * per - vrows : (d + 1) * per, :] = half


def self_backward_kernel(
    sizes, idx, tlen, q_ref, k_ref, v_ref, ot, lse, kt, target, qkv, gsn, *rest
):
    mem, dp, head = sizes
    pieces = rest[:mem]
    qkv_keep, qkv_send, keep_out, send_out, go, gproj, gk, gv, gqt, qkv_out, held, sem = rest[mem:]
    length, wide = q_ref.shape
    share, width = gsn.shape
    copies = own_weights_copies(idx, qkv, held, sem, wide)
    for b in range(mem):
        at = pl.multiple_of((idx[0] ^ b) * share, share)
        go[pl.ds(at, share), :] = pieces[b][...]
    gk[...] = jnp.zeros_like(gk)
    gv[...] = jnp.zeros_like(gv)
    scale = head**-0.5
    work = [(at, h) for at in range(0, length, HALF) for h in range(wide // head)]

    def products(at, h):
        first = max(0, at - SEG_MOST)
        keys, cols = slice(first, at + HALF), slice(at, at + HALF)
        qh = head_lanes(q_ref[cols, :] * jnp.asarray(scale, bf16), h, head)
        gh = head_lanes(go[cols, :], h, head)
        scores = mm_nt(k_ref[keys, :], qh) + self_bias(tlen, at, first, HALF) - lse[h : h + 1, cols]
        return keys, cols, qh, gh, scores, mm_nt(v_ref[keys, :], gh)

    later = products(*work[0])
    for n, (at, h) in enumerate(work):
        (keys, cols, qh, gh, scores, grads), later = later, products(*work[n + 1]) if n + 1 < len(work) else None
        own = slice(h * head, (h + 1) * head)
        if h == 0:
            product = go[cols, :].astype(f32).T * ot[:, cols]
        delta = jnp.sum(product[own, :], axis=0, keepdims=True)
        probs = jnp.exp(scores)
        ds = (probs * (grads - delta)).astype(bf16)
        gv[keys, :] += mm(probs.astype(bf16), gh)
        gk[keys, :] += mm(ds, qh)
        gqt[own, cols] = mm(kt[own, keys], ds) * scale
    gproj[:, :wide] = gqt[...].T.astype(bf16)
    gproj[:, wide : 2 * wide] = gk[...].astype(bf16)
    gproj[:, 2 * wide :] = gv[...].astype(bf16)
    rows = width // dp
    qkv_out[:, :rows, :] = mm_tn(target[...], gproj[...]).astype(bf16).reshape(dp, rows, 3 * wide)
    total = sums(gproj[...]).astype(bf16)
    pad = qkv_out.shape[1] - rows
    qkv_out[:, rows:, :] = jnp.broadcast_to(total[None], (dp, pad, 3 * wide))
    for out, side in ((qkv_send, 1 - idx[1] % 2), (qkv_keep, idx[1] % 2)):
        for i in range(dp // 2):
            out[i] = qkv_out[2 * i + side]
    weights = own_weights_value(idx, copies, held, wide)
    for out, side in ((send_out, 1 - idx[0] % 2), (keep_out, idx[0] % 2)):
        for i in range(mem // 2):
            at = pl.multiple_of((2 * i + side) * share, share)
            part = mm_nt(gproj[pl.ds(at, share), :], weights)
            if out is keep_out:
                part = part + jnp.where(idx[0] // 2 == i, 1.0, 0.0) * gsn[...]
            out[i] = part.astype(bf16)


def own_weights_copies(idx, qkv, held, sem, wide):
    width, full = qkv.shape[0], qkv.shape[1] // 3
    lanes = max(wide, LANES)
    copies = []
    for c in range(3):
        at = pl.multiple_of(c * full + idx[0] * wide // LANES * LANES, LANES)
        copies.append(pltpu.make_async_copy(qkv.at[:, pl.ds(at, lanes)], held.at[c], sem.at[c]))
        copies[-1].start()
    return copies


def own_weights_value(idx, copies, held, wide):
    for copy in copies:
        copy.wait()
    return jnp.concatenate([own_lanes(held[c], idx[0], wide) for c in range(3)], axis=1)


def own_weights(idx, qkv, held, sem, wide):
    return own_weights_value(idx, own_weights_copies(idx, qkv, held, sem, wide), held, wide)


def split_kernel(axis_at, bit_at, dim, idx, keep, received, keep_out, send_out):
    bit = (idx[axis_at] >> bit_at) & 1
    if dim == keep.ndim - 1:
        total = keep[...].astype(f32) + received[...].astype(f32)
        middle = keep.shape[-1] // 2
        low, high = total[..., :middle], total[..., middle:]
        keep_out[...] = jnp.where(bit == 0, low, high).astype(bf16)
        send_out[...] = jnp.where(bit == 0, high, low).astype(bf16)
        return
    lead = (slice(None),) * dim
    for out, which in ((send_out, 1 - bit), (keep_out, bit)):
        out[...] = (keep[lead + (which,)].astype(f32) + received[lead + (which,)].astype(f32)).astype(bf16)


def add_kernel(idx, *refs):
    out, pairs, at = refs[-1], refs[:-1], 0
    for keep, received in zip(pairs[::2], pairs[1::2]):
        part = keep[...].astype(f32) + received[...].astype(f32)
        out[at : at + part.shape[0]] = part.astype(out.dtype)
        at += part.shape[0]


def join_kernel(parts, idx, keep, received, *refs):
    more, out = refs[:-1], refs[-1]
    for i in range(parts):
        out[i] = (keep[i].astype(f32) + received[i].astype(f32)).astype(bf16)
    at = parts
    for ref in more or (keep, received):
        if more:
            out[at] = ref[...]
            at += 1
            continue
        for i in range(parts, ref.shape[0]):
            out[at] = ref[i]
            at += 1


def rows_out_kernel(masks, idx, own, other, target_out, layer_out, held, sem):
    share = own.shape[1]
    copies = []
    blocks = own.shape[0] - len(masks)

    def send(source, out, at):
        at = pl.ds(pl.multiple_of(at * share, share), share)
        copies.append(pltpu.make_async_copy(source, out.at[at, :], sem.at[len(copies)]))
        copies[-1].start()

    for ref, flip in ((own, 0), (other, 1)):
        for i, mask in enumerate(masks):
            send(ref.at[blocks + i], layer_out, idx[0] ^ (mask + flip))
    for i in range(blocks):
        for k, ref in enumerate((own, other)):
            held[2 * i + k] = ref[i].astype(f32)
            send(held.at[2 * i + k], target_out, 2 * i + (idx[0] + k) % 2)
    for copy in copies:
        copy.wait()


def ffn_out_kernel(idx, own, other, up_out, down_out, co_out):
    rows, width = co_out.shape
    blocks = up_out.shape[1] // width
    for piece, side in ((own, idx[0] % 2), (other, 1 - idx[0] % 2)):
        for i in range(blocks):
            at = pl.multiple_of(i * width + side * HALF, HALF)
            up_out.held[:, pl.ds(at, HALF)] = piece[i * rows : (i + 1) * rows, :].astype(f32)
        cols = pl.ds(pl.multiple_of(side * HALF, HALF), HALF)
        co_out.held[:, cols] = piece[blocks * rows : (blocks + 1) * rows, :].astype(f32)
        down_out.held[:, cols] = piece[(blocks + 1) * rows :, :].astype(f32)


def lanes_from(ref, first, count, at, wide):
    if wide % LANES == 0:
        return ref[pl.ds(first, count), pl.ds(pl.multiple_of(at, LANES), wide)]
    block = ref[pl.ds(first, count), pl.ds(pl.multiple_of(at // LANES * LANES, LANES), LANES)]
    result = block[:, :wide]
    for k in range(1, LANES // wide):
        result = jnp.where(at % LANES == k * wide, block[:, k * wide : (k + 1) * wide], result)
    return result


def middle_out_kernel(count, idx, qkv_sums, *refs):
    pieces = refs[:-10]
    cq_out, so_out, kv_out, cb_out, ub_out, db_out, gain_out, shift_out, sb_out, vec = refs[-10:]
    rows, width = cq_out.shape
    for b, piece in enumerate(pieces):
        other = idx[0] ^ b
        at = other % 2 * HALF + other // 2 % 2 * LANES
        cols = pl.ds(pl.multiple_of(at, LANES), LANES)
        for i, out in enumerate((cq_out, so_out)):
            out.held[:, cols] = piece[i * rows : (i + 1) * rows, :].astype(f32)
        for i in range(2):
            part = piece[(2 + i) * rows : (3 + i) * rows, :].astype(f32)
            kv_out.held[:, pl.ds(pl.multiple_of(i * width + at, LANES), LANES)] = part
        vec[:, cols] = piece[4 * rows :, :].astype(f32)
    here = idx[1] * rows
    take = lambda first, count: lanes_from(vec, first, count, here, rows)
    cb_out[...] = take(17, 3)
    db_out[...] = take(4, 1)
    for out, places in ((gain_out, (20, 0, 2)), (shift_out, (21, 1, 3))):
        for i, first in enumerate(places):
            out[i : i + 1, :] = take(first, 1)
    per = ub_out.shape[1]
    first = idx[1] * per
    part = lanes_from(vec, 5, 1, first % width, per)
    for i in range(1, count):
        part = jnp.where(first // width == i, lanes_from(vec, 5 + i, 1, first % width, per), part)
    ub_out[...] = part
    for i, (ref, at) in enumerate(((qkv_sums, 0), (qkv_sums, 2 * width), (vec, 0))):
        sb_out[i : i + 1, :] = lanes_from(ref, 16 if ref is vec else 0, 1, at + here, rows)


def qkv_out_kernel(idx, *refs):
    pieces, (qkv_out, full) = refs[:-2], refs[-2:]
    rows, width = qkv_out.shape[0], qkv_out.shape[1] // 3
    wide = pieces[0].shape[1] // 3

    def put(out, first, count):
        for c in range(3):
            lanes = slice(c * wide, (c + 1) * wide)
            parts = [piece[first : first + count, lanes].astype(f32) for piece in pieces]
            if wide < LANES:
                odd = idx[0] % 2
                parts = [
                    jnp.where(odd == 0, jnp.concatenate([a, b], 1), jnp.concatenate([b, a], 1))
                    for a, b in zip(parts[::2], parts[1::2])
                ]
            for b, part in enumerate(parts):
                j = idx[0] ^ b if wide >= LANES else (idx[0] // 2) ^ b
                at = pl.multiple_of(c * width + j * max(wide, LANES), LANES)
                out[:count, pl.ds(at, max(wide, LANES))] = part

    put(qkv_out.held, 0, rows)
    put(full, rows, full.shape[0])


def middle_columns_kernel(bit_at, count, idx, keep, received, keep_out, memory_out, send_out):
    bit = (idx[0] >> bit_at) & 1
    per = keep_out.shape[1]
    for d in range(keep_out.shape[0]):
        at = slice(d * per, (d + 1) * per)
        total = keep[at, :].astype(f32) + received[at, :].astype(f32)
        low, high = total[:, :LANES], total[:, LANES:]
        keep_out[d] = jnp.where(bit == 0, low, high).astype(bf16)
        send_out[at, :] = jnp.where(bit == 0, high, low).astype(bf16)
    place = keep_out.shape[0] * per
    share = memory_out.shape[1]
    for i in range(memory_out.shape[0]):
        for k in range(2):
            for which in (0, 1):
                side = bit if which else 1 - bit
                at = pl.ds(pl.multiple_of(place + ((2 * i + side) * 2 + k) * share, 16), share)
                total = (keep[at, :].astype(f32) + received[at, :].astype(f32)).astype(bf16)
                if which:
                    memory_out[i, :, k * HALF : (k + 1) * HALF] = total
                    continue
                for n in range(HALF // LANES):
                    rest = place + ((i * 2 + k) * 2 + n) * share
                    send_out[rest : rest + share, :] = total[:, n * LANES : (n + 1) * LANES]


def middle_rows_kernel(bit_at, idx, keep, memory, received, keep_out, send_out, memory_out):
    bit = (idx[1] >> bit_at) & 1
    per = keep.shape[2]
    for out, side in ((send_out, 1 - bit), (keep_out, bit)):
        for i in range(keep.shape[0]):
            at = pl.ds(pl.multiple_of((2 * i + side) * per, 16), per)
            out[i] = (keep[i, side].astype(f32) + received[at, :].astype(f32)).astype(bf16)
    place = keep.shape[0] * 2 * per
    share = memory.shape[1]
    for i in range(memory.shape[0]):
        for k in range(memory.shape[2] // LANES):
            cols = slice(k * LANES, (k + 1) * LANES)
            rest = place + (i * (memory.shape[2] // LANES) + k) * share
            total = memory[i, :, cols].astype(f32) + received[rest : rest + share, :].astype(f32)
            memory_out[i * share : (i + 1) * share, cols] = total.astype(memory_out.dtype)


class Staged:
    def __init__(self, source, held, sem):
        self.held, self.shape, self.dtype = held, held.shape, held.dtype
        self.copy = pltpu.make_async_copy(source, held, sem)
        self.copy.start()
        self.waited = False

    def wait(self):
        if not self.waited:
            self.copy.wait()
            self.waited = True

    def __getitem__(self, at):
        self.wait()
        return self.held[at]

    def value(self):
        self.wait()
        return self.held


class Result:
    def __init__(self, place, held, sem):
        self.held, self.shape, self.dtype = held, held.shape, held.dtype
        self.copy, self.sent = pltpu.make_async_copy(held, place, sem), False

    def __getitem__(self, at):
        return self.held[at]

    def __setitem__(self, at, value):
        self.held[at] = value

    def send(self):
        if not self.sent:
            self.copy.start()
            self.sent = True


class Plain:
    def __init__(self, ref):
        self.held, self.shape, self.dtype = ref, ref.shape, ref.dtype

    def __getitem__(self, at):
        return self.held[at]

    def __setitem__(self, at, value):
        self.held[at] = value

    def value(self):
        return self.held

    def send(self):
        pass


def call(kernel, ins, outs, scratch=(), vmem=16, us=1.0):
    ins = [(pltpu.with_memory_space_constraint(x, pltpu.HBM) if mode in "hr" else x, mode) for x, mode in ins]
    spaces = {"s": pltpu.SMEM, "v": pltpu.VMEM, "w": pltpu.VMEM, "h": pltpu.HBM, "r": pltpu.HBM}
    held = [(x.shape, x.dtype) for x, mode in ins if mode == "h"]
    held += [(shape, dtype) for shape, dtype, mode in outs if mode == "h"]
    modes = [mode for _, mode in ins] + [mode for _, _, mode in outs]

    def body(*refs):
        count = len(modes)
        own = refs[count + len(held) : len(refs) - 1 if held else len(refs)]
        spare, sems = iter(refs[count : count + len(held)]), refs[-1]
        given, place = [], 0
        for i, mode in enumerate(modes):
            ref = refs[i]
            if mode == "h":
                ref = (Staged if i < len(ins) else Result)(ref, next(spare), sems.at[place])
                place += 1
            if mode == "w":
                ref = Plain(ref)
            given.append(ref)
        kernel(*given, *own)
        for ref in given:
            if isinstance(ref, Staged):
                ref.wait()
            if isinstance(ref, Result):
                ref.send()
        for ref in given:
            if isinstance(ref, Result):
                ref.copy.wait()

    held_scratch = [pltpu.VMEM(shape, dtype) for shape, dtype in held]
    sems = [pltpu.SemaphoreType.DMA((len(held),))] if held else []
    return pl.pallas_call(
        body,
        out_shape=[
            (pltpu.HBM if mode in "hr" else jax.ShapeDtypeStruct)(shape, dtype) for shape, dtype, mode in outs
        ],
        in_specs=[pl.BlockSpec(memory_space=spaces[mode]) for _, mode in ins],
        out_specs=[pl.BlockSpec(memory_space=spaces[mode]) for _, _, mode in outs],
        scratch_shapes=held_scratch + list(scratch) + sems,
        compiler_params=pltpu.CompilerParams(vmem_limit_bytes=vmem * 1024 * 1024),
        cost_estimate=pl.CostEstimate(
            flops=int(us * 1.1e9), bytes_accessed=int(us * 1e6), transcendentals=0
        ),
    )(*[x for x, _ in ins])


def own_lanes(block, which, wide):
    if wide % LANES == 0:
        return block
    return jnp.where(which % 2 == 0, block[:, :wide], block[:, wide : 2 * wide])


def lane_block(which, wide):
    return pl.ds(pl.multiple_of(which * wide // LANES * LANES, LANES), max(wide, LANES))


class Axis:
    def __init__(self, name, size, place):
        self.name, self.size, self.place = name, size, place
        self.index = lax.axis_index(name)
        self.bits = [1 << k for k in range(size.bit_length() - 1)]

    def bit(self, b):
        return (self.index // b) % 2

    def swap(self, value, b):
        return lax.ppermute(value, self.name, [(i, i ^ b) for i in range(self.size)])


def gather_pieces(axis, value, bits):
    pieces = {0: value}
    for b in reversed(bits):
        for k in sorted(pieces):
            pieces[k ^ b] = axis.swap(pieces[k], b)
    return [pieces[k] for k in sorted(pieces)]


class Order:
    def __init__(self, idx):
        self.idx, self.before, self.now = idx, [], []

    def call(self, kernel, ins, outs, scratch=(), vmem=16, us=2.0, alone=True):
        if alone:
            self.next()
        idx = lax.optimization_barrier((self.idx, *self.before))[0] if self.before else self.idx
        results = call(kernel, [(idx, "s")] + ins, outs, scratch, vmem, us)
        self.now.append(results[0])
        return results

    def next(self):
        if self.now:
            self.before, self.now = self.now, []

    def split(self, axis, b, keep, received, dim):
        shape = list(keep.shape)
        if dim == keep.ndim - 1:
            shape[dim] //= 2
        else:
            del shape[dim]
        kernel = functools.partial(split_kernel, axis.place, b.bit_length() - 1, dim)
        return self.call(kernel, [(keep, "v"), (received, "v")], [(shape, bf16, "v")] * 2, alone=False)

    def total(self, pairs, dtype=bf16, mode="v"):
        shape = (sum(keep.shape[0] for keep, _ in pairs),) + pairs[0][0].shape[1:]
        return self.call(add_kernel, [(x, "v") for pair in pairs for x in pair], [(shape, dtype, mode)], alone=False)[0]


class Chain:
    def __init__(self, order, keep, received, bits):
        self.order, self.keep, self.received = order, keep, received
        self.left = list(reversed(bits))

    def step(self, axis, b):
        dim = self.keep.ndim - 1
        if axis.name == "dp":
            dim = self.left.index(b)
            self.left.remove(b)
        self.keep, send = self.order.split(axis, b, self.keep, self.received, dim)
        self.received = axis.swap(send, b)

    def last(self):
        return self.keep, self.received


def on_device(
    dp_size,
    mem_size,
    target,
    memory,
    target_lengths,
    source_lengths,
    cotangent,
    self_qkv,
    self_bias_,
    self_out,
    cross_query,
    cross_kv,
    cross_bias,
    cross_out,
    ffn_up,
    ffn_up_bias,
    ffn_down,
    ffn_down_bias,
    norm_gains,
    norm_biases,
):
    mem, dp = Axis("mem", mem_size, 0), Axis("dp", dp_size, 1)
    target, memory, cotangent = target[0], memory[0], cotangent[0]
    tlen, slen = target_lengths[0], source_lengths[0]
    length, width = target.shape
    share = memory.shape[0]
    sources = share * mem_size
    head = width // HEADS
    wide = width // mem_size
    hidden = ffn_up.shape[1]
    count = length // mem_size
    rows = width // dp_size
    idx = jnp.stack([mem.index, dp.index]).astype(jnp.int32)
    vecs = jnp.concatenate(
        [self_bias_, cross_bias, norm_gains, norm_biases, ffn_down_bias.reshape(1, width),
         ffn_up_bias.reshape(-1, width), jnp.zeros((7, width), bf16)]
    ).astype(f32)

    far_pieces = gather_pieces(mem, memory, mem.bits[1:])

    weights_held = [pltpu.VMEM((3, width, max(wide, LANES)), bf16)]
    order = Order(idx)
    q, k, v, kt, ot, lse, *mixed = order.call(
        functools.partial(self_forward_kernel, (mem_size, head)),
        [(tlen, "r"), (target, "h"), (self_qkv, "r"), (self_bias_, "h")],
        [((length, wide), bf16, "h")] * 3
        + [((wide, length), bf16, "h"), ((wide, length), f32, "h"), ((8, length), f32, "h")]
        + [((count, wide), bf16, "v")] * mem_size,
        [pltpu.VMEM((length, wide), bf16)] + weights_held
        + [pltpu.SemaphoreType.DMA((3,)), pltpu.SMEM(tlen.shape, tlen.dtype), pltpu.SemaphoreType.DMA],
        us=5,
    )
    *far_pieces, mixed[0] = lax.optimization_barrier((*far_pieces, mixed[0]))
    near_pieces = [mem.swap(piece, 1) for piece in far_pieces]
    memory_pieces = [piece for pair in zip(far_pieces, near_pieces) for piece in pair]
    mixed = [mem.swap(piece, b) if b else piece for b, piece in enumerate(mixed)]

    memory_all, mk, mv, mkt, mvt = order.call(
        memory_kernel,
        [(memory, "w")] + [(x, "v") for x in memory_pieces[1:]] + [(cross_kv, "w")],
        [((sources, width), bf16, "w")] * 3 + [((width, sources), bf16, "w")] * 2,
        us=2.5,
    )

    up_rows, down_rows = (hidden // width + 1) * rows, hidden // dp_size
    far = (q, k, v, ot, lse, kt, target)
    (layer_own, up_keep, up_send, down_keep, down_send, h0, mixed_all, cq, att, clse, gcn, vec1,
     q, k, v, ot, lse, kt, target_near) = order.call(
        functools.partial(token_kernel, (mem_size, dp_size, head)),
        [(tlen, "s"), (slen, "s"), (target, "r"), (cotangent, "r"), (self_out, "w"), (vecs, "w"),
         (cross_query, "w"), (mk, "w"), (mvt, "w"), (cross_out, "w"), (ffn_up, "w"), (ffn_down, "w")]
        + [(x, "v") for x in mixed] + [(x, "r") for x in far],
        [((count, width), bf16, "v")] + [((dp_size, up_rows, HALF), bf16, "v")] * 2
        + [((dp_size, down_rows, HALF), bf16, "v")] * 2
        + [((count, width), f32, "w"), ((count, width), bf16, "w"), ((count, width), bf16, "w"),
           ((width, count), f32, "w"), ((8, count), f32, "w"),
           ((count, width), f32, "w"), ((16, width), f32, "w")]
        + [(x.shape, x.dtype, "v") for x in far],
        [pltpu.VMEM((count, width), bf16), pltpu.VMEM((count, width), bf16), pltpu.VMEM((sources, count), f32),
         pltpu.VMEM((count, hidden), bf16), pltpu.VMEM((count, hidden), f32), pltpu.VMEM((count, hidden), bf16),
         pltpu.VMEM((count, width), bf16), pltpu.VMEM((count, width), bf16), pltpu.VMEM((count, width), bf16), pltpu.SemaphoreType.DMA((2,)),
         pltpu.SemaphoreType.DMA((len(far),))],
        us=14,
        vmem=20,
    )
    dims = (2,) * len(dp.bits)
    shaped = lambda x: x.reshape(dims + x.shape[1:])
    up = Chain(order, shaped(up_keep), shaped(mem.swap(up_send, 1)), dp.bits)
    down = Chain(order, shaped(down_keep), shaped(mem.swap(down_send, 1)), dp.bits)

    gk, gv, gcq, gsb, gsn, vec2, *gsm = order.call(
        functools.partial(cross_backward_kernel, (mem_size, head)),
        [(tlen, "s"), (slen, "s"), (gcn, "w"), (cross_out, "w"), (cq, "w"), (clse, "w"), (att, "w"),
         (mk, "w"), (mv, "w"), (mkt, "w"), (cross_query, "w"), (vecs, "w"), (h0, "w"), (self_out, "w")],
        [((sources, width), bf16, "w")] * 2 + [((count, width), bf16, "w")] * 2
        + [((count, width), f32, "w"), ((16, width), f32, "w")] + [((count, wide), bf16, "v")] * mem_size,
        [pltpu.VMEM((sources, count), f32), pltpu.VMEM((width, count), f32)],
        us=9,
    )
    gsm = [mem.swap(piece, b) if b else piece for b, piece in enumerate(gsm)]

    up.step(dp, dp.bits[0])
    down.step(dp, dp.bits[1])
    middle_rows = 4 * rows + vec1.shape[0] + vec2.shape[0]
    joint_rows = dp_size * middle_rows + mem_size // 2 * 2 * share
    middle_keep, middle_send = order.call(
        functools.partial(middle_kernel, (mem_size, dp_size)),
        [(x, "w") for x in (gk, gv, memory_all, cross_kv, h0, vecs, gcq, mixed_all, gsb, vec1, vec2)],
        [((joint_rows, HALF), bf16, "v")] * 2,
        us=5,
    )
    middle_send, gsm[1] = lax.optimization_barrier((middle_send, gsm[1]))
    middle_keep, memory_keep, middle_send = order.call(
        functools.partial(middle_columns_kernel, 1, middle_rows),
        [(middle_keep, "v"), (mem.swap(middle_send, 1), "v")],
        [((dp_size, middle_rows, LANES), bf16, "v"), ((mem_size // 4, share, width), bf16, "v"),
         ((joint_rows, LANES), bf16, "v")],
    )
    middle_received = mem.swap(middle_send, mem.bits[1])

    qkv_keep, qkv_send, target_keep, target_send = order.call(
        functools.partial(self_backward_kernel, (mem_size, dp_size, head)),
        [(tlen, "s")] + [(x, "w") for x in (q, k, v, ot, lse, kt, target_near)] + [(self_qkv, "r"), (gsn, "w")] + [(x, "v") for x in gsm],
        [((dp_size // 2, rows + 16, 3 * wide), bf16, "v")] * 2 + [((mem_size // 2, count, width), bf16, "v")] * 2,
        [pltpu.VMEM((length, wide), bf16), pltpu.VMEM((length, 3 * wide), bf16), pltpu.VMEM((length, wide), f32),
         pltpu.VMEM((length, wide), f32), pltpu.VMEM((wide, length), f32),
         pltpu.VMEM((dp_size, rows + 16, 3 * wide), bf16)] + weights_held
        + [pltpu.SemaphoreType.DMA((3,))],
        us=6,
    )
    half_dims = dims[1:] + qkv_keep.shape[1:]
    qkv = Chain(order, qkv_keep.reshape(half_dims), dp.swap(qkv_send, 1).reshape(half_dims), dp.bits[1:])

    blocks = mem_size // 2
    last = len(dp.bits) - 1
    free = functools.partial(order.call, alone=False)
    order.next()
    grad = free(
        functools.partial(join_kernel, blocks),
        [(target_keep, "v"), (mem.swap(target_send, 1), "v"), (layer_own, "v")],
        [((blocks + 1, count, width), bf16, "v")],
    )[0]
    grad_far = mem.swap(grad, mem.bits[1])
    middle = None
    for n in range(1, len(dp.bits)):
        up.step(dp, dp.bits[n])
        if n < last:
            down.step(dp, dp.bits[n + 1])
        else:
            down.step(dp, dp.bits[0])
        if middle is None:
            keep, send, memory_grad = free(
                functools.partial(middle_rows_kernel, 0),
                [(middle_keep.reshape(dp_size // 2, 2, middle_rows, LANES), "v"), (memory_keep, "v"), (middle_received, "v")],
                [((dp_size // 2, middle_rows, LANES), bf16, "v")] * 2
                + [((mem_size // 4 * share, width), f32 if mem_size == 4 else bf16, "h")],
            )
            shape = dims[1:] + (middle_rows, LANES)
            middle = Chain(order, keep.reshape(shape), dp.swap(send, 1).reshape(shape), dp.bits[1:])
        else:
            middle.step(dp, dp.bits[n - 1])
        qkv.step(dp, dp.bits[n])
        order.next()
    for b in mem.bits[2:]:
        parts = memory_grad.reshape(-1, 2, share, width)
        keep, send = (lax.dynamic_index_in_dim(parts, x, 1, keepdims=False) for x in (mem.bit(b), 1 - mem.bit(b)))
        memory_grad = keep.astype(f32) + mem.swap(send, b).astype(f32)
        if b != mem.bits[-1]:
            memory_grad = memory_grad.astype(bf16)
    memory_grad = memory_grad.reshape(share, width)
    qkv_pieces = gather_pieces(mem, order.total([qkv.last()]), mem.bits)
    middle.step(dp, dp.bits[last])
    ffn = order.total([up.last(), down.last()])
    ffn_far = mem.swap(ffn, mem.bits[1])
    masks = [0]
    for b in mem.bits[1:]:
        masks = masks + [mask + b for mask in masks]
        grad = free(
            functools.partial(join_kernel, blocks),
            [(grad, "v"), (grad_far, "v")],
            [((blocks + len(masks), count, width), bf16, "v")],
        )[0]
        if b != mem.bits[-1]:
            grad_far = mem.swap(grad, 2 * b)
    order.next()
    mid = order.total([middle.last()])
    for b in mem.bits[2:]:
        mid = order.total([(mid, mem.swap(mid, b))])
    middle_pieces = gather_pieces(mem, mid, mem.bits[:2])
    for b in mem.bits[1:]:
        ffn = order.total([(ffn, ffn_far)])
        if b != mem.bits[-1]:
            ffn_far = mem.swap(ffn, 2 * b)
    target_grad, layer_output = free(
        functools.partial(rows_out_kernel, masks),
        [(grad, "v"), (mem.swap(grad, 1), "v")],
        [((length, width), f32, "r"), ((length, width), bf16, "r")],
        [pltpu.VMEM((mem_size, count, width), f32), pltpu.SemaphoreType.DMA((2 * mem_size,))],
    )
    qkv_grad, qkv_sums = free(
        qkv_out_kernel,
        [(x, "v") for x in qkv_pieces],
        [((rows, 3 * width), f32, "h"), ((8, 3 * width), f32, "v")],
    )
    order.next()
    up_grad, down_grad, co_grad = free(
        ffn_out_kernel,
        [(ffn, "v"), (mem.swap(ffn, 1), "v")],
        [((rows, hidden), f32, "h"), ((down_rows, width), f32, "h"), ((rows, width), f32, "h")],
    )
    cq_grad, so_grad, kv_grad, cb_grad, ub_grad, db_grad, gain_grad, shift_grad, sb_grad = free(
        functools.partial(middle_out_kernel, hidden // width),
        [(qkv_sums, "v")] + [(x, "v") for x in middle_pieces],
        [((rows, width), f32, "h")] * 2 + [((rows, 2 * width), f32, "h"), ((3, rows), f32, "v"),
         ((1, hidden // dp_size), f32, "v"), ((1, rows), f32, "v")] + [((3, rows), f32, "v")] * 3,
        [pltpu.VMEM((32, width), f32)],
    )
    return (
        layer_output[None],
        target_grad[None],
        memory_grad[None],
        qkv_grad,
        sb_grad,
        so_grad,
        cq_grad,
        kv_grad,
        cb_grad,
        co_grad,
        up_grad,
        ub_grad.reshape(-1),
        down_grad,
        db_grad.reshape(-1),
        gain_grad,
        shift_grad,
    )


def solution(mesh):
    row, whole = P("dp", None, None), P()
    in_specs = (row, P("dp", "mem", None), P("dp", None), P("dp", None), row) + (whole,) * 13
    out_specs = (
        row,
        row,
        P("dp", "mem", None),
        P("dp", None),
        P(None, "dp"),
        P("dp", None),
        P("dp", None),
        P("dp", None),
        P(None, "dp"),
        P("dp", None),
        P("dp", None),
        P("dp"),
        P("dp", None),
        P("dp"),
        P(None, "dp"),
        P(None, "dp"),
    )
    body = functools.partial(on_device, mesh.shape["dp"], mesh.shape["mem"])
    return jax.shard_map(body, mesh=mesh, in_specs=in_specs, out_specs=out_specs, check_vma=False)
```

```python
import functools

import jax
import jax.numpy as jnp
from jax import lax
from jax.experimental import pallas as pl
from jax.experimental.pallas import tpu as pltpu
from jax.sharding import PartitionSpec as P

HEADS = 8
SEG_MOST = 512
LANES = 128
COSTS = [
    5, 2.5, 14, 9, 4.205, 0.182, 6.5, 0.239, 2.0, 0.562,
    2.277, 0.156, 1.198, 0.674, 9.654, 4.76, 0.422, 2.782, 0.335, 0.432,
    15.718, 0.664, 1.944, 1.387, 5.101, 1.67, 6.976, 0.167, 1.068, 6.716,
    0.528, 3.629, 0.363, 1.246, 4.38, 3.273, 1.264, 2.795, 3.538, 2.944,
    0.359, 4.312, 0.732, 10.359, 2.176, 1.168, 0.288, 4.091, 1.464, 1.71,
    0.355, 4.29, 9.184, 1.848, 1.004, 1.77, 1.154, 1.237, 0.776, 1.088,
    1.598, 0.381, 0.51, 3.058,
]
ROUNDS = [0, 1, 1, 1, 1, 0, 0, 1, 1, 1, 1, 1, 1, 1, 1, 1]
HALF = 256
very_negative = -1e30
epsilon = 1e-05
SELF_BIAS, CROSS_BIAS, GAINS, SHIFTS, DOWN_BIAS, UP_BIAS = 0, 3, 6, 9, 12, 13
f32 = jnp.float32
bf16 = jnp.bfloat16


def mm(left, right):
    return jnp.dot(left, right, preferred_element_type=f32)


def mm_tn(left, right):
    return lax.dot_general(left, right, (((0,), (0,)), ((), ())), preferred_element_type=f32)


def mm_nt(left, right):
    return lax.dot_general(left, right, (((1,), (1,)), ((), ())), preferred_element_type=f32)


def norm_parts(hidden):
    center = hidden - jnp.mean(hidden, axis=-1, keepdims=True)
    scaled = lax.rsqrt(jnp.mean(center * center, axis=-1, keepdims=True) + epsilon)
    return center * scaled, scaled


def norm_backward(upstream, normed, scaled, gain_row):
    gained = upstream * gain_row
    gained_mean = jnp.mean(gained, axis=-1, keepdims=True)
    mean_cross = jnp.mean(gained * normed, axis=-1, keepdims=True)
    return scaled * (gained - gained_mean - normed * mean_cross)


def sums(matrix):
    return jnp.sum(matrix.astype(f32), axis=0, keepdims=True)


def started(lengths, places, ends, amounts):
    total = jnp.zeros(places.shape, jnp.int32)
    edge = jnp.int32(0)
    for j in range(lengths.shape[0]):
        if ends:
            edge = edge + lengths[j]
        total = total + jnp.where(places >= edge, amounts[j], 0)
        if not ends:
            edge = edge + lengths[j]
    return total


def head_lanes(value, h, head):
    if value.shape[-1] == head:
        return value
    lanes = lax.broadcasted_iota(jnp.int32, value.shape, 1)
    return jnp.where(lanes // head == h, value, jnp.zeros_like(value))


def self_bias(tlen_ref, begin, first, count):
    queries = begin + lax.broadcasted_iota(jnp.int32, (1, count), 1)
    start = started(tlen_ref, queries, True, tlen_ref)
    keys = first + lax.broadcasted_iota(jnp.int32, (begin + count - first, count), 0)
    return jnp.where((keys >= start) & (keys <= queries), 0.0, very_negative)


def self_forward_kernel(
    sizes, idx, tlen, target, qkv, shifts, q_out, k_out, v_out, kt_out, ot_out, lse_out, *rest
):
    mem, head = sizes
    pieces, (mixed, held, sem, lengths, lengths_sem) = rest[:mem], rest[mem:]
    known = pltpu.make_async_copy(tlen, lengths, lengths_sem)
    known.start()
    tlen = lengths
    length = target.shape[0]
    wide = q_out.shape[1]
    share = length // mem
    weights = own_weights(idx, qkv, held, sem, wide)
    zero = jnp.zeros((1, wide), f32)
    block = lane_block(idx[0], wide)
    shift = [own_lanes(shifts.value()[i : i + 1, block].astype(f32), idx[0], wide) for i in (0, 1)]
    shift = jnp.concatenate([shift[0], zero, shift[1]], axis=1)
    for at in range(0, length, HALF):
        rows = slice(at, at + HALF)
        part = (mm(target[rows, :], weights) + shift).astype(bf16)
        q_out[rows, :] = part[:, :wide]
        k_out[rows, :] = part[:, wide : 2 * wide]
        v_out[rows, :] = part[:, 2 * wide :]
        kt_out[:, rows] = part[:, wide : 2 * wide].T
        mixed[rows, :] = part[:, 2 * wide :]
    for out in (q_out, k_out, v_out, kt_out):
        out.send()
    known.wait()
    vt = mixed[...].T
    lse_out[...] = jnp.zeros(lse_out.shape, f32)
    work = [(at, h) for at in range(0, length, HALF) for h in range(wide // head)]

    def score(at, h):
        first = max(0, at - SEG_MOST)
        q = q_out[at : at + HALF, :] * jnp.asarray(head**-0.5, bf16)
        return mm_nt(k_out[first : at + HALF, :], head_lanes(q, h, head)) + self_bias(tlen, at, first, HALF)

    later = score(*work[0])
    for n, (at, h) in enumerate(work):
        scores, later = later, score(*work[n + 1]) if n + 1 < len(work) else None
        keys, cols = slice(max(0, at - SEG_MOST), at + HALF), slice(at, at + HALF)
        own = slice(h * head, (h + 1) * head)
        top = jnp.max(scores, axis=0, keepdims=True)
        terms = jnp.exp(scores - top)
        total = jnp.sum(terms, axis=0, keepdims=True)
        ot_out[own, cols] = mm(vt[own, keys], terms.astype(bf16)) / total
        lse_out[h : h + 1, cols] = top + jnp.log(total)
        if h == wide // head - 1:
            mixed[cols, :] = ot_out[:, cols].T.astype(bf16)
    for b in range(mem):
        at = pl.multiple_of((idx[0] ^ b) * share, share)
        pieces[b][...] = mixed[pl.ds(at, share), :]


def memory_kernel(idx, *refs):
    pieces, (weights, all_out, k_out, v_out, kt_out, vt_out) = refs[:-6], refs[-6:]
    share, width = pieces[0].shape
    for b, piece in enumerate(pieces):
        at = pl.multiple_of((idx[0] ^ b) * share, share)
        all_out[pl.ds(at, share), :] = piece[...]
        both = mm(piece[...], weights[...]).astype(bf16)
        k_out[pl.ds(at, share), :] = both[:, :width]
        v_out[pl.ds(at, share), :] = both[:, width:]
        kt_out[:, pl.ds(at, share)] = both[:, :width].T
        vt_out[:, pl.ds(at, share)] = both[:, width:].T


def cross_bias_of(idx, tlen, slen, count, keys):
    queries = idx[0] * count + lax.broadcasted_iota(jnp.int32, (1, count), 1)
    low = started(tlen, queries, True, slen)
    high = started(tlen, queries, False, slen)
    places = lax.broadcasted_iota(jnp.int32, (keys, count), 0)
    return jnp.where((places >= low) & (places < high), 0.0, very_negative)


def column_of(row, count):
    return jnp.broadcast_to(row, (count, row.shape[1])).T


def token_kernel(
    sizes, idx, tlen, slen, target, cotangent, wo, vecs, cq, keys, vt, co, up, down, *rest,
):
    mem, dp, head = sizes
    pieces, rest = rest[:mem], rest[mem:]
    (lo_out, up_keep, up_send, down_keep, down_send, h0_out, mixed_out, q_out, att_out, lse_out, gcn_out,
     vec_out, x, ct, bias, act, fac, gi, gfo_s, acl_s, gcb_s, sem) = rest
    count, width = lo_out.shape
    wide = width // mem
    hidden = up.shape[1]
    share = pl.ds(pl.multiple_of(idx[0] * count, count), count)
    copies = [
        pltpu.make_async_copy(target.at[share, :], x, sem.at[0]),
        pltpu.make_async_copy(cotangent.at[share, :], ct, sem.at[1]),
    ]
    for copy in copies:
        copy.start()
    bias[...] = cross_bias_of(idx, tlen, slen, count, keys.shape[0])
    row = lambda i: vecs[i : i + 1, :]
    h0 = row(SELF_BIAS + 2)
    for b in range(mem):
        at = pl.multiple_of((idx[0] ^ b) * wide, wide)
        h0 = h0 + mm(pieces[b][...], wo.value()[pl.ds(at, wide), :])
        mixed_out[:, b * wide : (b + 1) * wide] = pieces[b][...]
    copies[0].wait()
    h0 = h0 + x[...].astype(f32)
    h0_out[...] = h0
    mixed_out.send()
    h0_out.send()
    normed0, _ = norm_parts(h0)
    after_self = normed0 * row(GAINS) + row(SHIFTS)
    q = (mm(after_self.astype(bf16), cq[...]) + row(CROSS_BIAS)).astype(bf16)
    q_out[...] = q
    q_out.send()
    q = q * jnp.asarray(head**-0.5, bf16)

    def score(h):
        pair = slice(h * head // LANES * LANES, h * head // LANES * LANES + LANES)
        return mm_nt(keys[:, pair], head_lanes(q[:, pair], h % (LANES // head), head)) + bias[...]

    later = score(0)
    for h in range(HEADS):
        scores, later = later, score(h + 1) if h + 1 < HEADS else None
        top = jnp.max(scores, axis=0, keepdims=True)
        terms = jnp.exp(scores - top)
        total = jnp.sum(terms, axis=0, keepdims=True)
        own = slice(h * head, (h + 1) * head)
        att_out[own, :] = mm(vt[own, :], terms.astype(bf16)) / total
        lse_out[h : h + 1, :] = top + jnp.log(total)
    cmt = (att_out[...] + column_of(row(CROSS_BIAS + 1), count)).astype(bf16)
    for out in (att_out, lse_out):
        out.send()
    normed1, scaled1 = norm_parts(after_self + mm_tn(cmt, co[...]) + row(CROSS_BIAS + 2))
    after_cross = normed1 * row(GAINS + 1) + row(SHIFTS + 1)
    acl = after_cross.astype(bf16)
    acl_s[...] = acl
    step = width
    h2 = after_cross + row(DOWN_BIAS)
    chunks = [slice(at, at + step) for at in range(0, hidden, step)]
    later = mm(acl, up[:, chunks[0]])
    for i, cols in enumerate(chunks):
        inner = later + row(UP_BIAS + i)
        later = mm(acl, up[:, chunks[i + 1]]) if i + 1 < len(chunks) else None
        sig = jax.nn.sigmoid(inner)
        part = (inner * sig).astype(bf16)
        act[:, cols] = part
        fac[:, cols] = sig * (1.0 + inner * (1.0 - sig))
        h2 = h2 + mm(part, down[cols, :])
    normed2, scaled2 = norm_parts(h2)
    lo_out[...] = (normed2 * row(GAINS + 2) + row(SHIFTS + 2)).astype(bf16)
    copies[1].wait()
    cot = ct[...].astype(f32)
    gf = norm_backward(cot, normed2, scaled2, row(GAINS + 2))
    gfo = gf.astype(bf16)
    gfo_s[...] = gfo
    u1 = gf
    vec_out[...] = jnp.zeros(vec_out.shape, f32)
    later = mm_nt(gfo, down[chunks[0], :])
    for i, cols in enumerate(chunks):
        part = (later * fac[:, cols]).astype(bf16)
        later = mm_nt(gfo, down[chunks[i + 1], :]) if i + 1 < len(chunks) else None
        gi[:, cols] = part
        u1 = u1 + mm_nt(part, up[:, cols])
        vec_out[5 + i : 6 + i, :] = sums(part)
    rows, hrows = width // dp, hidden // dp
    some = width // hrows
    sides = ((up_send, down_send, 1 - idx[0] % 2), (up_keep, down_keep, idx[0] % 2))
    own_cols = lambda side, at: pl.ds(pl.multiple_of(side * HALF + at, HALF), HALF)
    for i in range(hidden // width):
        actt = act[:, i * width : (i + 1) * width].T
        for _, down_out, side in sides:
            part = mm(actt, gfo_s[:, own_cols(side, 0)]).astype(bf16)
            down_out[i * some : (i + 1) * some] = part.reshape(some, hrows, HALF)
    gcn = norm_backward(u1, normed1, scaled1, row(GAINS + 1))
    gcn_out[...] = gcn
    gcb_s[...] = gcn.astype(bf16)
    aclt = acl_s[...].T
    for i in range(hidden // width):
        for up_out, _, side in sides:
            part = mm(aclt, gi[:, own_cols(side, i * width)]).astype(bf16)
            up_out[:, i * rows : (i + 1) * rows, :] = part.reshape(dp, rows, HALF)
    for i, part in enumerate((u1 * normed1, u1, cot * normed2, cot, gfo)):
        vec_out[i : i + 1, :] = sums(part)
    last = hidden // width * rows
    for up_out, _, side in sides:
        part = mm(cmt, gcb_s[:, own_cols(side, 0)]).astype(bf16)
        up_out[:, last : last + rows, :] = part.reshape(dp, rows, HALF)


def cross_backward_kernel(
    sizes, idx, tlen, slen, gcn, co, q_ref, lse, att, keys, values, kt, cq, vecs, h0, wo,
    gk_out, gv_out, gcq_out, gsb_out, gsn_out, vec_out, *rest,
):
    mem, head = sizes
    pieces, (bias, gcqt) = rest[:mem], rest[mem:]
    count, width = gcn.shape
    wide = width // mem
    bias[...] = cross_bias_of(idx, tlen, slen, count, keys.shape[0])
    gcb = gcn[...].astype(bf16)
    gcm = mm_nt(gcb, co[...]).astype(bf16)
    gcmt = mm_nt(co[...], gcb).astype(bf16)
    scale = head**-0.5
    q = q_ref[...] * jnp.asarray(scale, bf16)
    per = LANES // head

    def products(h):
        pair = slice(h // per * LANES, (h // per + 1) * LANES)
        qh, gh = head_lanes(q[:, pair], h % per, head), head_lanes(gcm[:, pair], h % per, head)
        scores = mm_nt(keys[:, pair], qh) + bias[...] - lse[h : h + 1, :]
        return qh, gh, scores, mm_nt(values[:, pair], gh)

    later = products(0)
    for h in range(width // head):
        (qh, gh, scores, grads), later = later, products(h + 1) if h + 1 < width // head else None
        pair, own = slice(h // per * LANES, (h // per + 1) * LANES), slice(h * head, (h + 1) * head)
        delta = jnp.sum(gcmt[own, :].astype(f32) * att[own, :], axis=0, keepdims=True)
        probs = jnp.exp(scores)
        ds = (probs * (grads - delta)).astype(bf16)
        gv_part, gk_part = mm(probs.astype(bf16), gh), mm(ds, qh)
        gcqt[own, :] = mm(kt[own, :], ds) * scale
        gv, gk = (gv_part, gk_part) if h % per == 0 else (gv + gv_part, gk + gk_part)
        if h % per == per - 1:
            gk_out[:, pair] = gk.astype(bf16)
            gv_out[:, pair] = gv.astype(bf16)
    gk_out.send()
    gv_out.send()
    gcq = gcqt[...].T.astype(bf16)
    gcq_out[...] = gcq
    gcq_out.send()
    u0 = gcn[...] + mm_nt(gcq, cq[...])
    normed0, scaled0 = norm_parts(h0[...])
    gsn = norm_backward(u0, normed0, scaled0, vecs[GAINS : GAINS + 1, :])
    gsn_out[...] = gsn
    gsb = gsn.astype(bf16)
    gsb_out[...] = gsb
    for b in range(mem):
        at = pl.multiple_of((idx[0] ^ b) * wide, wide)
        pieces[b][...] = mm_nt(gsb, wo.value()[pl.ds(at, wide), :]).astype(bf16)
    vec_out[...] = jnp.zeros(vec_out.shape, f32)
    for i, part in enumerate((gsb, gcq, gcm, gcb, u0 * normed0, u0)):
        vec_out[i : i + 1, :] = sums(part)


def middle_kernel(
    sizes, idx, gk, gv, memory, wkv, h0, vecs, gcq, mixed, gsb, vec1, vec2, keep_out, send_out
):
    mem, dp = sizes
    width = gsb.shape[1]
    wide, share = width // mem, memory.shape[0] // mem
    rows = width // dp
    place = keep_out.shape[0] - mem // 2 * 2 * share
    for out, side in ((send_out, 1 - idx[0] % 2), (keep_out, idx[0] % 2)):
        for i in range(mem // 2):
            at = pl.ds(pl.multiple_of((2 * i + side) * share, share), share)
            part = mm_nt(gk.value()[at, :], wkv[:, :width]) + mm_nt(gv.value()[at, :], wkv[:, width:])
            for k in range(2):
                rest = place + (2 * i + k) * share
                out[rest : rest + share, :] = part[:, k * HALF : (k + 1) * HALF].astype(bf16)
    normed0, _ = norm_parts(h0[...])
    asl = (normed0 * vecs[GAINS : GAINS + 1, :] + vecs[SHIFTS : SHIFTS + 1, :]).astype(bf16)
    vec = jnp.concatenate([vec1[...], vec2[...]], axis=0).astype(bf16)
    some, per = wide // rows, 4 * rows + vec.shape[0]
    for out, side in ((send_out, 1 - idx[0] % 2), (keep_out, idx[0] % 2)):
        cols = pl.ds(pl.multiple_of(side * HALF, HALF), HALF)

        def put(at, matrix):
            for d in range(dp):
                first = d * per + at * rows
                out[first : first + rows, :] = matrix[d * rows : (d + 1) * rows].astype(bf16)

        put(0, mm_tn(asl, gcq.value()[:, cols]))
        part = mm_tn(mixed[...], gsb.value()[:, cols]).astype(bf16)
        for b in range(mem):
            j = idx[0] ^ b
            for i in range(some):
                first = pl.multiple_of((j * some + i) * per + rows, 16)
                out[pl.ds(first, rows), :] = part[b * wide + i * rows : b * wide + (i + 1) * rows]
        put(2, mm_tn(memory[...], gk.value()[:, cols]))
        put(3, mm_tn(memory[...], gv.value()[:, cols]))
        vrows = vec.shape[0]
        half = jnp.where(side == 0, vec[:, :HALF], vec[:, HALF:])
        for d in range(dp):
            out[(d + 1) * per - vrows : (d + 1) * per, :] = half


def self_backward_kernel(
    sizes, idx, tlen, q_ref, k_ref, v_ref, ot, lse, kt, target, qkv, gsn, *rest
):
    mem, dp, head = sizes
    pieces = rest[:mem]
    qkv_keep, qkv_send, keep_out, send_out, go, gproj, gk, gv, gqt, qkv_out, held, sem = rest[mem:]
    length, wide = q_ref.shape
    share, width = gsn.shape
    copies = own_weights_copies(idx, qkv, held, sem, wide)
    for b in range(mem):
        at = pl.multiple_of((idx[0] ^ b) * share, share)
        go[pl.ds(at, share), :] = pieces[b][...]
    gk[...] = jnp.zeros_like(gk)
    gv[...] = jnp.zeros_like(gv)
    scale = head**-0.5
    work = [(at, h) for at in range(0, length, HALF) for h in range(wide // head)]

    def products(at, h):
        first = max(0, at - SEG_MOST)
        keys, cols = slice(first, at + HALF), slice(at, at + HALF)
        qh = head_lanes(q_ref[cols, :] * jnp.asarray(scale, bf16), h, head)
        gh = head_lanes(go[cols, :], h, head)
        scores = mm_nt(k_ref[keys, :], qh) + self_bias(tlen, at, first, HALF) - lse[h : h + 1, cols]
        return keys, cols, qh, gh, scores, mm_nt(v_ref[keys, :], gh)

    later = products(*work[0])
    for n, (at, h) in enumerate(work):
        (keys, cols, qh, gh, scores, grads), later = later, products(*work[n + 1]) if n + 1 < len(work) else None
        own = slice(h * head, (h + 1) * head)
        if h == 0:
            product = go[cols, :].astype(f32).T * ot[:, cols]
        delta = jnp.sum(product[own, :], axis=0, keepdims=True)
        probs = jnp.exp(scores)
        ds = (probs * (grads - delta)).astype(bf16)
        gv[keys, :] += mm(probs.astype(bf16), gh)
        gk[keys, :] += mm(ds, qh)
        gqt[own, cols] = mm(kt[own, keys], ds) * scale
    gproj[:, :wide] = gqt[...].T.astype(bf16)
    gproj[:, wide : 2 * wide] = gk[...].astype(bf16)
    gproj[:, 2 * wide :] = gv[...].astype(bf16)
    rows = width // dp
    qkv_out[:, :rows, :] = mm_tn(target[...], gproj[...]).astype(bf16).reshape(dp, rows, 3 * wide)
    total = sums(gproj[...]).astype(bf16)
    pad = qkv_out.shape[1] - rows
    qkv_out[:, rows:, :] = jnp.broadcast_to(total[None], (dp, pad, 3 * wide))
    for out, side in ((qkv_send, 1 - idx[1] % 2), (qkv_keep, idx[1] % 2)):
        for i in range(dp // 2):
            out[i] = qkv_out[2 * i + side]
    weights = own_weights_value(idx, copies, held, wide)
    for out, side in ((send_out, 1 - idx[0] % 2), (keep_out, idx[0] % 2)):
        for i in range(mem // 2):
            at = pl.multiple_of((2 * i + side) * share, share)
            part = mm_nt(gproj[pl.ds(at, share), :], weights)
            if out is keep_out:
                part = part + jnp.where(idx[0] // 2 == i, 1.0, 0.0) * gsn[...]
            out[i] = part.astype(bf16)


def own_weights_copies(idx, qkv, held, sem, wide):
    width, full = qkv.shape[0], qkv.shape[1] // 3
    lanes = max(wide, LANES)
    copies = []
    for c in range(3):
        at = pl.multiple_of(c * full + idx[0] * wide // LANES * LANES, LANES)
        copies.append(pltpu.make_async_copy(qkv.at[:, pl.ds(at, lanes)], held.at[c], sem.at[c]))
        copies[-1].start()
    return copies


def own_weights_value(idx, copies, held, wide):
    for copy in copies:
        copy.wait()
    return jnp.concatenate([own_lanes(held[c], idx[0], wide) for c in range(3)], axis=1)


def own_weights(idx, qkv, held, sem, wide):
    return own_weights_value(idx, own_weights_copies(idx, qkv, held, sem, wide), held, wide)


def split_kernel(axis_at, bit_at, dim, idx, keep, received, keep_out, send_out):
    bit = (idx[axis_at] >> bit_at) & 1
    if dim == keep.ndim - 1:
        total = keep[...].astype(f32) + received[...].astype(f32)
        middle = keep.shape[-1] // 2
        low, high = total[..., :middle], total[..., middle:]
        keep_out[...] = jnp.where(bit == 0, low, high).astype(bf16)
        send_out[...] = jnp.where(bit == 0, high, low).astype(bf16)
        return
    lead = (slice(None),) * dim
    for out, which in ((send_out, 1 - bit), (keep_out, bit)):
        out[...] = (keep[lead + (which,)].astype(f32) + received[lead + (which,)].astype(f32)).astype(bf16)


def add_kernel(idx, *refs):
    out, pairs, at = refs[-1], refs[:-1], 0
    for keep, received in zip(pairs[::2], pairs[1::2]):
        part = keep[...].astype(f32) + received[...].astype(f32)
        out[at : at + part.shape[0]] = part.astype(out.dtype)
        at += part.shape[0]


def join_kernel(parts, idx, keep, received, *refs):
    more, out = refs[:-1], refs[-1]
    for i in range(parts):
        out[i] = (keep[i].astype(f32) + received[i].astype(f32)).astype(bf16)
    at = parts
    for ref in more or (keep, received):
        if more:
            out[at] = ref[...]
            at += 1
            continue
        for i in range(parts, ref.shape[0]):
            out[at] = ref[i]
            at += 1


def rows_out_kernel(masks, idx, own, other, target_out, layer_out, held, sem):
    share = own.shape[1]
    copies = []
    blocks = own.shape[0] - len(masks)

    def send(source, out, at):
        at = pl.ds(pl.multiple_of(at * share, share), share)
        copies.append(pltpu.make_async_copy(source, out.at[at, :], sem.at[len(copies)]))
        copies[-1].start()

    for ref, flip in ((own, 0), (other, 1)):
        for i, mask in enumerate(masks):
            send(ref.at[blocks + i], layer_out, idx[0] ^ (mask + flip))
    for i in range(blocks):
        for k, ref in enumerate((own, other)):
            held[2 * i + k] = ref[i].astype(f32)
            send(held.at[2 * i + k], target_out, 2 * i + (idx[0] + k) % 2)
    for copy in copies:
        copy.wait()


def ffn_out_kernel(idx, own, other, up_out, down_out, co_out):
    rows, width = co_out.shape
    blocks = up_out.shape[1] // width
    for piece, side in ((own, idx[0] % 2), (other, 1 - idx[0] % 2)):
        for i in range(blocks):
            at = pl.multiple_of(i * width + side * HALF, HALF)
            up_out.held[:, pl.ds(at, HALF)] = piece[i * rows : (i + 1) * rows, :].astype(f32)
        cols = pl.ds(pl.multiple_of(side * HALF, HALF), HALF)
        co_out.held[:, cols] = piece[blocks * rows : (blocks + 1) * rows, :].astype(f32)
        down_out.held[:, cols] = piece[(blocks + 1) * rows :, :].astype(f32)


def lanes_from(ref, first, count, at, wide):
    if wide % LANES == 0:
        return ref[pl.ds(first, count), pl.ds(pl.multiple_of(at, LANES), wide)]
    block = ref[pl.ds(first, count), pl.ds(pl.multiple_of(at // LANES * LANES, LANES), LANES)]
    result = block[:, :wide]
    for k in range(1, LANES // wide):
        result = jnp.where(at % LANES == k * wide, block[:, k * wide : (k + 1) * wide], result)
    return result


def middle_out_kernel(count, idx, qkv_sums, *refs):
    pieces = refs[:-10]
    cq_out, so_out, kv_out, cb_out, ub_out, db_out, gain_out, shift_out, sb_out, vec = refs[-10:]
    rows, width = cq_out.shape
    for b, piece in enumerate(pieces):
        other = idx[0] ^ b
        at = other % 2 * HALF + other // 2 % 2 * LANES
        cols = pl.ds(pl.multiple_of(at, LANES), LANES)
        for i, out in enumerate((cq_out, so_out)):
            out.held[:, cols] = piece[i * rows : (i + 1) * rows, :].astype(f32)
        for i in range(2):
            part = piece[(2 + i) * rows : (3 + i) * rows, :].astype(f32)
            kv_out.held[:, pl.ds(pl.multiple_of(i * width + at, LANES), LANES)] = part
        vec[:, cols] = piece[4 * rows :, :].astype(f32)
    here = idx[1] * rows
    take = lambda first, count: lanes_from(vec, first, count, here, rows)
    cb_out[...] = take(17, 3)
    db_out[...] = take(4, 1)
    for out, places in ((gain_out, (20, 0, 2)), (shift_out, (21, 1, 3))):
        for i, first in enumerate(places):
            out[i : i + 1, :] = take(first, 1)
    per = ub_out.shape[1]
    first = idx[1] * per
    part = lanes_from(vec, 5, 1, first % width, per)
    for i in range(1, count):
        part = jnp.where(first // width == i, lanes_from(vec, 5 + i, 1, first % width, per), part)
    ub_out[...] = part
    for i, (ref, at) in enumerate(((qkv_sums, 0), (qkv_sums, 2 * width), (vec, 0))):
        sb_out[i : i + 1, :] = lanes_from(ref, 16 if ref is vec else 0, 1, at + here, rows)


def qkv_out_kernel(idx, *refs):
    pieces, (qkv_out, full) = refs[:-2], refs[-2:]
    rows, width = qkv_out.shape[0], qkv_out.shape[1] // 3
    wide = pieces[0].shape[1] // 3

    def put(out, first, count):
        for c in range(3):
            lanes = slice(c * wide, (c + 1) * wide)
            parts = [piece[first : first + count, lanes].astype(f32) for piece in pieces]
            if wide < LANES:
                odd = idx[0] % 2
                parts = [
                    jnp.where(odd == 0, jnp.concatenate([a, b], 1), jnp.concatenate([b, a], 1))
                    for a, b in zip(parts[::2], parts[1::2])
                ]
            for b, part in enumerate(parts):
                j = idx[0] ^ b if wide >= LANES else (idx[0] // 2) ^ b
                at = pl.multiple_of(c * width + j * max(wide, LANES), LANES)
                out[:count, pl.ds(at, max(wide, LANES))] = part

    put(qkv_out.held, 0, rows)
    put(full, rows, full.shape[0])


def middle_columns_kernel(bit_at, count, idx, keep, received, keep_out, memory_out, send_out):
    bit = (idx[0] >> bit_at) & 1
    per = keep_out.shape[1]
    for d in range(keep_out.shape[0]):
        at = slice(d * per, (d + 1) * per)
        total = keep[at, :].astype(f32) + received[at, :].astype(f32)
        low, high = total[:, :LANES], total[:, LANES:]
        keep_out[d] = jnp.where(bit == 0, low, high).astype(bf16)
        send_out[at, :] = jnp.where(bit == 0, high, low).astype(bf16)
    place = keep_out.shape[0] * per
    share = memory_out.shape[1]
    for i in range(memory_out.shape[0]):
        for k in range(2):
            for which in (0, 1):
                side = bit if which else 1 - bit
                at = pl.ds(pl.multiple_of(place + ((2 * i + side) * 2 + k) * share, 16), share)
                total = (keep[at, :].astype(f32) + received[at, :].astype(f32)).astype(bf16)
                if which:
                    memory_out[i, :, k * HALF : (k + 1) * HALF] = total
                    continue
                for n in range(HALF // LANES):
                    rest = place + ((i * 2 + k) * 2 + n) * share
                    send_out[rest : rest + share, :] = total[:, n * LANES : (n + 1) * LANES]


def middle_rows_kernel(bit_at, idx, keep, memory, received, keep_out, send_out, memory_out):
    bit = (idx[1] >> bit_at) & 1
    per = keep.shape[2]
    for out, side in ((send_out, 1 - bit), (keep_out, bit)):
        for i in range(keep.shape[0]):
            at = pl.ds(pl.multiple_of((2 * i + side) * per, 16), per)
            out[i] = (keep[i, side].astype(f32) + received[at, :].astype(f32)).astype(bf16)
    place = keep.shape[0] * 2 * per
    share = memory.shape[1]
    for i in range(memory.shape[0]):
        for k in range(memory.shape[2] // LANES):
            cols = slice(k * LANES, (k + 1) * LANES)
            rest = place + (i * (memory.shape[2] // LANES) + k) * share
            total = memory[i, :, cols].astype(f32) + received[rest : rest + share, :].astype(f32)
            memory_out[i * share : (i + 1) * share, cols] = total.astype(memory_out.dtype)


class Staged:
    def __init__(self, source, held, sem):
        self.held, self.shape, self.dtype = held, held.shape, held.dtype
        self.copy = pltpu.make_async_copy(source, held, sem)
        self.copy.start()
        self.waited = False

    def wait(self):
        if not self.waited:
            self.copy.wait()
            self.waited = True

    def __getitem__(self, at):
        self.wait()
        return self.held[at]

    def value(self):
        self.wait()
        return self.held


class Result:
    def __init__(self, place, held, sem):
        self.held, self.shape, self.dtype = held, held.shape, held.dtype
        self.copy, self.sent = pltpu.make_async_copy(held, place, sem), False

    def __getitem__(self, at):
        return self.held[at]

    def __setitem__(self, at, value):
        self.held[at] = value

    def send(self):
        if not self.sent:
            self.copy.start()
            self.sent = True


class Plain:
    def __init__(self, ref):
        self.held, self.shape, self.dtype = ref, ref.shape, ref.dtype

    def __getitem__(self, at):
        return self.held[at]

    def __setitem__(self, at, value):
        self.held[at] = value

    def value(self):
        return self.held

    def send(self):
        pass


def call(kernel, ins, outs, scratch=(), vmem=16, us=1.0):
    ins = [(pltpu.with_memory_space_constraint(x, pltpu.HBM) if mode in "hr" else x, mode) for x, mode in ins]
    spaces = {"s": pltpu.SMEM, "v": pltpu.VMEM, "w": pltpu.VMEM, "h": pltpu.HBM, "r": pltpu.HBM}
    held = [(x.shape, x.dtype) for x, mode in ins if mode == "h"]
    held += [(shape, dtype) for shape, dtype, mode in outs if mode == "h"]
    modes = [mode for _, mode in ins] + [mode for _, _, mode in outs]

    def body(*refs):
        count = len(modes)
        own = refs[count + len(held) : len(refs) - 1 if held else len(refs)]
        spare, sems = iter(refs[count : count + len(held)]), refs[-1]
        given, place = [], 0
        for i, mode in enumerate(modes):
            ref = refs[i]
            if mode == "h":
                ref = (Staged if i < len(ins) else Result)(ref, next(spare), sems.at[place])
                place += 1
            if mode == "w":
                ref = Plain(ref)
            given.append(ref)
        kernel(*given, *own)
        for ref in given:
            if isinstance(ref, Staged):
                ref.wait()
            if isinstance(ref, Result):
                ref.send()
        for ref in given:
            if isinstance(ref, Result):
                ref.copy.wait()

    held_scratch = [pltpu.VMEM(shape, dtype) for shape, dtype in held]
    sems = [pltpu.SemaphoreType.DMA((len(held),))] if held else []
    return pl.pallas_call(
        body,
        out_shape=[
            (pltpu.HBM if mode in "hr" else jax.ShapeDtypeStruct)(shape, dtype) for shape, dtype, mode in outs
        ],
        in_specs=[pl.BlockSpec(memory_space=spaces[mode]) for _, mode in ins],
        out_specs=[pl.BlockSpec(memory_space=spaces[mode]) for _, _, mode in outs],
        scratch_shapes=held_scratch + list(scratch) + sems,
        compiler_params=pltpu.CompilerParams(vmem_limit_bytes=vmem * 1024 * 1024),
        cost_estimate=pl.CostEstimate(
            flops=int(us * 1.1e9), bytes_accessed=int(us * 1e6), transcendentals=0
        ),
    )(*[x for x, _ in ins])


def own_lanes(block, which, wide):
    if wide % LANES == 0:
        return block
    return jnp.where(which % 2 == 0, block[:, :wide], block[:, wide : 2 * wide])


def lane_block(which, wide):
    return pl.ds(pl.multiple_of(which * wide // LANES * LANES, LANES), max(wide, LANES))


class Axis:
    def __init__(self, name, size, place):
        self.name, self.size, self.place = name, size, place
        self.index = lax.axis_index(name)
        self.bits = [1 << k for k in range(size.bit_length() - 1)]

    def bit(self, b):
        return (self.index // b) % 2

    def swap(self, value, b):
        return lax.ppermute(value, self.name, [(i, i ^ b) for i in range(self.size)])


def gather_pieces(axis, value, bits):
    pieces = {0: value}
    for b in reversed(bits):
        for k in sorted(pieces):
            pieces[k ^ b] = axis.swap(pieces[k], b)
    return [pieces[k] for k in sorted(pieces)]


class Order:
    def __init__(self, idx):
        self.costs, self.rounds = iter(COSTS), iter(ROUNDS)
        self.idx, self.before, self.now = idx, [], []

    def call(self, kernel, ins, outs, scratch=(), vmem=16, us=2.0, alone=True):
        if alone:
            self.next(True)
        idx = lax.optimization_barrier((self.idx, *self.before))[0] if self.before else self.idx
        results = call(kernel, [(idx, "s")] + ins, outs, scratch, vmem, next(self.costs))
        self.now.append(results[0])
        return results

    def next(self, always=False):
        if (always or next(self.rounds)) and self.now:
            self.before, self.now = self.now, []

    def split(self, axis, b, keep, received, dim):
        shape = list(keep.shape)
        if dim == keep.ndim - 1:
            shape[dim] //= 2
        else:
            del shape[dim]
        kernel = functools.partial(split_kernel, axis.place, b.bit_length() - 1, dim)
        return self.call(kernel, [(keep, "v"), (received, "v")], [(shape, bf16, "v")] * 2, alone=False)

    def total(self, pairs, dtype=bf16, mode="v"):
        shape = (sum(keep.shape[0] for keep, _ in pairs),) + pairs[0][0].shape[1:]
        return self.call(add_kernel, [(x, "v") for pair in pairs for x in pair], [(shape, dtype, mode)], alone=False)[0]


class Chain:
    def __init__(self, order, keep, received, bits):
        self.order, self.keep, self.received = order, keep, received
        self.left = list(reversed(bits))

    def step(self, axis, b):
        dim = self.keep.ndim - 1
        if axis.name == "dp":
            dim = self.left.index(b)
            self.left.remove(b)
        self.keep, send = self.order.split(axis, b, self.keep, self.received, dim)
        self.received = axis.swap(send, b)

    def last(self):
        return self.keep, self.received


def on_device(
    dp_size,
    mem_size,
    target,
    memory,
    target_lengths,
    source_lengths,
    cotangent,
    self_qkv,
    self_bias_,
    self_out,
    cross_query,
    cross_kv,
    cross_bias,
    cross_out,
    ffn_up,
    ffn_up_bias,
    ffn_down,
    ffn_down_bias,
    norm_gains,
    norm_biases,
):
    mem, dp = Axis("mem", mem_size, 0), Axis("dp", dp_size, 1)
    target, memory, cotangent = target[0], memory[0], cotangent[0]
    tlen, slen = target_lengths[0], source_lengths[0]
    length, width = target.shape
    share = memory.shape[0]
    sources = share * mem_size
    head = width // HEADS
    wide = width // mem_size
    hidden = ffn_up.shape[1]
    count = length // mem_size
    rows = width // dp_size
    idx = jnp.stack([mem.index, dp.index]).astype(jnp.int32)
    vecs = jnp.concatenate(
        [self_bias_, cross_bias, norm_gains, norm_biases, ffn_down_bias.reshape(1, width),
         ffn_up_bias.reshape(-1, width), jnp.zeros((7, width), bf16)]
    ).astype(f32)

    far_pieces = gather_pieces(mem, memory, mem.bits[1:])

    weights_held = [pltpu.VMEM((3, width, max(wide, LANES)), bf16)]
    order = Order(idx)
    q, k, v, kt, ot, lse, *mixed = order.call(
        functools.partial(self_forward_kernel, (mem_size, head)),
        [(tlen, "r"), (target, "h"), (self_qkv, "r"), (self_bias_, "h")],
        [((length, wide), bf16, "h")] * 3
        + [((wide, length), bf16, "h"), ((wide, length), f32, "h"), ((8, length), f32, "h")]
        + [((count, wide), bf16, "v")] * mem_size,
        [pltpu.VMEM((length, wide), bf16)] + weights_held
        + [pltpu.SemaphoreType.DMA((3,)), pltpu.SMEM(tlen.shape, tlen.dtype), pltpu.SemaphoreType.DMA],
        us=5,
    )
    *far_pieces, mixed[0] = lax.optimization_barrier((*far_pieces, mixed[0]))
    near_pieces = [mem.swap(piece, 1) for piece in far_pieces]
    memory_pieces = [piece for pair in zip(far_pieces, near_pieces) for piece in pair]
    mixed = [mem.swap(piece, b) if b else piece for b, piece in enumerate(mixed)]

    memory_all, mk, mv, mkt, mvt = order.call(
        memory_kernel,
        [(memory, "w")] + [(x, "v") for x in memory_pieces[1:]] + [(cross_kv, "w")],
        [((sources, width), bf16, "w")] * 3 + [((width, sources), bf16, "w")] * 2,
        us=2.5,
    )

    up_rows, down_rows = (hidden // width + 1) * rows, hidden // dp_size
    (layer_own, up_keep, up_send, down_keep, down_send, h0, mixed_all, cq, att, clse, gcn, vec1) = order.call(
        functools.partial(token_kernel, (mem_size, dp_size, head)),
        [(tlen, "s"), (slen, "s"), (target, "r"), (cotangent, "r"), (self_out, "w"), (vecs, "w"),
         (cross_query, "w"), (mk, "w"), (mvt, "w"), (cross_out, "w"), (ffn_up, "w"), (ffn_down, "w")]
        + [(x, "v") for x in mixed],
        [((count, width), bf16, "v")] + [((dp_size, up_rows, HALF), bf16, "v")] * 2
        + [((dp_size, down_rows, HALF), bf16, "v")] * 2
        + [((count, width), f32, "w"), ((count, width), bf16, "w"), ((count, width), bf16, "w"),
           ((width, count), f32, "w"), ((8, count), f32, "w"),
           ((count, width), f32, "w"), ((16, width), f32, "w")],
        [pltpu.VMEM((count, width), bf16), pltpu.VMEM((count, width), bf16), pltpu.VMEM((sources, count), f32),
         pltpu.VMEM((count, hidden), bf16), pltpu.VMEM((count, hidden), f32), pltpu.VMEM((count, hidden), bf16),
         pltpu.VMEM((count, width), bf16), pltpu.VMEM((count, width), bf16), pltpu.VMEM((count, width), bf16), pltpu.SemaphoreType.DMA((2,))],
        us=14,
        vmem=20,
    )
    dims = (2,) * len(dp.bits)
    shaped = lambda x: x.reshape(dims + x.shape[1:])
    up = Chain(order, shaped(up_keep), shaped(mem.swap(up_send, 1)), dp.bits)
    down = Chain(order, shaped(down_keep), shaped(mem.swap(down_send, 1)), dp.bits)

    gk, gv, gcq, gsb, gsn, vec2, *gsm = order.call(
        functools.partial(cross_backward_kernel, (mem_size, head)),
        [(tlen, "s"), (slen, "s"), (gcn, "w"), (cross_out, "w"), (cq, "w"), (clse, "w"), (att, "w"),
         (mk, "w"), (mv, "w"), (mkt, "w"), (cross_query, "w"), (vecs, "w"), (h0, "w"), (self_out, "w")],
        [((sources, width), bf16, "w")] * 2 + [((count, width), bf16, "w")] * 2
        + [((count, width), f32, "w"), ((16, width), f32, "w")] + [((count, wide), bf16, "v")] * mem_size,
        [pltpu.VMEM((sources, count), f32), pltpu.VMEM((width, count), f32)],
        us=9,
    )
    gsm = [mem.swap(piece, b) if b else piece for b, piece in enumerate(gsm)]

    up.step(dp, dp.bits[0])
    down.step(dp, dp.bits[1])
    middle_rows = 4 * rows + vec1.shape[0] + vec2.shape[0]
    joint_rows = dp_size * middle_rows + mem_size // 2 * 2 * share
    middle_keep, middle_send = order.call(
        functools.partial(middle_kernel, (mem_size, dp_size)),
        [(x, "w") for x in (gk, gv, memory_all, cross_kv, h0, vecs, gcq, mixed_all, gsb, vec1, vec2)],
        [((joint_rows, HALF), bf16, "v")] * 2,
        us=5,
    )
    middle_send, gsm[1] = lax.optimization_barrier((middle_send, gsm[1]))
    middle_keep, memory_keep, middle_send = order.call(
        functools.partial(middle_columns_kernel, 1, middle_rows),
        [(middle_keep, "v"), (mem.swap(middle_send, 1), "v")],
        [((dp_size, middle_rows, LANES), bf16, "v"), ((mem_size // 4, share, width), bf16, "v"),
         ((joint_rows, LANES), bf16, "v")],
    )
    middle_received = mem.swap(middle_send, mem.bits[1])

    qkv_keep, qkv_send, target_keep, target_send = order.call(
        functools.partial(self_backward_kernel, (mem_size, dp_size, head)),
        [(tlen, "s")] + [(x, "h") for x in (q, k, v, ot, lse, kt, target)] + [(self_qkv, "r"), (gsn, "w")] + [(x, "v") for x in gsm],
        [((dp_size // 2, rows + 16, 3 * wide), bf16, "v")] * 2 + [((mem_size // 2, count, width), bf16, "v")] * 2,
        [pltpu.VMEM((length, wide), bf16), pltpu.VMEM((length, 3 * wide), bf16), pltpu.VMEM((length, wide), f32),
         pltpu.VMEM((length, wide), f32), pltpu.VMEM((wide, length), f32),
         pltpu.VMEM((dp_size, rows + 16, 3 * wide), bf16)] + weights_held
        + [pltpu.SemaphoreType.DMA((3,))],
        us=6,
    )
    half_dims = dims[1:] + qkv_keep.shape[1:]
    qkv = Chain(order, qkv_keep.reshape(half_dims), dp.swap(qkv_send, 1).reshape(half_dims), dp.bits[1:])

    blocks = mem_size // 2
    last = len(dp.bits) - 1
    free = functools.partial(order.call, alone=False)
    order.next()
    grad = free(
        functools.partial(join_kernel, blocks),
        [(target_keep, "v"), (mem.swap(target_send, 1), "v"), (layer_own, "v")],
        [((blocks + 1, count, width), bf16, "v")],
    )[0]
    grad_far = mem.swap(grad, mem.bits[1])
    middle = None
    for n in range(1, len(dp.bits)):
        up.step(dp, dp.bits[n])
        if n < last:
            down.step(dp, dp.bits[n + 1])
        else:
            down.step(dp, dp.bits[0])
        if middle is None:
            keep, send, memory_grad = free(
                functools.partial(middle_rows_kernel, 0),
                [(middle_keep.reshape(dp_size // 2, 2, middle_rows, LANES), "v"), (memory_keep, "v"), (middle_received, "v")],
                [((dp_size // 2, middle_rows, LANES), bf16, "v")] * 2
                + [((mem_size // 4 * share, width), f32 if mem_size == 4 else bf16, "h")],
            )
            shape = dims[1:] + (middle_rows, LANES)
            middle = Chain(order, keep.reshape(shape), dp.swap(send, 1).reshape(shape), dp.bits[1:])
        else:
            middle.step(dp, dp.bits[n - 1])
        qkv.step(dp, dp.bits[n])
        order.next()
    for b in mem.bits[2:]:
        parts = memory_grad.reshape(-1, 2, share, width)
        keep, send = (lax.dynamic_index_in_dim(parts, x, 1, keepdims=False) for x in (mem.bit(b), 1 - mem.bit(b)))
        memory_grad = keep.astype(f32) + mem.swap(send, b).astype(f32)
        if b != mem.bits[-1]:
            memory_grad = memory_grad.astype(bf16)
    memory_grad = memory_grad.reshape(share, width)
    qkv_pieces = gather_pieces(mem, order.total([qkv.last()]), mem.bits)
    middle.step(dp, dp.bits[last])
    ffn = order.total([up.last(), down.last()])
    ffn_far = mem.swap(ffn, mem.bits[1])
    masks = [0]
    for b in mem.bits[1:]:
        masks = masks + [mask + b for mask in masks]
        grad = free(
            functools.partial(join_kernel, blocks),
            [(grad, "v"), (grad_far, "v")],
            [((blocks + len(masks), count, width), bf16, "v")],
        )[0]
        if b != mem.bits[-1]:
            grad_far = mem.swap(grad, 2 * b)
    order.next()
    mid = order.total([middle.last()])
    for b in mem.bits[2:]:
        mid = order.total([(mid, mem.swap(mid, b))])
    middle_pieces = gather_pieces(mem, mid, mem.bits[:2])
    for b in mem.bits[1:]:
        ffn = order.total([(ffn, ffn_far)])
        if b != mem.bits[-1]:
            ffn_far = mem.swap(ffn, 2 * b)
    target_grad, layer_output = free(
        functools.partial(rows_out_kernel, masks),
        [(grad, "v"), (mem.swap(grad, 1), "v")],
        [((length, width), f32, "r"), ((length, width), bf16, "r")],
        [pltpu.VMEM((mem_size, count, width), f32), pltpu.SemaphoreType.DMA((2 * mem_size,))],
    )
    qkv_grad, qkv_sums = free(
        qkv_out_kernel,
        [(x, "v") for x in qkv_pieces],
        [((rows, 3 * width), f32, "h"), ((8, 3 * width), f32, "v")],
    )
    order.next()
    up_grad, down_grad, co_grad = free(
        ffn_out_kernel,
        [(ffn, "v"), (mem.swap(ffn, 1), "v")],
        [((rows, hidden), f32, "h"), ((down_rows, width), f32, "h"), ((rows, width), f32, "h")],
    )
    cq_grad, so_grad, kv_grad, cb_grad, ub_grad, db_grad, gain_grad, shift_grad, sb_grad = free(
        functools.partial(middle_out_kernel, hidden // width),
        [(qkv_sums, "v")] + [(x, "v") for x in middle_pieces],
        [((rows, width), f32, "h")] * 2 + [((rows, 2 * width), f32, "h"), ((3, rows), f32, "v"),
         ((1, hidden // dp_size), f32, "v"), ((1, rows), f32, "v")] + [((3, rows), f32, "v")] * 3,
        [pltpu.VMEM((32, width), f32)],
    )
    return (
        layer_output[None],
        target_grad[None],
        memory_grad[None],
        qkv_grad,
        sb_grad,
        so_grad,
        cq_grad,
        kv_grad,
        cb_grad,
        co_grad,
        up_grad,
        ub_grad.reshape(-1),
        down_grad,
        db_grad.reshape(-1),
        gain_grad,
        shift_grad,
    )


def solution(mesh):
    row, whole = P("dp", None, None), P()
    in_specs = (row, P("dp", "mem", None), P("dp", None), P("dp", None), row) + (whole,) * 13
    out_specs = (
        row,
        row,
        P("dp", "mem", None),
        P("dp", None),
        P(None, "dp"),
        P("dp", None),
        P("dp", None),
        P("dp", None),
        P(None, "dp"),
        P("dp", None),
        P("dp", None),
        P("dp"),
        P("dp", None),
        P("dp"),
        P(None, "dp"),
        P(None, "dp"),
    )
    body = functools.partial(on_device, mesh.shape["dp"], mesh.shape["mem"])
    return jax.shard_map(body, mesh=mesh, in_specs=in_specs, out_specs=out_specs, check_vma=False)
```
